32 devices in a mesh: group: 1, pre: 4 (over z), dec: 4 (over y, x), tp: 2 (over core).
Axes of the slice: x: 2, y: 2, z: 4, core: 2. Of those that a mesh axis runs over, the one named last changes fastest.
Arguments:
- hidden: bfloat16 [1536, 8192], P(('group', 'pre')), may hold values from -6 to 6
- queries: bfloat16 [1536, 8192], P(('group', 'pre'), ('dec', 'tp')), may hold values from -60 to 60
- key_weight: bfloat16 [8192, 1024], P('pre', ('dec', 'tp')), may hold values from -0.0625 to 0.0625
- value_weight: bfloat16 [8192, 1024], P('pre', ('dec', 'tp')), may hold values from -0.0625 to 0.0625
- key_bias: bfloat16 [1024], P(('dec', 'tp')), may hold values from -3 to 3
- value_bias: bfloat16 [1024], P(('dec', 'tp')), may hold values from -3 to 3
- segment_ids: int32 [1536], P('group'), may hold values from 0 to 3, never falling along the last dimension, each value on 1 to 1152 neighbouring positions
- page_owner: int32 [96, 1], P(('group', 'pre')), may hold values from 0 to 3; in each aligned block of 24 rows (0 to 23, 24 to 47, ...) at most 12 rows name the same one
Outputs:
- attention: bfloat16 [1536, 8192], P(('group', 'pre'), ('dec', 'tp'))
- kv_cache: bfloat16 [4, 4, 192, 2048], P(('group', 'pre'), None, None, ('dec', 'tp'))
The draws below stay inside these ranges and needn't reach their ends.
Inputs may be any that keep to these rules, and one draw needn't show every extreme that they name: `segment_ids`: prompts are contiguous runs of tokens; ids never fall; every prompt has 1 to 1152 tokens and one has exactly 1152. `page_owner`: among the 24 pages of one device no owner is named more than 12 times, and on at least one device on at least one device that many is reached.
All inputs are finite; a program needn't handle non-finite values.
Results may differ from the reference program's by a relative error of at most 0.0074.
Values may be sent and summed in bfloat16 or wider, within the bound.
No kernel may reach another device: no remote copies, remote signals or barrier semaphores. Data moves between devices by JAX's collectives and lax.ppermute only.
A program may use at most 192 MiB of HBM per device.

```python
import math
import jax
import jax.numpy as jnp
import numpy as np
from jax import lax

D = 8192
QH = 64
KVH = 8
HD = 128
PAGE = 16
PROMPTS = 4
TOKENS = 1536
LONGEST = 1152
PAGES = 96
PAGES_DEV = 24
PAGE_CAP = 12
N_PRE = 4


def draw_queries(key, part):
    key = jax.random.fold_in(key, 7)
    first = jax.random.fold_in(key, 0)
    return jnp.clip(jax.random.normal(first, (TOKENS, QH * HD), jnp.float32), -6.0, 6.0).astype(jnp.bfloat16)


def level_of(rng, dims, shards, low, largest):
    gain, own = 1.0, jax.random.fold_in(rng, 6)
    for dim, shards_of in shards:
        draws = jnp.exp(jax.random.uniform(jax.random.fold_in(own, dim), (shards_of,), jnp.float32, low / len(shards), largest / len(shards)))
        gain = gain * jnp.repeat(draws, dims[dim] // shards_of).reshape([-1 if axis == dim else 1 for axis in range(len(dims))])
    return gain


def length_profile(amount, total, bound, slope):
    loads = [(1 << 20) // math.isqrt(standing ** slope) + 1 for standing in range(2, amount + 1)]
    spare, given = total - bound - (amount - 1), [1] * (amount - 1)
    while spare > 0:
        free = [i for i in range(amount - 1) if given[i] < bound]
        whole, budget = sum([loads[i] for i in free]), spare
        for i in free:
            addition = min(bound - given[i], max(1, budget * loads[i] // whole), spare)
            given[i] = given[i] + addition
            spare = spare - addition
    return np.array([bound] + given)


def uneven(own_key, amount, total, most, slope):
    if amount == 2:
        one = jax.random.randint(own_key, (), max(1, total - most), min(most, total - 1) + 1)
        return jnp.stack([one, total - one])
    tallies = jnp.asarray(length_profile(amount, total, most, slope), jnp.int32)
    couples = (amount - 1) // 2
    source_of, taker = tallies[1:1 + 2 * couples:2], tallies[2:2 + 2 * couples:2]
    margin = jnp.minimum(source_of - 1, most - taker)
    moved = jax.random.randint(jax.random.fold_in(own_key, 1), (couples,), 0, 1 << 20) % (margin + 1)
    tallies = tallies.at[1:1 + 2 * couples:2].set(source_of - moved).at[2:2 + 2 * couples:2].set(taker + moved)
    return tallies[jax.random.permutation(jax.random.fold_in(own_key, 2), amount)]


def assign_block(own_key, own, number, rows, count, top, bound, skew):
    ranking = jax.random.permutation(own_key, count)
    crowded, ordinary = load_shares(count, rows * top, bound, skew, True), load_shares(count, rows * top, bound, skew, False)
    places = jnp.arange(count)

    def named(sizes, turn):
        used = int((sizes > 0).sum())
        fixed = max(1, used // 4)
        shifted = fixed + (places - fixed + turn * (used - fixed)) % max(1, count - fixed)
        return jnp.zeros((count,), jnp.int32).at[ranking[jnp.where(places < fixed, places, shifted)]].set(jnp.asarray(sizes, jnp.int32))

    sizes = jnp.where(number % 4 == 0, named(crowded, number // 4), named(ordinary, number - number // 4 - 1))
    mixed = jax.random.permutation(jax.random.fold_in(own, 3), count)
    donor, taker = mixed[0:count // 2 * 2:2], mixed[1:count // 2 * 2:2]
    room = jnp.minimum(sizes[donor] - 1, bound - sizes[taker]) // 2
    room = jnp.where((donor == ranking[0]) | (taker == ranking[0]) | (sizes[taker] == 0), 0, jnp.maximum(room, 0))
    shifted = jax.random.randint(jax.random.fold_in(own, 4), (count // 2,), 0, 1 << 20) % (room + 1)
    sizes = sizes.at[donor].add(-shifted).at[taker].add(shifted)
    items = jnp.searchsorted(jnp.cumsum(sizes), jnp.arange(rows * top), side="right").astype(jnp.int32)
    table = items.reshape(top, rows).T
    table = table[jax.random.permutation(jax.random.fold_in(own, 1), rows)]
    turn = jax.random.randint(jax.random.fold_in(own, 2), (rows, 1), 0, top)
    return jnp.take_along_axis(table, (jnp.arange(top)[None, :] + turn) % top, axis=1)


def load_shares(number_of, total, reach, skew, full):
    portions = [(1 << 20) // math.isqrt(grade ** skew) + 1 for grade in range(1, number_of + 1)]
    largest = reach if full else min(reach, max(-(-total // number_of), total * portions[0] // sum(portions)))
    least = 1 if total - largest >= number_of - 1 else 0
    given, rest = [largest] + [least] * (number_of - 1), total - largest - least * (number_of - 1)
    while rest > 0:
        movable = [i for i in range(1, number_of) if given[i] < largest] or [i for i in range(1, number_of) if given[i] < reach]
        whole, budget = sum([portions[i] for i in movable]), rest
        for i in movable:
            addition = min(reach - given[i], max(1, budget * portions[i] // whole), rest)
            given[i] = given[i] + addition
            rest = rest - addition
    return np.array(given)


def normal_values(own_key, extent, width, reach, cuts=(), kind=jnp.bfloat16):
    entries = jax.random.normal(own_key, extent, jnp.float32) * width
    if len(cuts) > 0:
        entries = level_of(own_key, extent, cuts, -0.22, 0.18) * entries
    return jnp.clip(entries, min=-reach, max=reach).astype(kind)


def setup_inputs(seed: int = 0, part: int = 0) -> dict:
    splits = jax.random.split(jax.random.key(seed), 9)
    own_keys = jax.random.split(jax.random.fold_in(splits[8], part), 9)
    hidden = normal_values(own_keys[0], (TOKENS, D), 1.0, 6.0, ((0, 4),))
    queries = draw_queries(jax.random.fold_in(jax.random.fold_in(splits[8], part), 71), part)
    key_weight = normal_values(splits[2], (D, KVH * HD), D ** -0.5, 0.0625, ((0, 4), (1, 8)))
    value_weight = normal_values(splits[3], (D, KVH * HD), D ** -0.5, 0.0625, ((0, 4), (1, 8)))
    key_bias = normal_values(splits[4], (KVH * HD,), 0.5, 3.0, ((0, 8),))
    value_bias = normal_values(splits[5], (KVH * HD,), 0.5, 3.0, ((0, 8),))
    segment_ids = jnp.searchsorted(jnp.cumsum(uneven(own_keys[6], PROMPTS, TOKENS, LONGEST, 2)), jnp.arange(TOKENS), side="right").astype(jnp.int32)
    page_owner_keys = jax.random.split(jax.random.fold_in(own_keys[7], 1), PAGES // PAGES_DEV)
    page_owner_turns = jax.random.permutation(jax.random.fold_in(own_keys[7], 3), PAGES // PAGES_DEV)
    page_owner = jax.vmap(lambda own, number: assign_block(jax.random.fold_in(own_keys[7], 2), own, number, PAGES_DEV, N_PRE, 1, PAGE_CAP, 2))(page_owner_keys, page_owner_turns).reshape((PAGES, 1))
    return dict(hidden=hidden, queries=queries, key_weight=key_weight, value_weight=value_weight, key_bias=key_bias, value_bias=value_bias, segment_ids=segment_ids, page_owner=page_owner)


def reference(hidden, queries, key_weight, value_weight, key_bias, value_bias, segment_ids, page_owner):
    keys = (jnp.dot(hidden, key_weight, preferred_element_type=jnp.float32) + key_bias.astype(jnp.float32)).astype(jnp.bfloat16)
    values = (jnp.dot(hidden, value_weight, preferred_element_type=jnp.float32) + value_bias.astype(jnp.float32)).astype(jnp.bfloat16)
    group_size = QH // KVH
    scale = float(HD) ** -0.5
    position = jnp.arange(TOKENS, dtype=jnp.int32)
    allowed = (segment_ids[:, None] == segment_ids[None, :]) & (position[None, :] <= position[:, None])
    query_heads = queries.reshape(TOKENS, QH, HD).transpose(1, 0, 2)
    key_heads = keys.reshape(TOKENS, KVH, HD).transpose(1, 0, 2)
    value_heads = values.reshape(TOKENS, KVH, HD).transpose(1, 0, 2)

    def one_head(head):
        query = query_heads[head]
        key = key_heads[head // group_size]
        value = value_heads[head // group_size]
        scores = jnp.dot(query, key.T, preferred_element_type=jnp.float32) * scale
        top = jnp.max(jnp.where(allowed, scores, -jnp.inf), axis=1, keepdims=True)
        weights = jnp.where(allowed, jnp.exp(scores - top), 0.0)
        total = jnp.sum(weights, axis=1, keepdims=True)
        mixed = jnp.dot(weights.astype(jnp.bfloat16), value, preferred_element_type=jnp.float32)
        return (mixed / total).astype(jnp.bfloat16)

    heads_out = lax.map(one_head, jnp.arange(QH, dtype=jnp.int32))
    attention = heads_out.transpose(1, 0, 2).reshape(TOKENS, QH * HD)

    paired = jnp.stack([keys.reshape(TOKENS, KVH, HD), values.reshape(TOKENS, KVH, HD)], axis=2)
    pages = paired.reshape(PAGES, PAGE, KVH * 2 * HD)
    owner = page_owner[:, 0].astype(jnp.int32)
    onehot = (owner[:, None] == jnp.arange(N_PRE, dtype=jnp.int32)[None, :]).astype(jnp.int32)
    blocks = onehot.reshape(N_PRE, PAGES_DEV, N_PRE)
    before = (jnp.cumsum(blocks, axis=1) - blocks).reshape(PAGES, N_PRE)
    rank = jnp.sum(before * onehot, axis=1).astype(jnp.int32)
    source = (jnp.arange(PAGES, dtype=jnp.int32) // PAGES_DEV).astype(jnp.int32)
    cache = jnp.zeros((N_PRE, N_PRE, PAGE_CAP, PAGE, KVH * 2 * HD), keys.dtype)
    cache = cache.at[owner, source, rank].set(pages)
    return attention, cache.reshape(N_PRE, N_PRE, PAGE_CAP * PAGE, KVH * 2 * HD)
```

```python
import functools
import math

import jax
import jax.numpy as jnp
from jax import lax
from jax.experimental import pallas as pl
from jax.experimental.pallas import tpu as pltpu
from jax.sharding import PartitionSpec as P

HD = 128
PAGE = 16
NEG = -1e30
VMEM_LIMIT = 48 * 1024 * 1024


def attention_kernel(heads, span, info, slots, q_ref, kv_ref, start_ref, out_ref, cache_ref, acc, top):
    index = info[0]
    first = info[1]
    factor = HD**-0.5 * math.log2(math.e)
    columns = lax.broadcasted_iota(jnp.int32, (span, span), 1)
    rows = lax.broadcasted_iota(jnp.int32, (span, span), 0)

    def block(j, diagonal):
        at = pl.multiple_of(j * span, span)
        keys = kv_ref[pl.ds(at, span), :HD]
        values = jnp.concatenate(
            [kv_ref[pl.ds(at, span), HD:], jnp.ones((span, HD), jnp.bfloat16)], axis=1
        )
        allowed = columns >= start_ref[...] - at
        if diagonal:
            allowed = allowed & (columns <= rows)
        for g in range(heads):
            scores = lax.dot_general(
                q_ref[:, g * HD : (g + 1) * HD],
                keys,
                (((1,), (1,)), ((), ())),
                preferred_element_type=jnp.float32,
            )
            scores = jnp.where(allowed, scores, NEG)
            peak = jnp.max(scores, axis=1, keepdims=True)
            if not diagonal:
                before = top[g]
                peak = jnp.maximum(peak, before)
            weights = jnp.exp2(scores * factor - peak * factor).astype(jnp.bfloat16)
            mixed = jnp.dot(weights, values, preferred_element_type=jnp.float32)
            if not diagonal:
                mixed = mixed + acc[g] * jnp.exp2((before - peak) * factor)
            top[g] = peak
            acc[g] = mixed

    block(index, True)

    @pl.loop(first, index)
    def _(j):
        block(j, False)

    for g in range(heads):
        mixed = acc[g]
        out_ref[:, g * HD : (g + 1) * HD] = (mixed[:, :HD] / mixed[:, HD:]).astype(out_ref.dtype)

    capacity = cache_ref.shape[1] // PAGE
    for s in range(cache_ref.shape[0]):

        @pl.loop(0, capacity)
        def _(r):
            page = slots[s * capacity + r]
            held = kv_ref[pl.ds(pl.multiple_of(jnp.maximum(page, 0) * PAGE, PAGE), PAGE), :]
            cache_ref[s, pl.ds(pl.multiple_of(r * PAGE, PAGE), PAGE), :] = jnp.where(
                page >= 0, held, jnp.zeros_like(held)
            )


def attention(info, slots, queries, kv, start, n_pre, capacity):
    span = queries.shape[0]
    heads = queries.shape[1] // HD
    return pl.pallas_call(
        functools.partial(attention_kernel, heads, span),
        in_specs=[
            pl.BlockSpec(memory_space=pltpu.SMEM),
            pl.BlockSpec(memory_space=pltpu.SMEM),
            pl.BlockSpec(memory_space=pltpu.VMEM),
            pl.BlockSpec(memory_space=pltpu.VMEM),
            pl.BlockSpec(memory_space=pltpu.VMEM),
        ],
        out_specs=[
            pl.BlockSpec(memory_space=pltpu.VMEM),
            pl.BlockSpec(memory_space=pltpu.VMEM),
        ],
        out_shape=[
            jax.ShapeDtypeStruct(queries.shape, jnp.bfloat16),
            jax.ShapeDtypeStruct((n_pre, capacity * PAGE, 2 * HD), jnp.bfloat16),
        ],
        scratch_shapes=[
            pltpu.VMEM((heads, span, 2 * HD), jnp.float32),
            pltpu.VMEM((heads, span, 1), jnp.float32),
        ],
        compiler_params=pltpu.CompilerParams(vmem_limit_bytes=VMEM_LIMIT),
        cost_estimate=pl.CostEstimate(
            flops=4 * heads * span * span * n_pre * HD,
            bytes_accessed=4 * queries.size * 2,
            transcendentals=heads * span * span * n_pre,
        ),
        name="attention",
    )(info, slots, queries, kv, start)


STEP = 1024


def project_kernel(mode, place, own_ref, outer_ref, kw_ref, vw_ref, *rest):
    if mode == "first":
        (acc,) = rest
    elif mode == "middle":
        before, acc = rest
    else:
        before, kb_ref, vb_ref, kv_ref, acc = rest
    k = pl.program_id(0)
    span = own_ref.shape[0]

    @pl.when(k == 0)
    def _():
        acc[...] = jnp.zeros_like(acc) if mode == "first" else before[...]

    weights = jnp.concatenate([kw_ref[...], vw_ref[...]], axis=1)
    acc[:span] += jnp.dot(own_ref[...], weights, preferred_element_type=jnp.float32)
    acc[span:] += jnp.dot(outer_ref[0], weights, preferred_element_type=jnp.float32)
    if mode == "last":

        @pl.when(k == pl.num_programs(0) - 1)
        def _():
            bias = jnp.concatenate([kb_ref[...], vb_ref[...]], axis=1).astype(jnp.float32)
            done = (acc[...] + bias).astype(jnp.bfloat16)
            own_at = pl.multiple_of(place[1] * span, span)
            outer_at = pl.multiple_of((1 - place[1]) * span, span)
            kv_ref[pl.ds(own_at, span), :] = done[:span]
            kv_ref[pl.ds(outer_at, span), :] = done[span:]


def project(mode, place, own, outer, key_weight, value_weight, before=None, biases=None):
    span = own.shape[0]
    depth = key_weight.shape[0]
    steps = depth // STEP
    columns = 2 * HD
    in_specs = [
        pl.BlockSpec((span, STEP), lambda k, place: (0, place[0] + k)),
        pl.BlockSpec((1, span, STEP), lambda k, place: (place[0] + k, 0, 0)),
        pl.BlockSpec((STEP, HD), lambda k, place: (k, 0)),
        pl.BlockSpec((STEP, HD), lambda k, place: (k, 0)),
    ]
    operands = [own, outer, key_weight, value_weight]
    whole = pl.BlockSpec((2 * span, columns), lambda k, place: (0, 0))
    if mode != "first":
        in_specs.append(whole)
        operands.append(before)
    out_shape = jax.ShapeDtypeStruct((2 * span, columns), jnp.float32)
    scratch = []
    if mode == "last":
        in_specs += [pl.BlockSpec((1, HD), lambda k, place: (0, 0))] * 2
        operands += biases
        out_shape = jax.ShapeDtypeStruct((2 * span, columns), jnp.bfloat16)
        scratch = [pltpu.VMEM((2 * span, columns), jnp.float32)]
    return pl.pallas_call(
        functools.partial(project_kernel, mode),
        grid_spec=pltpu.PrefetchScalarGridSpec(
            num_scalar_prefetch=1,
            grid=(steps,),
            in_specs=in_specs,
            out_specs=whole,
            scratch_shapes=scratch,
        ),
        out_shape=out_shape,
        compiler_params=pltpu.CompilerParams(
            vmem_limit_bytes=VMEM_LIMIT, dimension_semantics=("arbitrary",)
        ),
        cost_estimate=pl.CostEstimate(
            flops=4 * span * depth * columns,
            bytes_accessed=4 * span * depth + 2 * depth * columns + 8 * span * columns,
            transcendentals=0,
        ),
        name="project_" + mode,
    )(place, *operands)


INWARD = [(0, 1), (3, 2)]
ACROSS = [(1, 2), (2, 1)]
OUTWARD = [(1, 0), (2, 3)]


def line_of_four(hidden, key_weight, value_weight, key_bias, value_bias):
    index = lax.axis_index("pre")
    span, width = hidden.shape
    depth = key_weight.shape[0]
    share = width // lax.axis_size(("dec", "tp"))
    mine = lax.axis_index(("dec", "tp")) * share

    def send(x, pairs):
        return lax.ppermute(x, "pre", pairs)

    cut = lax.dynamic_slice_in_dim(hidden, mine, share, axis=1)
    cut = send(cut, INWARD)
    other = lax.all_gather(cut, ("dec", "tp"))
    half = depth // 2
    parts = [
        (key_weight[:half], value_weight[:half]),
        (key_weight[half:], value_weight[half:]),
    ]
    crossed = [send(key_weight, ACROSS), send(value_weight, ACROSS)]
    came, far = [], []
    for part in parts:
        got = [send(part[0], INWARD), send(part[1], INWARD)]
        came.append(got)
        far.append([send(got[0], ACROSS), send(got[1], ACROSS)])

    blocks = depth // STEP
    second = jnp.where(index < 2, 1, 0)
    facing = 3 - index

    def place(chunk, row=0):
        return jnp.stack([chunk * blocks + row // STEP, second]).astype(jnp.int32)

    acc = project("first", place(index), hidden, other, key_weight, value_weight)
    acc = project("middle", place(facing), hidden, other, crossed[0], crossed[1], acc)
    outer = jnp.bitwise_xor(index, 1)
    for i in range(2):
        acc = project("middle", place(outer, i * half), hidden, other, came[i][0], came[i][1], acc)
    distant = jnp.bitwise_xor(facing, 1)
    acc = project("middle", place(distant), hidden, other, far[0][0], far[0][1], acc)
    pair = project(
        "last",
        place(distant, half),
        hidden,
        other,
        far[1][0],
        far[1][1],
        acc,
        [key_bias[None, :], value_bias[None, :]],
    )
    facing_pair = send(pair, ACROSS)
    own_pair = send(pair, OUTWARD)
    far_pair = send(facing_pair, OUTWARD)
    low = jnp.where(
        index == 0, own_pair, jnp.where(index == 1, pair, jnp.where(index == 2, facing_pair, far_pair))
    )
    high = jnp.where(
        index == 3, own_pair, jnp.where(index == 2, pair, jnp.where(index == 1, facing_pair, far_pair))
    )
    return jnp.concatenate([low, high], axis=0)


def gathered(hidden, key_weight, value_weight, key_bias, value_bias):
    joined = jnp.concatenate([key_weight, value_weight], axis=1)
    joined = lax.all_gather(joined, "pre", axis=0, tiled=True)
    bias = jnp.concatenate([key_bias, value_bias]).astype(jnp.float32)
    local = jnp.dot(hidden, joined, preferred_element_type=jnp.float32) + bias
    return lax.all_gather(local.astype(jnp.bfloat16), "pre", axis=0, tiled=True)


def body(hidden, queries, key_weight, value_weight, key_bias, value_bias, segment_ids, page_owner):
    n_pre = lax.axis_size("pre")
    index = lax.axis_index("pre")
    span = hidden.shape[0]
    pages_dev = span // PAGE
    capacity = 2 * pages_dev // n_pre
    assert key_weight.shape[1] == HD

    owners = lax.all_gather(page_owner[:, 0], "pre")
    mine = (owners == index).astype(jnp.int32)
    rank = jnp.cumsum(mine, axis=1) - mine
    numbers = jnp.arange(n_pre * pages_dev, dtype=jnp.int32).reshape(n_pre, 1, pages_dev)
    wanted = (mine[:, None, :] == 1) & (
        rank[:, None, :] == jnp.arange(capacity, dtype=jnp.int32)[None, :, None]
    )
    slots = jnp.max(jnp.where(wanted, numbers, -1), axis=2).reshape(-1)

    own_segments = lax.dynamic_slice_in_dim(segment_ids, index * span, span)
    start = jnp.sum(
        (segment_ids[None, :] < own_segments[:, None]).astype(jnp.int32), axis=1, keepdims=True
    )
    info = jnp.stack([index, start[0, 0] // span]).astype(jnp.int32)

    project_all = line_of_four if n_pre == 4 else gathered
    kv = project_all(hidden, key_weight, value_weight, key_bias, value_bias)
    mixed, cache = attention(info, slots, queries, kv, start, n_pre, capacity)
    return (mixed, cache[None])


def solution(mesh):
    return jax.shard_map(
        body,
        mesh=mesh,
        in_specs=(
            P(("group", "pre"), None),
            P(("group", "pre"), ("dec", "tp")),
            P("pre", ("dec", "tp")),
            P("pre", ("dec", "tp")),
            P(("dec", "tp")),
            P(("dec", "tp")),
            P("group"),
            P(("group", "pre"), None),
        ),
        out_specs=(
            P(("group", "pre"), ("dec", "tp")),
            P(("group", "pre"), None, None, ("dec", "tp")),
        ),
        check_vma=False,
    )
```

```python
import functools
import math

import jax
import jax.numpy as jnp
from jax import lax
from jax.experimental import pallas as pl
from jax.experimental.pallas import tpu as pltpu
from jax.sharding import PartitionSpec as P

HD = 128
PAGE = 16
NEG = -1e30
VMEM_LIMIT = 48 * 1024 * 1024


def attention_kernel(heads, span, info, slots, q_ref, k_ref, v_ref, start_ref, out_ref, cache_ref, acc, top):
    index = info[0]
    first = info[1]
    factor = HD**-0.5 * math.log2(math.e)
    columns = lax.broadcasted_iota(jnp.int32, (span, span), 1)
    rows = lax.broadcasted_iota(jnp.int32, (span, span), 0)

    def block(j, diagonal):
        at = pl.multiple_of(j * span, span)
        keys = k_ref[pl.ds(at, span), :]
        values = jnp.concatenate(
            [v_ref[pl.ds(at, span), :], jnp.ones((span, HD), jnp.bfloat16)], axis=1
        )
        allowed = columns >= start_ref[...] - at
        if diagonal:
            allowed = allowed & (columns <= rows)
        for g in range(heads):
            scores = lax.dot_general(
                q_ref[:, g * HD : (g + 1) * HD],
                keys,
                (((1,), (1,)), ((), ())),
                preferred_element_type=jnp.float32,
            )
            scores = jnp.where(allowed, scores, NEG)
            peak = jnp.max(scores, axis=1, keepdims=True)
            if not diagonal:
                before = top[g]
                peak = jnp.maximum(peak, before)
            weights = jnp.exp2(scores * factor - peak * factor).astype(jnp.bfloat16)
            mixed = jnp.dot(weights, values, preferred_element_type=jnp.float32)
            if not diagonal:
                mixed = mixed + acc[g] * jnp.exp2((before - peak) * factor)
            top[g] = peak
            acc[g] = mixed

    block(index, True)

    @pl.loop(first, index)
    def _(j):
        block(j, False)

    for g in range(heads):
        mixed = acc[g]
        out_ref[:, g * HD : (g + 1) * HD] = (mixed[:, :HD] / mixed[:, HD:]).astype(out_ref.dtype)

    capacity = cache_ref.shape[1] // PAGE
    for s in range(cache_ref.shape[0]):

        @pl.loop(0, capacity)
        def _(r):
            page = slots[s * capacity + r]
            token = pl.ds(pl.multiple_of(jnp.maximum(page, 0) * PAGE, PAGE), PAGE)
            row = pl.ds(pl.multiple_of(r * PAGE, PAGE), PAGE)
            empty = jnp.zeros((PAGE, HD), cache_ref.dtype)
            cache_ref[s, row, :HD] = jnp.where(page >= 0, k_ref[token, :], empty)
            cache_ref[s, row, HD:] = jnp.where(page >= 0, v_ref[token, :], empty)


def attention(info, slots, queries, keys, values, start, n_pre, capacity):
    span = queries.shape[0]
    heads = queries.shape[1] // HD
    return pl.pallas_call(
        functools.partial(attention_kernel, heads, span),
        in_specs=[
            pl.BlockSpec(memory_space=pltpu.SMEM),
            pl.BlockSpec(memory_space=pltpu.SMEM),
            pl.BlockSpec(memory_space=pltpu.VMEM),
            pl.BlockSpec(memory_space=pltpu.VMEM),
            pl.BlockSpec(memory_space=pltpu.VMEM),
            pl.BlockSpec(memory_space=pltpu.VMEM),
        ],
        out_specs=[
            pl.BlockSpec(memory_space=pltpu.VMEM),
            pl.BlockSpec(memory_space=pltpu.VMEM),
        ],
        out_shape=[
            jax.ShapeDtypeStruct(queries.shape, jnp.bfloat16),
            jax.ShapeDtypeStruct((n_pre, capacity * PAGE, 2 * HD), jnp.bfloat16),
        ],
        scratch_shapes=[
            pltpu.VMEM((heads, span, 2 * HD), jnp.float32),
            pltpu.VMEM((heads, span, 1), jnp.float32),
        ],
        compiler_params=pltpu.CompilerParams(vmem_limit_bytes=VMEM_LIMIT),
        cost_estimate=pl.CostEstimate(
            flops=4 * heads * span * span * n_pre * HD,
            bytes_accessed=4 * queries.size * 2,
            transcendentals=heads * span * span * n_pre,
        ),
        name="attention",
    )(info, slots, queries, keys, values, start)


STEP = 1024


def project_kernel(spans, last, place, *refs):
    refs = list(refs)
    span_refs = [refs.pop(0) for _ in range(spans)]
    weight_refs = [refs.pop(0) for _ in range(3 - spans)]
    before = [refs.pop(0) for _ in range(spans)] if spans == 2 else []
    bias_ref = refs.pop(0) if last else None
    out_ref = refs.pop(0)
    acc = refs.pop(0) if last else out_ref
    k = pl.program_id(0)
    span = span_refs[0].shape[-2]
    half = pl.num_programs(0) // 2

    @pl.when(k == 0)
    def _():
        if spans == 1:
            acc[...] = jnp.zeros_like(acc)
        else:
            acc[:span] = before[0][...]
            acc[span:] = before[1][...]

    if spans == 1:
        weight = jnp.where(k < half, weight_refs[0][...], weight_refs[1][...])
        acc[...] += jnp.dot(span_refs[0][...], weight, preferred_element_type=jnp.float32)
    else:
        weight = weight_refs[0][...]
        acc[:span] += jnp.dot(span_refs[0][...], weight, preferred_element_type=jnp.float32)
        share = span_refs[1].shape[2]
        for i in range(STEP // share):
            acc[span:] += jnp.dot(
                span_refs[1][i],
                weight[i * share : (i + 1) * share],
                preferred_element_type=jnp.float32,
            )
    if last:

        @pl.when(k == pl.num_programs(0) - 1)
        def _():
            done = (acc[...] + bias_ref[...].astype(jnp.float32)).astype(jnp.bfloat16)
            own_at = pl.multiple_of(place[2] * span, span)
            outer_at = pl.multiple_of((1 - place[2]) * span, span)
            out_ref[pl.ds(own_at, span), :] = done[:span]
            out_ref[pl.ds(outer_at, span), :] = done[span:]


def compiled_with(span, depth, rows):
    return dict(
        compiler_params=pltpu.CompilerParams(
            vmem_limit_bytes=VMEM_LIMIT, dimension_semantics=("arbitrary",)
        ),
        cost_estimate=pl.CostEstimate(
            flops=2 * rows * depth * HD,
            bytes_accessed=2 * rows * depth + 2 * depth * HD + 8 * rows * HD,
            transcendentals=0,
        ),
    )


def project_near(place, own, weight, swapped):
    span = own.shape[0]
    depth = weight.shape[0]
    steps = depth // STEP
    return pl.pallas_call(
        functools.partial(project_kernel, 1, False),
        grid_spec=pltpu.PrefetchScalarGridSpec(
            num_scalar_prefetch=1,
            grid=(2 * steps,),
            in_specs=[
                pl.BlockSpec(
                    (span, STEP), lambda k, place: (0, place[k // steps] + lax.rem(k, steps))
                ),
                pl.BlockSpec((STEP, HD), lambda k, place: (jnp.minimum(k, steps - 1), 0)),
                pl.BlockSpec((STEP, HD), lambda k, place: (jnp.maximum(k - steps, 0), 0)),
            ],
            out_specs=pl.BlockSpec((span, HD), lambda k, place: (0, 0)),
        ),
        out_shape=jax.ShapeDtypeStruct((span, HD), jnp.float32),
        name="project_near",
        **compiled_with(span, 2 * depth, span),
    )(place, own, weight, swapped)


def project_far(place, own, other, weight, before, bias=None):
    span = own.shape[0]
    depth = weight.shape[0]
    share = other.shape[2]
    last = bias is not None
    half = pl.BlockSpec((span, HD), lambda k, place: (0, 0))
    whole = pl.BlockSpec((2 * span, HD), lambda k, place: (0, 0))
    in_specs = [
        pl.BlockSpec((span, STEP), lambda k, place: (0, place[0] + k)),
        pl.BlockSpec((STEP // share, span, share), lambda k, place: (place[1] + k, 0, 0)),
        pl.BlockSpec((STEP, HD), lambda k, place: (k, 0)),
    ]
    operands = [own, other, weight]
    if isinstance(before, tuple):
        in_specs += [half, half]
        operands += before
    else:
        in_specs += [half, pl.BlockSpec((span, HD), lambda k, place: (1, 0))]
        operands += [before, before]
    scratch = []
    if last:
        in_specs.append(pl.BlockSpec((1, HD), lambda k, place: (0, 0)))
        operands.append(bias)
        scratch = [pltpu.VMEM((2 * span, HD), jnp.float32)]
    return pl.pallas_call(
        functools.partial(project_kernel, 2, last),
        grid_spec=pltpu.PrefetchScalarGridSpec(
            num_scalar_prefetch=1,
            grid=(depth // STEP,),
            in_specs=in_specs,
            out_specs=whole,
            scratch_shapes=scratch,
        ),
        out_shape=jax.ShapeDtypeStruct((2 * span, HD), jnp.bfloat16 if last else jnp.float32),
        name="project_last" if last else "project_far",
        **compiled_with(span, depth, 2 * span),
    )(place, *operands)


INWARD = [(0, 1), (3, 2)]
ACROSS = [(1, 2), (2, 1)]
OUTWARD = [(1, 0), (2, 3)]
SWAP = [(0, 1), (1, 0), (2, 3), (3, 2)]


def line_of_four(hidden, key_weight, value_weight, key_bias, value_bias):
    index = lax.axis_index("pre")
    span, width = hidden.shape
    depth = key_weight.shape[0]
    blocks = depth // STEP
    share = width // 2 // lax.axis_size(("dec", "tp"))
    facing = 3 - index
    near = jnp.bitwise_xor(index, 1)
    distant = jnp.bitwise_xor(facing, 1)
    second = (index < 2).astype(jnp.int32)

    def send(x, pairs):
        return lax.ppermute(x, "pre", pairs)

    mine = second * (width // 2) + lax.axis_index(("dec", "tp")) * share
    cut = send(lax.dynamic_slice_in_dim(hidden, mine, share, axis=1), INWARD)
    key_facing = send(key_weight, ACROSS)
    cut, key_facing = lax.optimization_barrier((cut, key_facing))
    other = lax.all_gather(cut, ("dec", "tp"))

    def chain(weight, faced, bias):
        swapped = send(weight, SWAP)
        faced = send(weight, ACROSS) if faced is None else faced
        crossed = send(swapped, ACROSS)
        at_near = jnp.stack([index * blocks, near * blocks])
        own = project_near(at_near, hidden, weight, swapped)
        outer = send(own, INWARD)

        def place(chunk):
            return jnp.stack([chunk * blocks, lax.rem(chunk, 2) * blocks, second])

        total = project_far(place(facing), hidden, other, faced, (own, outer))
        pair = project_far(place(distant), hidden, other, crossed, total, bias[None, :])
        facing_pair = send(pair, ACROSS)
        own_pair = send(pair, OUTWARD)
        far_pair = send(facing_pair, OUTWARD)
        low = jnp.where(
            index == 0, own_pair, jnp.where(index == 1, pair, jnp.where(index == 2, facing_pair, far_pair))
        )
        high = jnp.where(
            index == 3, own_pair, jnp.where(index == 2, pair, jnp.where(index == 1, facing_pair, far_pair))
        )
        return jnp.concatenate([low, high], axis=0)

    return chain(key_weight, key_facing, key_bias), chain(value_weight, None, value_bias)


def gathered(hidden, key_weight, value_weight, key_bias, value_bias):
    joined = jnp.concatenate([key_weight, value_weight], axis=1)
    joined = lax.all_gather(joined, "pre", axis=0, tiled=True)
    bias = jnp.concatenate([key_bias, value_bias]).astype(jnp.float32)
    local = jnp.dot(hidden, joined, preferred_element_type=jnp.float32) + bias
    both = lax.all_gather(local.astype(jnp.bfloat16), "pre", axis=0, tiled=True)
    return both[:, :HD], both[:, HD:]


def body(hidden, queries, key_weight, value_weight, key_bias, value_bias, segment_ids, page_owner):
    n_pre = lax.axis_size("pre")
    index = lax.axis_index("pre")
    span = hidden.shape[0]
    pages_dev = span // PAGE
    capacity = 2 * pages_dev // n_pre
    assert key_weight.shape[1] == HD

    owners = lax.all_to_all(
        jnp.broadcast_to(page_owner[:, 0], (n_pre, pages_dev)), "pre", 0, 0, tiled=True
    )
    mine = (owners == index).astype(jnp.int32)
    rank = jnp.cumsum(mine, axis=1) - mine
    numbers = jnp.arange(n_pre * pages_dev, dtype=jnp.int32).reshape(n_pre, 1, pages_dev)
    wanted = (mine[:, None, :] == 1) & (
        rank[:, None, :] == jnp.arange(capacity, dtype=jnp.int32)[None, :, None]
    )
    slots = jnp.max(jnp.where(wanted, numbers, -1), axis=2).reshape(-1)

    own_segments = lax.dynamic_slice_in_dim(segment_ids, index * span, span)
    start = jnp.sum(
        (segment_ids[None, :] < own_segments[:, None]).astype(jnp.int32), axis=1, keepdims=True
    )
    info = jnp.stack([index, start[0, 0] // span]).astype(jnp.int32)

    project_all = line_of_four if n_pre == 4 else gathered
    keys, values = project_all(hidden, key_weight, value_weight, key_bias, value_bias)
    mixed, cache = attention(info, slots, queries, keys, values, start, n_pre, capacity)
    return (mixed, cache[None])


def solution(mesh):
    return jax.shard_map(
        body,
        mesh=mesh,
        in_specs=(
            P(("group", "pre"), None),
            P(("group", "pre"), ("dec", "tp")),
            P("pre", ("dec", "tp")),
            P("pre", ("dec", "tp")),
            P(("dec", "tp")),
            P(("dec", "tp")),
            P("group"),
            P(("group", "pre"), None),
        ),
        out_specs=(
            P(("group", "pre"), ("dec", "tp")),
            P(("group", "pre"), None, None, ("dec", "tp")),
        ),
        check_vma=False,
    )
```

```python
import functools
import math

import jax
import jax.numpy as jnp
from jax import lax
from jax.experimental import pallas as pl
from jax.experimental.pallas import tpu as pltpu
from jax.sharding import PartitionSpec as P

HD = 128
PAGE = 16
NEG = -1e30
VMEM_LIMIT = 48 * 1024 * 1024


def attention_kernel(heads, span, info, slots, q_ref, k_ref, v_ref, start_ref, out_ref, cache_ref, acc, top):
    index = info[0]
    first = info[1]
    factor = HD**-0.5 * math.log2(math.e)
    columns = lax.broadcasted_iota(jnp.int32, (span, span), 1)
    rows = lax.broadcasted_iota(jnp.int32, (span, span), 0)

    def block(j, diagonal):
        at = pl.multiple_of(j * span, span)
        keys = k_ref[pl.ds(at, span), :]
        values = jnp.concatenate(
            [v_ref[pl.ds(at, span), :], jnp.ones((span, HD), jnp.bfloat16)], axis=1
        )
        allowed = columns >= start_ref[...] - at
        if diagonal:
            allowed = allowed & (columns <= rows)
        for g in range(heads):
            scores = lax.dot_general(
                q_ref[:, g * HD : (g + 1) * HD],
                keys,
                (((1,), (1,)), ((), ())),
                preferred_element_type=jnp.float32,
            )
            scores = jnp.where(allowed, scores, NEG)
            peak = jnp.max(scores, axis=1, keepdims=True)
            if not diagonal:
                before = top[g]
                peak = jnp.maximum(peak, before)
            weights = jnp.exp2(scores * factor - peak * factor).astype(jnp.bfloat16)
            mixed = jnp.dot(weights, values, preferred_element_type=jnp.float32)
            if not diagonal:
                mixed = mixed + acc[g] * jnp.exp2((before - peak) * factor)
            top[g] = peak
            acc[g] = mixed

    block(index, True)

    @pl.loop(first, index)
    def _(j):
        block(j, False)

    for g in range(heads):
        mixed = acc[g]
        out_ref[:, g * HD : (g + 1) * HD] = (mixed[:, :HD] / mixed[:, HD:]).astype(out_ref.dtype)

    pick_pages(slots, k_ref, v_ref, cache_ref)


def attention(info, slots, queries, keys, values, start, n_pre, capacity):
    span = queries.shape[0]
    heads = queries.shape[1] // HD
    return pl.pallas_call(
        functools.partial(attention_kernel, heads, span),
        in_specs=[
            pl.BlockSpec(memory_space=pltpu.SMEM),
            pl.BlockSpec(memory_space=pltpu.SMEM),
            pl.BlockSpec(memory_space=pltpu.VMEM),
            pl.BlockSpec(memory_space=pltpu.VMEM),
            pl.BlockSpec(memory_space=pltpu.VMEM),
            pl.BlockSpec(memory_space=pltpu.VMEM),
        ],
        out_specs=[
            pl.BlockSpec(memory_space=pltpu.VMEM),
            pl.BlockSpec(memory_space=pltpu.VMEM),
        ],
        out_shape=[
            jax.ShapeDtypeStruct(queries.shape, jnp.bfloat16),
            jax.ShapeDtypeStruct((n_pre, capacity * PAGE, 2 * HD), jnp.bfloat16),
        ],
        scratch_shapes=[
            pltpu.VMEM((heads, span, 2 * HD), jnp.float32),
            pltpu.VMEM((heads, span, 1), jnp.float32),
        ],
        compiler_params=pltpu.CompilerParams(vmem_limit_bytes=VMEM_LIMIT),
        cost_estimate=pl.CostEstimate(
            flops=4 * heads * span * span * n_pre * HD,
            bytes_accessed=4 * queries.size * 2,
            transcendentals=heads * span * span * n_pre,
        ),
        name="attention",
    )(info, slots, queries, keys, values, start)


STEP = 1024


def near_kernel(place, own_ref, kw_ref, vw_ref, kx_ref, vx_ref, out_ref):
    k = pl.program_id(0)

    @pl.when(k == 0)
    def _():
        out_ref[...] = jnp.zeros_like(out_ref)

    def add(key_ref, value_ref):
        weight = jnp.concatenate([key_ref[...], value_ref[...]], axis=1)
        out_ref[...] += jnp.dot(own_ref[...], weight, preferred_element_type=jnp.float32)

    @pl.when(k < pl.num_programs(0) // 2)
    def _():
        add(kw_ref, vw_ref)

    @pl.when(k >= pl.num_programs(0) // 2)
    def _():
        add(kx_ref, vx_ref)


def facing_kernel(place, own_ref, other_ref, kw_ref, vw_ref, out_ref):
    k = pl.program_id(0)
    span = own_ref.shape[0]
    share = other_ref.shape[3]

    @pl.when(k == 0)
    def _():
        out_ref[...] = jnp.zeros_like(out_ref)

    weight = jnp.concatenate([kw_ref[...], vw_ref[...]], axis=1)
    other = jnp.concatenate([other_ref[i, 0] for i in range(STEP // share)], axis=1)
    out_ref[:span] += jnp.dot(own_ref[...], weight, preferred_element_type=jnp.float32)
    out_ref[span:] += jnp.dot(other, weight, preferred_element_type=jnp.float32)


def distant_kernel(
    place, own_ref, other_ref, w_ref, near_ref, outer_ref, facing_ref, bias_ref, out_ref, acc
):
    k = pl.program_id(0)
    span = own_ref.shape[0]
    share = other_ref.shape[3]

    @pl.when(k == 0)
    def _():
        bias = bias_ref[...].astype(jnp.float32)
        acc[:span] = near_ref[...] + facing_ref[:span] + bias
        acc[span:] = outer_ref[...] + facing_ref[span:] + bias

    weight = w_ref[...]
    other = jnp.concatenate([other_ref[i, 0] for i in range(STEP // share)], axis=1)
    acc[:span] += jnp.dot(own_ref[...], weight, preferred_element_type=jnp.float32)
    acc[span:] += jnp.dot(other, weight, preferred_element_type=jnp.float32)

    @pl.when(k == pl.num_programs(0) - 1)
    def _():
        own_at = pl.multiple_of(place[2] * span, span)
        outer_at = pl.multiple_of((1 - place[2]) * span, span)
        out_ref[pl.ds(own_at, span), :] = acc[:span].astype(jnp.bfloat16)
        out_ref[pl.ds(outer_at, span), :] = acc[span:].astype(jnp.bfloat16)


def call_project(kernel, name, place, operands, in_specs, steps, rows, columns, kind, scratch=()):
    return pl.pallas_call(
        kernel,
        grid_spec=pltpu.PrefetchScalarGridSpec(
            num_scalar_prefetch=1,
            grid=(steps,),
            in_specs=in_specs,
            out_specs=pl.BlockSpec((rows, columns), lambda k, place: (0, 0)),
            scratch_shapes=list(scratch),
        ),
        out_shape=jax.ShapeDtypeStruct((rows, columns), kind),
        compiler_params=pltpu.CompilerParams(
            vmem_limit_bytes=VMEM_LIMIT, dimension_semantics=("arbitrary",)
        ),
        cost_estimate=pl.CostEstimate(
            flops=2 * rows * STEP * steps * columns,
            bytes_accessed=2 * rows * STEP * steps + 2 * STEP * steps * columns,
            transcendentals=0,
        ),
        name=name,
    )(place, *operands)


def project_near(place, own, key_weight, value_weight, key_swapped, value_swapped):
    span = own.shape[0]
    steps = key_weight.shape[0] // STEP
    first = pl.BlockSpec((STEP, HD), lambda k, place: (jnp.minimum(k, steps - 1), 0))
    second = pl.BlockSpec((STEP, HD), lambda k, place: (jnp.maximum(k - steps, 0), 0))
    in_specs = [
        pl.BlockSpec((span, STEP), lambda k, place: (0, place[k // steps] + lax.rem(k, steps))),
        first,
        first,
        second,
        second,
    ]
    operands = [own, key_weight, value_weight, key_swapped, value_swapped]
    return call_project(
        near_kernel, "near", place, operands, in_specs, 2 * steps, span, 2 * HD, jnp.float32
    )


def far_specs(span, share):
    return [
        pl.BlockSpec((span, STEP), lambda k, place: (0, place[0] + k)),
        pl.BlockSpec((STEP // share, 1, span, share), lambda k, place: (0, place[1] + k, 0, 0)),
    ]


def project_facing(place, own, other, key_weight, value_weight):
    span = own.shape[0]
    weight = pl.BlockSpec((STEP, HD), lambda k, place: (k, 0))
    in_specs = far_specs(span, other.shape[3]) + [weight, weight]
    operands = [own, other, key_weight, value_weight]
    steps = key_weight.shape[0] // STEP
    return call_project(
        facing_kernel, "facing", place, operands, in_specs, steps, 2 * span, 2 * HD, jnp.float32
    )


def project_distant(place, column, own, other, weight, near, outer, facing, bias):
    span = own.shape[0]
    part = pl.BlockSpec((span, HD), lambda k, place: (0, column))
    in_specs = far_specs(span, other.shape[3]) + [
        pl.BlockSpec((STEP, HD), lambda k, place: (k, 0)),
        part,
        part,
        pl.BlockSpec((2 * span, HD), lambda k, place: (0, column)),
        pl.BlockSpec((1, HD), lambda k, place: (0, 0)),
    ]
    operands = [own, other, weight, near, outer, facing, bias]
    return call_project(
        distant_kernel,
        "distant",
        place,
        operands,
        in_specs,
        weight.shape[0] // STEP,
        2 * span,
        HD,
        jnp.bfloat16,
        [pltpu.VMEM((2 * span, HD), jnp.float32)],
    )


INWARD = [(0, 1), (3, 2)]
ACROSS = [(1, 2), (2, 1)]
OUTWARD = [(1, 0), (2, 3)]
SWAP = [(0, 1), (1, 0), (2, 3), (3, 2)]


def line_of_four(hidden, key_weight, value_weight, key_bias, value_bias, owners):
    index = lax.axis_index("pre")
    width = hidden.shape[1]
    blocks = key_weight.shape[0] // STEP
    share = width // 2 // lax.axis_size(("dec", "tp"))
    facing = 3 - index
    near = jnp.bitwise_xor(index, 1)
    distant = jnp.bitwise_xor(facing, 1)
    second = (index < 2).astype(jnp.int32)

    def send(x, pairs):
        return lax.ppermute(x, "pre", pairs)

    mine = second * (width // 2) + lax.axis_index(("dec", "tp")) * share
    cut = send(lax.dynamic_slice_in_dim(hidden, mine, share, axis=1), INWARD)
    key_facing = send(key_weight, ACROSS)
    cut, key_facing, owners = lax.optimization_barrier((cut, key_facing, owners))
    other = lax.all_gather(cut, "dec")
    value_facing = send(value_weight, ACROSS)
    key_swapped = send(key_weight, SWAP)
    other, value_facing, key_swapped = lax.optimization_barrier((other, value_facing, key_swapped))
    other = lax.all_gather(other, "tp")
    value_swapped = send(value_weight, SWAP)
    key_distant = send(key_swapped, ACROSS)
    value_distant = send(value_swapped, ACROSS)

    def place(chunk):
        return jnp.stack([chunk * blocks, lax.rem(chunk, 2) * blocks, second])

    at_near = jnp.stack([index * blocks, near * blocks])
    own_part = project_near(
        at_near, hidden, key_weight, value_weight, key_swapped, value_swapped
    )
    outer_part = send(own_part, INWARD)
    faced = project_facing(place(facing), hidden, other, key_facing, value_facing)

    def finish(column, weight, bias):
        pair = project_distant(
            place(distant), column, hidden, other, weight, own_part, outer_part, faced, bias[None, :]
        )
        across = send(pair, ACROSS)
        return pair, send(pair, OUTWARD), across, send(across, OUTWARD)

    keys = finish(0, key_distant, key_bias)
    values = finish(1, value_distant, value_bias)
    return keys, values, owners


def softmax_step(q, keys, values, allowed, before):
    factor = HD**-0.5 * math.log2(math.e)
    scores = lax.dot_general(q, keys, (((1,), (1,)), ((), ())), preferred_element_type=jnp.float32)
    scores = jnp.where(allowed, scores, NEG)
    peak = jnp.max(scores, axis=1, keepdims=True)
    if before is not None:
        peak = jnp.maximum(peak, before[0])
    weights = jnp.exp2(scores * factor - peak * factor).astype(jnp.bfloat16)
    mixed = jnp.dot(weights, values, preferred_element_type=jnp.float32)
    total, mixed = mixed[:, HD:], mixed[:, :HD]
    if before is not None:
        shrink = jnp.exp2((before[0] - peak) * factor)
        total = total + before[1] * shrink
        mixed = mixed + before[2] * shrink
    return peak, total, mixed


def with_ones(values):
    return jnp.concatenate([values, jnp.ones_like(values)], axis=1)


def own_kernel(heads, info, q_ref, start_ref, k_in, k_out, v_in, v_out, top, total, mix):
    span = q_ref.shape[0]
    index = info[0]
    inner = (index == 1) | (index == 2)
    keys = jnp.where(inner, k_in[...], k_out[...])
    values = with_ones(jnp.where(inner, v_in[...], v_out[...]))
    columns = lax.broadcasted_iota(jnp.int32, (span, 2 * span), 1)
    rows = lax.broadcasted_iota(jnp.int32, (span, 2 * span), 0)
    allowed = (columns <= rows + lax.rem(index, 2) * span) & (
        columns >= start_ref[...] - (index // 2) * 2 * span
    )
    for g in range(heads):
        q = q_ref[:, g * HD : (g + 1) * HD]
        peak, sums, mixed = softmax_step(q, keys, values, allowed, None)
        top[g] = peak
        total[g] = sums[:, :1]
        mix[g] = mixed


def far_kernel(
    heads,
    info,
    slots,
    q_ref,
    start_ref,
    k_in,
    k_out,
    k_across,
    k_far,
    v_in,
    v_out,
    v_across,
    v_far,
    top,
    total,
    mix,
    out_ref,
    cache_ref,
    held_k,
    held_v,
):
    span = q_ref.shape[0]
    index = info[0]
    inner = (index == 1) | (index == 2)
    own_at = pl.multiple_of((index // 2) * 2 * span, 2 * span)
    far_at = pl.multiple_of((1 - index // 2) * 2 * span, 2 * span)
    held_k[pl.ds(own_at, 2 * span), :] = jnp.where(inner, k_in[...], k_out[...])
    held_v[pl.ds(own_at, 2 * span), :] = jnp.where(inner, v_in[...], v_out[...])
    held_k[pl.ds(far_at, 2 * span), :] = jnp.where(inner, k_across[...], k_far[...])
    held_v[pl.ds(far_at, 2 * span), :] = jnp.where(inner, v_across[...], v_far[...])

    @pl.when((index < 2) | (info[1] >= 2))
    def _():
        for g in range(heads):
            out_ref[:, g * HD : (g + 1) * HD] = (mix[g] / total[g]).astype(out_ref.dtype)

    @pl.when((index >= 2) & (info[1] < 2))
    def _():
        keys = held_k[: 2 * span]
        values = with_ones(held_v[: 2 * span])
        columns = lax.broadcasted_iota(jnp.int32, (span, 2 * span), 1)
        allowed = columns >= start_ref[...]
        for g in range(heads):
            q = q_ref[:, g * HD : (g + 1) * HD]
            _, sums, mixed = softmax_step(q, keys, values, allowed, (top[g], total[g], mix[g]))
            out_ref[:, g * HD : (g + 1) * HD] = (mixed / sums).astype(out_ref.dtype)

    pick_pages(slots, held_k, held_v, cache_ref)


def pick_pages(slots, k_ref, v_ref, cache_ref):
    capacity = cache_ref.shape[1] // PAGE
    empty = jnp.zeros((PAGE, HD), cache_ref.dtype)
    for s in range(cache_ref.shape[0]):

        @pl.loop(0, capacity)
        def _(r):
            page = slots[s * capacity + r]
            token = pl.ds(pl.multiple_of(jnp.maximum(page, 0) * PAGE, PAGE), PAGE)
            row = pl.ds(pl.multiple_of(r * PAGE, PAGE), PAGE)
            cache_ref[s, row, :HD] = jnp.where(page >= 0, k_ref[token, :], empty)
            cache_ref[s, row, HD:] = jnp.where(page >= 0, v_ref[token, :], empty)


def attention_of_pairs(info, slots, queries, start, keys, values, capacity):
    span = queries.shape[0]
    heads = queries.shape[1] // HD
    smem = pl.BlockSpec(memory_space=pltpu.SMEM)
    vmem = pl.BlockSpec(memory_space=pltpu.VMEM)
    cost = pl.CostEstimate(
        flops=8 * heads * span * span * HD,
        bytes_accessed=4 * queries.size * 2,
        transcendentals=2 * heads * span * span,
    )
    params = pltpu.CompilerParams(vmem_limit_bytes=VMEM_LIMIT)
    state = pl.pallas_call(
        functools.partial(own_kernel, heads),
        in_specs=[smem] + [vmem] * 6,
        out_specs=[vmem] * 3,
        out_shape=[
            jax.ShapeDtypeStruct((heads, span, 1), jnp.float32),
            jax.ShapeDtypeStruct((heads, span, 1), jnp.float32),
            jax.ShapeDtypeStruct((heads, span, HD), jnp.float32),
        ],
        compiler_params=params,
        cost_estimate=cost,
        name="attend_own",
    )(info, queries, start, keys[0], keys[1], values[0], values[1])
    return pl.pallas_call(
        functools.partial(far_kernel, heads),
        in_specs=[smem, smem] + [vmem] * 13,
        out_specs=[vmem] * 2,
        out_shape=[
            jax.ShapeDtypeStruct(queries.shape, jnp.bfloat16),
            jax.ShapeDtypeStruct((4, capacity * PAGE, 2 * HD), jnp.bfloat16),
        ],
        scratch_shapes=[pltpu.VMEM((4 * span, HD), jnp.bfloat16)] * 2,
        compiler_params=params,
        cost_estimate=cost,
        name="attend_far",
    )(info, slots, queries, start, *keys, *values, *state)


def gathered(hidden, key_weight, value_weight, key_bias, value_bias):
    joined = jnp.concatenate([key_weight, value_weight], axis=1)
    joined = lax.all_gather(joined, "pre", axis=0, tiled=True)
    bias = jnp.concatenate([key_bias, value_bias]).astype(jnp.float32)
    local = jnp.dot(hidden, joined, preferred_element_type=jnp.float32) + bias
    both = lax.all_gather(local.astype(jnp.bfloat16), "pre", axis=0, tiled=True)
    return both[:, :HD], both[:, HD:]


def body(hidden, queries, key_weight, value_weight, key_bias, value_bias, segment_ids, page_owner):
    n_pre = lax.axis_size("pre")
    index = lax.axis_index("pre")
    span = hidden.shape[0]
    pages_dev = span // PAGE
    capacity = 2 * pages_dev // n_pre
    assert key_weight.shape[1] == HD

    own_segments = lax.dynamic_slice_in_dim(segment_ids, index * span, span)
    start = jnp.sum(
        (segment_ids[None, :] < own_segments[:, None]).astype(jnp.int32), axis=1, keepdims=True
    )
    info = jnp.stack([index, start[0, 0] // span]).astype(jnp.int32)
    owners = lax.all_to_all(
        jnp.broadcast_to(page_owner[:, 0], (n_pre, pages_dev)), "pre", 0, 0, tiled=True
    )
    arrays = (hidden, key_weight, value_weight, key_bias, value_bias)
    if n_pre == 4:
        keys, values, owners = line_of_four(*arrays, owners)
    else:
        keys, values = gathered(*arrays)

    mine = (owners == index).astype(jnp.int32)
    rank = jnp.cumsum(mine, axis=1) - mine
    numbers = jnp.arange(n_pre * pages_dev, dtype=jnp.int32).reshape(n_pre, 1, pages_dev)
    wanted = (mine[:, None, :] == 1) & (
        rank[:, None, :] == jnp.arange(capacity, dtype=jnp.int32)[None, :, None]
    )
    slots = jnp.max(jnp.where(wanted, numbers, -1), axis=2).reshape(-1)
    if n_pre == 4:
        mixed, cache = attention_of_pairs(info, slots, queries, start, keys, values, capacity)
    else:
        mixed, cache = attention(info, slots, queries, keys, values, start, n_pre, capacity)
    return (mixed, cache[None])


def solution(mesh):
    return jax.shard_map(
        body,
        mesh=mesh,
        in_specs=(
            P(("group", "pre"), None),
            P(("group", "pre"), ("dec", "tp")),
            P("pre", ("dec", "tp")),
            P("pre", ("dec", "tp")),
            P(("dec", "tp")),
            P(("dec", "tp")),
            P("group"),
            P(("group", "pre"), None),
        ),
        out_specs=(
            P(("group", "pre"), ("dec", "tp")),
            P(("group", "pre"), None, None, ("dec", "tp")),
        ),
        check_vma=False,
    )
```

```python
import functools
import math

import jax
import jax.numpy as jnp
from jax import lax
from jax.experimental import pallas as pl
from jax.experimental.pallas import tpu as pltpu
from jax.sharding import PartitionSpec as P

HD = 128
PAGE = 16
NEG = -1e30
VMEM_LIMIT = 24 * 1024 * 1024
PROJECT_VMEM = 24 * 1024 * 1024


def attention_kernel(heads, span, info, slots, q_ref, k_ref, v_ref, start_ref, out_ref, cache_ref, acc, top):
    index = info[0]
    first = info[1]
    factor = HD**-0.5 * math.log2(math.e)
    columns = lax.broadcasted_iota(jnp.int32, (span, span), 1)
    rows = lax.broadcasted_iota(jnp.int32, (span, span), 0)

    def block(j, diagonal):
        at = pl.multiple_of(j * span, span)
        keys = k_ref[pl.ds(at, span), :]
        values = jnp.concatenate(
            [v_ref[pl.ds(at, span), :], jnp.ones((span, HD), jnp.bfloat16)], axis=1
        )
        allowed = columns >= start_ref[...] - at
        if diagonal:
            allowed = allowed & (columns <= rows)
        for g in range(heads):
            scores = lax.dot_general(
                q_ref[:, g * HD : (g + 1) * HD],
                keys,
                (((1,), (1,)), ((), ())),
                preferred_element_type=jnp.float32,
            )
            scores = jnp.where(allowed, scores, NEG)
            peak = jnp.max(scores, axis=1, keepdims=True)
            if not diagonal:
                before = top[g]
                peak = jnp.maximum(peak, before)
            weights = jnp.exp2(scores * factor - peak * factor).astype(jnp.bfloat16)
            mixed = jnp.dot(weights, values, preferred_element_type=jnp.float32)
            if not diagonal:
                mixed = mixed + acc[g] * jnp.exp2((before - peak) * factor)
            top[g] = peak
            acc[g] = mixed

    block(index, True)

    @pl.loop(first, index)
    def _(j):
        block(j, False)

    for g in range(heads):
        mixed = acc[g]
        out_ref[:, g * HD : (g + 1) * HD] = (mixed[:, :HD] / mixed[:, HD:]).astype(out_ref.dtype)

    pick_pages(slots, 0, cache_ref.shape[0], k_ref, v_ref, cache_ref)


def attention(info, slots, queries, keys, values, start, n_pre, capacity):
    span = queries.shape[0]
    heads = queries.shape[1] // HD
    return pl.pallas_call(
        functools.partial(attention_kernel, heads, span),
        in_specs=[
            pl.BlockSpec(memory_space=pltpu.SMEM),
            pl.BlockSpec(memory_space=pltpu.SMEM),
            pl.BlockSpec(memory_space=pltpu.VMEM),
            pl.BlockSpec(memory_space=pltpu.VMEM),
            pl.BlockSpec(memory_space=pltpu.VMEM),
            pl.BlockSpec(memory_space=pltpu.VMEM),
        ],
        out_specs=[
            pl.BlockSpec(memory_space=pltpu.VMEM),
            pl.BlockSpec(memory_space=pltpu.VMEM),
        ],
        out_shape=[
            jax.ShapeDtypeStruct(queries.shape, jnp.bfloat16),
            jax.ShapeDtypeStruct((n_pre, capacity * PAGE, 2 * HD), jnp.bfloat16),
        ],
        scratch_shapes=[
            pltpu.VMEM((heads, span, 2 * HD), jnp.float32),
            pltpu.VMEM((heads, span, 1), jnp.float32),
        ],
        compiler_params=pltpu.CompilerParams(vmem_limit_bytes=VMEM_LIMIT),
        cost_estimate=pl.CostEstimate(
            flops=4 * heads * span * span * n_pre * HD,
            bytes_accessed=4 * queries.size * 2,
            transcendentals=heads * span * span * n_pre,
        ),
        name="attention",
    )(info, slots, queries, keys, values, start)


PIECES = 8


def near_kernel(place, own_ref, near_ref, kw_ref, vw_ref, kx_ref, vx_ref, out_ref):
    def part(h_ref, key_ref, value_ref):
        weight = jnp.concatenate([key_ref[...], value_ref[...]], axis=1)
        return jnp.dot(h_ref[...], weight, preferred_element_type=jnp.float32)

    out_ref[...] = part(own_ref, kw_ref, vw_ref) + part(near_ref, kx_ref, vx_ref)


def add_pieces(member, chunk, pieces, w_ref, acc_ref):
    share = pieces[0].shape[1]
    half = PIECES // 2
    for side in range(2):

        @pl.when(jnp.bitwise_xor(member // half, side) == lax.rem(chunk, 2))
        def _():
            total = acc_ref[...]
            for j in range(side * half, side * half + half):
                row = lax.rem(jnp.bitwise_xor(member, j), half) * share
                total += jnp.dot(
                    pieces[j][...],
                    w_ref[pl.ds(pl.multiple_of(row, share), share), :],
                    preferred_element_type=jnp.float32,
                )
            acc_ref[...] = total


def facing_kernel(place, own_ref, *refs):
    pieces = refs[:PIECES]
    kw_ref, vw_ref, out_ref, w_ref = refs[PIECES:]
    span = own_ref.shape[0]
    w_ref[:, :HD] = kw_ref[...]
    w_ref[:, HD:] = vw_ref[...]
    out_ref[:span] = jnp.dot(own_ref[...], w_ref[...], preferred_element_type=jnp.float32)
    out_ref[span:] = jnp.zeros((span, 2 * HD), jnp.float32)
    add_pieces(place[2], place[0], pieces, w_ref, out_ref.at[pl.ds(span, span)])


def distant_kernel(place, own_ref, *refs):
    pieces = refs[:PIECES]
    w_ref, near_ref, outer_ref, facing_ref, bias_ref, out_ref, acc = refs[PIECES:]
    span = own_ref.shape[0]
    bias = bias_ref[...].astype(jnp.float32)
    own = jnp.dot(own_ref[...], w_ref[...], preferred_element_type=jnp.float32)
    own = own + near_ref[...] + facing_ref[:span] + bias
    acc[...] = outer_ref[...] + facing_ref[span:] + bias
    add_pieces(place[2], place[0], pieces, w_ref, acc)
    own_at = pl.multiple_of(place[1] * span, span)
    outer_at = pl.multiple_of((1 - place[1]) * span, span)
    out_ref[pl.ds(own_at, span), :] = own.astype(jnp.bfloat16)
    out_ref[pl.ds(outer_at, span), :] = acc[...].astype(jnp.bfloat16)


def call_project(kernel, name, place, operands, in_specs, depth, rows, columns, kind, scratch=()):
    return pl.pallas_call(
        kernel,
        grid_spec=pltpu.PrefetchScalarGridSpec(
            num_scalar_prefetch=1,
            grid=(1,),
            in_specs=in_specs,
            out_specs=pl.BlockSpec((rows, columns), lambda k, place: (0, 0)),
            scratch_shapes=list(scratch),
        ),
        out_shape=jax.ShapeDtypeStruct((rows, columns), kind),
        compiler_params=pltpu.CompilerParams(vmem_limit_bytes=PROJECT_VMEM),
        cost_estimate=pl.CostEstimate(flops=0, bytes_accessed=0, transcendentals=0),
        name=name,
    )(place, *operands)


def all_of(x, column=0, columns=None):
    shape = (x.shape[0], columns or x.shape[1])
    return pl.BlockSpec(shape, lambda k, place: (0, column))


def project_near(place, own, key_weight, value_weight, key_swapped, value_swapped):
    span, depth = own.shape[0], key_weight.shape[0]
    weights = [key_weight, value_weight, key_swapped, value_swapped]
    in_specs = [
        pl.BlockSpec((span, depth), lambda k, place: (0, place[0])),
        pl.BlockSpec((span, depth), lambda k, place: (0, place[1])),
    ] + [all_of(w) for w in weights]
    operands = [own, own] + weights
    return call_project(
        near_kernel, "near", place, operands, in_specs, 2 * depth, span, 2 * HD, jnp.float32
    )


def project_facing(place, own, pieces, key_weight, value_weight):
    span, depth = own.shape[0], key_weight.shape[0]
    others = list(pieces) + [key_weight, value_weight]
    in_specs = [pl.BlockSpec((span, depth), lambda k, place: (0, place[0]))]
    in_specs += [all_of(x) for x in others]
    return call_project(
        facing_kernel,
        "facing",
        place,
        [own] + others,
        in_specs,
        depth,
        2 * span,
        2 * HD,
        jnp.float32,
        [pltpu.VMEM((depth, 2 * HD), jnp.bfloat16)],
    )


def project_distant(place, column, own, pieces, weight, near, outer, facing, bias):
    span, depth = own.shape[0], weight.shape[0]
    others = list(pieces) + [weight]
    parts = [near, outer, facing]
    in_specs = [pl.BlockSpec((span, depth), lambda k, place: (0, place[0]))]
    in_specs += [all_of(x) for x in others] + [all_of(x, column, HD) for x in parts]
    in_specs.append(all_of(bias))
    return call_project(
        distant_kernel,
        "distant",
        place,
        [own] + others + parts + [bias],
        in_specs,
        depth,
        2 * span,
        HD,
        jnp.bfloat16,
        [pltpu.VMEM((span, HD), jnp.float32)],
    )


INWARD = [(0, 1), (3, 2)]
ACROSS = [(1, 2), (2, 1)]
OUTWARD = [(1, 0), (2, 3)]
SWAP = [(0, 1), (1, 0), (2, 3), (3, 2)]


def spread_owners(page_owner):
    index = lax.axis_index("pre")
    mine = page_owner.T
    mate = lax.ppermute(mine, "pre", SWAP)
    even = lax.rem(index, 2) == 0
    pair = jnp.concatenate([jnp.where(even, mine, mate), jnp.where(even, mate, mine)], axis=0)
    across = lax.ppermute(pair, "pre", ACROSS)
    far = lax.ppermute(across, "pre", OUTWARD)
    other = jnp.where((index == 1) | (index == 2), across, far)
    return jnp.concatenate(
        [jnp.where(index < 2, pair, other), jnp.where(index < 2, other, pair)], axis=0
    )


def line_of_four(hidden, key_weight, value_weight, key_bias, value_bias):
    index = lax.axis_index("pre")
    member = lax.axis_index(("dec", "tp"))
    width = hidden.shape[1]
    share = width // 2 // PIECES
    facing = 3 - index
    near = jnp.bitwise_xor(index, 1)
    distant = jnp.bitwise_xor(facing, 1)
    second = (index < 2).astype(jnp.int32)

    def send(x, pairs):
        return lax.ppermute(x, "pre", pairs)

    def trade(x, apart):
        return lax.ppermute(x, ("dec", "tp"), [(m, m ^ apart) for m in range(PIECES)])

    mine = second * (width // 2) + member * share
    cut = send(lax.dynamic_slice_in_dim(hidden, mine, share, axis=1), INWARD)
    key_facing = send(key_weight, ACROSS)
    cut, key_facing, key_weight, value_weight = lax.optimization_barrier(
        (cut, key_facing, key_weight, value_weight)
    )
    chips = [cut, trade(cut, 2), trade(cut, 4), trade(cut, 6)]
    value_facing = send(value_weight, ACROSS)
    key_swapped = send(key_weight, SWAP)
    value_swapped = send(value_weight, SWAP)
    key_distant = send(key_swapped, ACROSS)
    value_distant = send(value_swapped, ACROSS)
    mates = [trade(x, 1) for x in chips]
    pieces = [x for both in zip(chips, mates) for x in both]

    def place(chunk):
        return jnp.stack([chunk, second, member])

    own_part = project_near(
        jnp.stack([index, near]), hidden, key_weight, value_weight, key_swapped, value_swapped
    )
    outer_part = send(own_part, INWARD)
    faced = project_facing(place(facing), hidden, pieces, key_facing, value_facing)

    def finish(column, weight, bias):
        pair = project_distant(
            place(distant), column, hidden, pieces, weight, own_part, outer_part, faced, bias[None, :]
        )
        out = send(pair, OUTWARD)
        across = send(pair, ACROSS)
        return pair, out, across, send(across, OUTWARD)

    keys = finish(0, key_distant, key_bias)
    values = finish(1, value_distant, value_bias)
    return keys, values


def softmax_step(q, keys, values, allowed, before):
    factor = HD**-0.5 * math.log2(math.e)
    scores = lax.dot_general(q, keys, (((1,), (1,)), ((), ())), preferred_element_type=jnp.float32)
    scores = jnp.where(allowed, scores, NEG)
    peak = jnp.max(scores, axis=1, keepdims=True)
    if before is not None:
        peak = jnp.maximum(peak, before[0])
    weights = jnp.exp2(scores * factor - peak * factor).astype(jnp.bfloat16)
    mixed = jnp.dot(weights, values, preferred_element_type=jnp.float32)
    total, mixed = mixed[:, HD:], mixed[:, :HD]
    if before is not None:
        shrink = jnp.exp2((before[0] - peak) * factor)
        total = total + before[1] * shrink
        mixed = mixed + before[2] * shrink
    return peak, total, mixed


def with_ones(values):
    return jnp.concatenate([values, jnp.ones_like(values)], axis=1)


def own_kernel(
    heads, info, slots, q_ref, start_ref, k_in, k_out, v_in, v_out, top, total, mix, cache_ref, held_k, held_v
):
    span = q_ref.shape[0]
    index = info[0]
    inner = (index == 1) | (index == 2)
    held_k[...] = jnp.where(inner, k_in[...], k_out[...])
    held_v[...] = jnp.where(inner, v_in[...], v_out[...])
    pick_pages(slots, 0, 2, held_k, held_v, cache_ref)
    values = with_ones(held_v[...])
    columns = lax.broadcasted_iota(jnp.int32, (span, 2 * span), 1)
    rows = lax.broadcasted_iota(jnp.int32, (span, 2 * span), 0)
    allowed = (columns <= rows + lax.rem(index, 2) * span) & (
        columns >= start_ref[...] - (index // 2) * 2 * span
    )
    for g in range(heads):
        q = q_ref[:, g * HD : (g + 1) * HD]
        peak, sums, mixed = softmax_step(q, held_k[...], values, allowed, None)
        top[g] = peak
        total[g] = sums[:, :1]
        mix[g] = mixed


def far_kernel(
    heads,
    info,
    slots,
    q_ref,
    start_ref,
    k_across,
    k_far,
    v_across,
    v_far,
    top,
    total,
    mix,
    own_cache,
    out_ref,
    cache_ref,
    held_k,
    held_v,
):
    span = q_ref.shape[0]
    index = info[0]
    inner = (index == 1) | (index == 2)
    held_k[...] = jnp.where(inner, k_across[...], k_far[...])
    held_v[...] = jnp.where(inner, v_across[...], v_far[...])

    @pl.when((index < 2) | (info[1] >= 2))
    def _():
        for g in range(heads):
            out_ref[:, g * HD : (g + 1) * HD] = (mix[g] / total[g]).astype(out_ref.dtype)

    @pl.when((index >= 2) & (info[1] < 2))
    def _():
        keys = held_k[...]
        values = with_ones(held_v[...])
        columns = lax.broadcasted_iota(jnp.int32, (span, 2 * span), 1)
        allowed = columns >= start_ref[...]
        for g in range(heads):
            q = q_ref[:, g * HD : (g + 1) * HD]
            _, sums, mixed = softmax_step(q, keys, values, allowed, (top[g], total[g], mix[g]))
            out_ref[:, g * HD : (g + 1) * HD] = (mixed / sums).astype(out_ref.dtype)

    cache_ref[pl.ds(index // 2 * 2, 2)] = own_cache[...]
    pick_pages(slots, 2, 2, held_k, held_v, cache_ref.at[pl.ds((1 - index // 2) * 2, 2)])


def pick_pages(slots, first, sources, k_ref, v_ref, cache_ref):
    capacity = cache_ref.shape[1] // PAGE
    empty = jnp.zeros((PAGE, HD), cache_ref.dtype)
    for s in range(sources):
        for r in range(capacity):
            page = slots[(first + s) * capacity + r]
            token = pl.ds(pl.multiple_of(jnp.maximum(page, 0) * PAGE, PAGE), PAGE)
            row = pl.ds(r * PAGE, PAGE)
            cache_ref[s, row, :HD] = jnp.where(page >= 0, k_ref[token, :], empty)
            cache_ref[s, row, HD:] = jnp.where(page >= 0, v_ref[token, :], empty)


def attention_of_pairs(info, slots, queries, start, keys, values, capacity):
    span = queries.shape[0]
    heads = queries.shape[1] // HD
    smem = pl.BlockSpec(memory_space=pltpu.SMEM)
    vmem = pl.BlockSpec(memory_space=pltpu.VMEM)
    cost = pl.CostEstimate(
        flops=8 * heads * span * span * HD,
        bytes_accessed=4 * queries.size * 2,
        transcendentals=2 * heads * span * span,
    )
    params = pltpu.CompilerParams(vmem_limit_bytes=VMEM_LIMIT)
    held = [pltpu.VMEM((2 * span, HD), jnp.bfloat16)] * 2
    state = pl.pallas_call(
        functools.partial(own_kernel, heads),
        in_specs=[smem] * 2 + [vmem] * 6,
        out_specs=[vmem] * 4,
        out_shape=[
            jax.ShapeDtypeStruct((heads, span, 1), jnp.float32),
            jax.ShapeDtypeStruct((heads, span, 1), jnp.float32),
            jax.ShapeDtypeStruct((heads, span, HD), jnp.float32),
            jax.ShapeDtypeStruct((2, capacity * PAGE, 2 * HD), jnp.bfloat16),
        ],
        scratch_shapes=held,
        compiler_params=params,
        cost_estimate=cost,
        name="attend_own",
    )(info, slots, queries, start, *keys[:2], *values[:2])
    return pl.pallas_call(
        functools.partial(far_kernel, heads),
        in_specs=[smem] * 2 + [vmem] * 10,
        out_specs=[vmem] * 2,
        out_shape=[
            jax.ShapeDtypeStruct(queries.shape, jnp.bfloat16),
            jax.ShapeDtypeStruct((4, capacity * PAGE, 2 * HD), jnp.bfloat16),
        ],
        scratch_shapes=held,
        compiler_params=params,
        cost_estimate=cost,
        name="attend_far",
    )(info, slots, queries, start, *keys[2:], *values[2:], *state)


def gathered(hidden, key_weight, value_weight, key_bias, value_bias):
    joined = jnp.concatenate([key_weight, value_weight], axis=1)
    joined = lax.all_gather(joined, "pre", axis=0, tiled=True)
    bias = jnp.concatenate([key_bias, value_bias]).astype(jnp.float32)
    local = jnp.dot(hidden, joined, preferred_element_type=jnp.float32) + bias
    both = lax.all_gather(local.astype(jnp.bfloat16), "pre", axis=0, tiled=True)
    return both[:, :HD], both[:, HD:]


def body(hidden, queries, key_weight, value_weight, key_bias, value_bias, segment_ids, page_owner):
    n_pre = lax.axis_size("pre")
    index = lax.axis_index("pre")
    span = hidden.shape[0]
    pages_dev = span // PAGE
    capacity = 2 * pages_dev // n_pre
    assert key_weight.shape[1] == HD

    own_segments = lax.dynamic_slice_in_dim(segment_ids, index * span, span)
    start = jnp.sum(
        (segment_ids[None, :] < own_segments[:, None]).astype(jnp.int32), axis=1, keepdims=True
    )
    info = jnp.stack([index, start[0, 0] // span]).astype(jnp.int32)
    arrays = (hidden, key_weight, value_weight, key_bias, value_bias)
    if n_pre == 4:
        owners = spread_owners(page_owner)
        keys, values = line_of_four(*arrays)
    else:
        owners = lax.all_gather(page_owner[:, 0], "pre")
        keys, values = gathered(*arrays)

    mine = (owners == index).astype(jnp.int32)
    rank = jnp.cumsum(mine, axis=1) - mine
    numbers = jnp.arange(n_pre * pages_dev, dtype=jnp.int32).reshape(n_pre, 1, pages_dev)
    wanted = (mine[:, None, :] == 1) & (
        rank[:, None, :] == jnp.arange(capacity, dtype=jnp.int32)[None, :, None]
    )
    slots = jnp.max(jnp.where(wanted, numbers, -1), axis=2)
    if n_pre == 4:
        low, high = slots[:2], jnp.where(slots[2:] < 0, -1, slots[2:] - 2 * pages_dev)
        slots = jnp.where(index < 2, jnp.stack([low, high]), jnp.stack([high, low]))
        mixed, cache = attention_of_pairs(
            info, slots.reshape(-1), queries, start, keys, values, capacity
        )
    else:
        slots = slots.reshape(-1)
        mixed, cache = attention(info, slots, queries, keys, values, start, n_pre, capacity)
    return (mixed, cache[None])


def solution(mesh):
    return jax.shard_map(
        body,
        mesh=mesh,
        in_specs=(
            P(("group", "pre"), None),
            P(("group", "pre"), ("dec", "tp")),
            P("pre", ("dec", "tp")),
            P("pre", ("dec", "tp")),
            P(("dec", "tp")),
            P(("dec", "tp")),
            P("group"),
            P(("group", "pre"), None),
        ),
        out_specs=(
            P(("group", "pre"), ("dec", "tp")),
            P(("group", "pre"), None, None, ("dec", "tp")),
        ),
        check_vma=False,
    )
```

```python
import functools
import math

import jax
import jax.numpy as jnp
from jax import lax
from jax.experimental import pallas as pl
from jax.experimental.pallas import tpu as pltpu
from jax.sharding import PartitionSpec as P

HD = 128
PAGE = 16
NEG = -1e30
VMEM_LIMIT = 48 * 1024 * 1024
PROJECT_VMEM = 48 * 1024 * 1024


def attention_kernel(heads, span, info, slots, q_ref, k_ref, v_ref, start_ref, out_ref, cache_ref, acc, top):
    index = info[0]
    first = info[1]
    factor = HD**-0.5 * math.log2(math.e)
    columns = lax.broadcasted_iota(jnp.int32, (span, span), 1)
    rows = lax.broadcasted_iota(jnp.int32, (span, span), 0)

    def block(j, diagonal):
        at = pl.multiple_of(j * span, span)
        keys = k_ref[pl.ds(at, span), :]
        values = jnp.concatenate(
            [v_ref[pl.ds(at, span), :], jnp.ones((span, HD), jnp.bfloat16)], axis=1
        )
        allowed = columns >= start_ref[...] - at
        if diagonal:
            allowed = allowed & (columns <= rows)
        for g in range(heads):
            scores = lax.dot_general(
                q_ref[:, g * HD : (g + 1) * HD],
                keys,
                (((1,), (1,)), ((), ())),
                preferred_element_type=jnp.float32,
            )
            scores = jnp.where(allowed, scores, NEG)
            peak = jnp.max(scores, axis=1, keepdims=True)
            if not diagonal:
                before = top[g]
                peak = jnp.maximum(peak, before)
            weights = jnp.exp2(scores * factor - peak * factor).astype(jnp.bfloat16)
            mixed = jnp.dot(weights, values, preferred_element_type=jnp.float32)
            if not diagonal:
                mixed = mixed + acc[g] * jnp.exp2((before - peak) * factor)
            top[g] = peak
            acc[g] = mixed

    block(index, True)

    @pl.loop(first, index)
    def _(j):
        block(j, False)

    for g in range(heads):
        mixed = acc[g]
        out_ref[:, g * HD : (g + 1) * HD] = (mixed[:, :HD] / mixed[:, HD:]).astype(out_ref.dtype)

    pick_pages(slots, 0, cache_ref.shape[0], k_ref, v_ref, cache_ref)


def attention(info, slots, queries, keys, values, start, n_pre, capacity):
    span = queries.shape[0]
    heads = queries.shape[1] // HD
    return pl.pallas_call(
        functools.partial(attention_kernel, heads, span),
        in_specs=[
            pl.BlockSpec(memory_space=pltpu.SMEM),
            pl.BlockSpec(memory_space=pltpu.SMEM),
            pl.BlockSpec(memory_space=pltpu.VMEM),
            pl.BlockSpec(memory_space=pltpu.VMEM),
            pl.BlockSpec(memory_space=pltpu.VMEM),
            pl.BlockSpec(memory_space=pltpu.VMEM),
        ],
        out_specs=[
            pl.BlockSpec(memory_space=pltpu.VMEM),
            pl.BlockSpec(memory_space=pltpu.VMEM),
        ],
        out_shape=[
            jax.ShapeDtypeStruct(queries.shape, jnp.bfloat16),
            jax.ShapeDtypeStruct((n_pre, capacity * PAGE, 2 * HD), jnp.bfloat16),
        ],
        scratch_shapes=[
            pltpu.VMEM((heads, span, 2 * HD), jnp.float32),
            pltpu.VMEM((heads, span, 1), jnp.float32),
        ],
        compiler_params=pltpu.CompilerParams(vmem_limit_bytes=VMEM_LIMIT),
        cost_estimate=pl.CostEstimate(
            flops=4 * heads * span * span * n_pre * HD,
            bytes_accessed=4 * queries.size * 2,
            transcendentals=heads * span * span * n_pre,
        ),
        name="attention",
    )(info, slots, queries, keys, values, start)


PIECES = 8


def chunk_of(h_ref, chunk, depth):
    return h_ref.at[:, pl.ds(pl.multiple_of(chunk * depth, depth), depth)]


def add_pieces(member, chunk, pieces, w_ref, acc_ref, held, sems):
    share = pieces[0].shape[1]
    half = PIECES // 2
    for side in range(2):

        @pl.when(jnp.bitwise_xor(member // half, side) == lax.rem(chunk, 2))
        def _():
            copies = [
                pltpu.make_async_copy(pieces[side * half + t], held.at[t], sems.at[t])
                for t in range(half)
            ]
            for copy in copies:
                copy.start()
            for t in range(half):
                row = lax.rem(jnp.bitwise_xor(member, side * half + t), half) * share
                weight = w_ref[pl.ds(pl.multiple_of(row, share), share), :]
                copies[t].wait()
                acc_ref[...] += jnp.dot(held[t], weight, preferred_element_type=jnp.float32)


def near_kernel(chained, place, h_ref, k_ref, v_ref, *refs):
    before = refs[0] if chained else None
    out_ref, h_buf, w_buf, sems = refs[1:] if chained else refs
    copies = [
        pltpu.make_async_copy(k_ref, w_buf.at[:, pl.ds(0, HD)], sems.at[0]),
        pltpu.make_async_copy(v_ref, w_buf.at[:, pl.ds(HD, HD)], sems.at[1]),
        pltpu.make_async_copy(chunk_of(h_ref, place[0], h_buf.shape[1]), h_buf, sems.at[2]),
    ]
    for copy in copies:
        copy.start()
    for copy in copies:
        copy.wait()
    part = jnp.dot(h_buf[...], w_buf[...], preferred_element_type=jnp.float32)
    out_ref[...] = part + before[...] if chained else part


def facing_kernel(place, h_ref, k_ref, v_ref, *refs):
    pieces = refs[:PIECES]
    out_ref, h_buf, w_buf, held, sems = refs[PIECES:]
    span = h_buf.shape[0]
    copies = [
        pltpu.make_async_copy(k_ref, w_buf.at[:, pl.ds(0, HD)], sems.at[4]),
        pltpu.make_async_copy(v_ref, w_buf.at[:, pl.ds(HD, HD)], sems.at[5]),
        pltpu.make_async_copy(chunk_of(h_ref, place[0], h_buf.shape[1]), h_buf, sems.at[6]),
    ]
    for copy in copies:
        copy.start()
    for copy in copies:
        copy.wait()
    out_ref[:span] = jnp.dot(h_buf[...], w_buf[...], preferred_element_type=jnp.float32)
    out_ref[span:] = jnp.zeros((span, 2 * HD), jnp.float32)
    add_pieces(place[2], place[0], pieces, w_buf, out_ref.at[pl.ds(span, span)], held, sems)


def distant_kernel(place, h_ref, w_ref, near_ref, outer_ref, facing_ref, bias_ref, *refs):
    pieces = refs[:PIECES]
    out_ref, h_buf, w_buf, held, acc, sems = refs[PIECES:]
    span = h_buf.shape[0]
    copies = [
        pltpu.make_async_copy(w_ref, w_buf, sems.at[4]),
        pltpu.make_async_copy(chunk_of(h_ref, place[0], h_buf.shape[1]), h_buf, sems.at[5]),
    ]
    for copy in copies:
        copy.start()
    bias = bias_ref[...].astype(jnp.float32)
    acc[...] = outer_ref[...] + facing_ref[span:] + bias
    own = near_ref[...] + facing_ref[:span] + bias
    for copy in copies:
        copy.wait()
    own += jnp.dot(h_buf[...], w_buf[...], preferred_element_type=jnp.float32)
    own_at = pl.multiple_of(place[1] * span, span)
    outer_at = pl.multiple_of((1 - place[1]) * span, span)
    out_ref[pl.ds(own_at, span), :] = own.astype(jnp.bfloat16)
    add_pieces(place[2], place[0], pieces, w_buf, acc, held, sems)
    out_ref[pl.ds(outer_at, span), :] = acc[...].astype(jnp.bfloat16)


ANY = pl.BlockSpec(memory_space=pl.ANY)


def call_project(kernel, name, place, operands, in_specs, rows, columns, kind, scratch):
    return pl.pallas_call(
        kernel,
        grid_spec=pltpu.PrefetchScalarGridSpec(
            num_scalar_prefetch=1,
            grid=(1,),
            in_specs=in_specs,
            out_specs=pl.BlockSpec((rows, columns), lambda k, place: (0, 0)),
            scratch_shapes=list(scratch),
        ),
        out_shape=jax.ShapeDtypeStruct((rows, columns), kind),
        compiler_params=pltpu.CompilerParams(vmem_limit_bytes=PROJECT_VMEM),
        cost_estimate=pl.CostEstimate(flops=0, bytes_accessed=0, transcendentals=0),
        name=name,
    )(place, *operands)


def all_of(x, column=0, columns=None):
    shape = (x.shape[0], columns or x.shape[1])
    return pl.BlockSpec(shape, lambda k, place: (0, column))


def project_near(place, own, key_weight, value_weight, before=None):
    span, depth = own.shape[0], key_weight.shape[0]
    chained = before is not None
    return call_project(
        functools.partial(near_kernel, chained),
        "near",
        place,
        [own, key_weight, value_weight] + [before] * chained,
        [ANY] * 3 + ([all_of(before)] if chained else []),
        span,
        2 * HD,
        jnp.float32,
        [
            pltpu.VMEM((span, depth), jnp.bfloat16),
            pltpu.VMEM((depth, 2 * HD), jnp.bfloat16),
            pltpu.SemaphoreType.DMA((3,)),
        ],
    )


def project_facing(place, own, pieces, key_weight, value_weight):
    span, depth = own.shape[0], key_weight.shape[0]
    return call_project(
        facing_kernel,
        "facing",
        place,
        [own, key_weight, value_weight] + pieces,
        [ANY] * (3 + PIECES),
        2 * span,
        2 * HD,
        jnp.float32,
        [
            pltpu.VMEM((span, depth), jnp.bfloat16),
            pltpu.VMEM((depth, 2 * HD), jnp.bfloat16),
            pltpu.VMEM((PIECES // 2,) + pieces[0].shape, jnp.bfloat16),
            pltpu.SemaphoreType.DMA((7,)),
        ],
    )


def project_distant(place, column, own, pieces, weight, near, outer, facing, bias):
    span, depth = own.shape[0], weight.shape[0]
    parts = [near, outer, facing]
    return call_project(
        distant_kernel,
        "distant",
        place,
        [own, weight] + parts + [bias] + pieces,
        [ANY] * 2 + [all_of(x, column, HD) for x in parts] + [all_of(bias)] + [ANY] * PIECES,
        2 * span,
        HD,
        jnp.bfloat16,
        [
            pltpu.VMEM((span, depth), jnp.bfloat16),
            pltpu.VMEM((depth, HD), jnp.bfloat16),
            pltpu.VMEM((PIECES // 2,) + pieces[0].shape, jnp.bfloat16),
            pltpu.VMEM((span, HD), jnp.float32),
            pltpu.SemaphoreType.DMA((6,)),
        ],
    )


INWARD = [(0, 1), (3, 2)]
ACROSS = [(1, 2), (2, 1)]
OUTWARD = [(1, 0), (2, 3)]
SWAP = [(0, 1), (1, 0), (2, 3), (3, 2)]


def spread_owners(page_owner):
    index = lax.axis_index("pre")
    mine = page_owner.T
    mate = lax.ppermute(mine, "pre", SWAP)
    even = lax.rem(index, 2) == 0
    pair = jnp.concatenate([jnp.where(even, mine, mate), jnp.where(even, mate, mine)], axis=0)
    other = lax.ppermute(pair, "pre", [(p, p ^ 2) for p in range(4)])
    return jnp.concatenate(
        [jnp.where(index < 2, pair, other), jnp.where(index < 2, other, pair)], axis=0
    )


def line_of_four(hidden, key_weight, value_weight, key_bias, value_bias, page_owner):
    index = lax.axis_index("pre")
    member = lax.axis_index(("dec", "tp"))
    width = hidden.shape[1]
    share = width // 2 // PIECES
    facing = 3 - index
    near = jnp.bitwise_xor(index, 1)
    distant = jnp.bitwise_xor(facing, 1)
    second = (index < 2).astype(jnp.int32)

    def send(x, pairs):
        return lax.ppermute(x, "pre", pairs)

    def trade(x, apart):
        return lax.ppermute(x, ("dec", "tp"), [(m, m ^ apart) for m in range(PIECES)])

    mine = second * (width // 2) + member * share
    cut = send(lax.dynamic_slice_in_dim(hidden, mine, share, axis=1), INWARD)
    key_facing = send(key_weight, ACROSS)
    cut, page_owner = lax.optimization_barrier((cut, page_owner))
    owners = spread_owners(page_owner)
    chips = [cut, trade(cut, 2), trade(cut, 4), trade(cut, 6)]
    value_facing = send(value_weight, ACROSS)
    key_swapped = send(key_weight, SWAP)
    value_swapped = send(value_weight, SWAP)
    key_distant = send(key_swapped, ACROSS)
    value_distant = send(value_swapped, ACROSS)
    mates = [trade(x, 1) for x in chips]
    pieces = [x for both in zip(chips, mates) for x in both]

    def place(chunk):
        return jnp.stack([chunk, second, member])

    own_part = project_near(index[None], hidden, key_weight, value_weight)
    own_part = project_near(near[None], hidden, key_swapped, value_swapped, own_part)
    outer_part = send(own_part, INWARD)
    faced = project_facing(place(facing), hidden, pieces, key_facing, value_facing)

    def finish(column, weight, bias):
        pair = project_distant(
            place(distant), column, hidden, pieces, weight, own_part, outer_part, faced, bias[None, :]
        )
        out = send(pair, OUTWARD)
        across = send(pair, ACROSS)
        return pair, out, across, send(across, OUTWARD)

    keys = finish(0, key_distant, key_bias)
    values = finish(1, value_distant, value_bias)
    return keys, values, owners


def softmax_step(q, keys, values, allowed, before):
    factor = HD**-0.5 * math.log2(math.e)
    scores = lax.dot_general(q, keys, (((1,), (1,)), ((), ())), preferred_element_type=jnp.float32)
    scores = jnp.where(allowed, scores, NEG)
    peak = jnp.max(scores, axis=1, keepdims=True)
    if before is not None:
        peak = jnp.maximum(peak, before[0])
    weights = jnp.exp2(scores * factor - peak * factor).astype(jnp.bfloat16)
    mixed = jnp.dot(weights, values, preferred_element_type=jnp.float32)
    total, mixed = mixed[:, HD:], mixed[:, :HD]
    if before is not None:
        shrink = jnp.exp2((before[0] - peak) * factor)
        total = total + before[1] * shrink
        mixed = mixed + before[2] * shrink
    return peak, total, mixed


def with_ones(values):
    return jnp.concatenate([values, jnp.ones_like(values)], axis=1)


def own_kernel(
    heads, info, slots, q_ref, start_ref, k_in, k_out, v_in, v_out, top, total, mix, cache_ref, held_k, held_v
):
    span = q_ref.shape[0]
    index = info[0]
    inner = (index == 1) | (index == 2)
    held_k[...] = jnp.where(inner, k_in[...], k_out[...])
    held_v[...] = jnp.where(inner, v_in[...], v_out[...])
    pick_pages(slots, 0, 2, held_k, held_v, cache_ref)
    values = with_ones(held_v[...])
    columns = lax.broadcasted_iota(jnp.int32, (span, 2 * span), 1)
    rows = lax.broadcasted_iota(jnp.int32, (span, 2 * span), 0)
    allowed = (columns <= rows + lax.rem(index, 2) * span) & (
        columns >= start_ref[...] - (index // 2) * 2 * span
    )
    for g in range(heads):
        q = q_ref[:, g * HD : (g + 1) * HD]
        peak, sums, mixed = softmax_step(q, held_k[...], values, allowed, None)
        top[g] = peak
        total[g] = sums[:, :1]
        mix[g] = mixed


def far_kernel(
    heads,
    info,
    slots,
    q_ref,
    start_ref,
    k_across,
    k_far,
    v_across,
    v_far,
    top,
    total,
    mix,
    own_cache,
    out_ref,
    cache_ref,
    held_k,
    held_v,
):
    span = q_ref.shape[0]
    index = info[0]
    inner = (index == 1) | (index == 2)
    held_k[...] = jnp.where(inner, k_across[...], k_far[...])
    held_v[...] = jnp.where(inner, v_across[...], v_far[...])

    @pl.when((index < 2) | (info[1] >= 2))
    def _():
        for g in range(heads):
            out_ref[:, g * HD : (g + 1) * HD] = (mix[g] / total[g]).astype(out_ref.dtype)

    @pl.when((index >= 2) & (info[1] < 2))
    def _():
        keys = held_k[...]
        values = with_ones(held_v[...])
        columns = lax.broadcasted_iota(jnp.int32, (span, 2 * span), 1)
        allowed = columns >= start_ref[...]
        for g in range(heads):
            q = q_ref[:, g * HD : (g + 1) * HD]
            _, sums, mixed = softmax_step(q, keys, values, allowed, (top[g], total[g], mix[g]))
            out_ref[:, g * HD : (g + 1) * HD] = (mixed / sums).astype(out_ref.dtype)

    cache_ref[pl.ds(index // 2 * 2, 2)] = own_cache[...]
    pick_pages(slots, 2, 2, held_k, held_v, cache_ref.at[pl.ds((1 - index // 2) * 2, 2)])


def pick_pages(slots, first, sources, k_ref, v_ref, cache_ref):
    capacity = cache_ref.shape[1] // PAGE
    empty = jnp.zeros((PAGE, HD), cache_ref.dtype)
    for s in range(sources):
        for r in range(capacity):
            page = slots[(first + s) * capacity + r]
            token = pl.ds(pl.multiple_of(jnp.maximum(page, 0) * PAGE, PAGE), PAGE)
            row = pl.ds(r * PAGE, PAGE)
            cache_ref[s, row, :HD] = jnp.where(page >= 0, k_ref[token, :], empty)
            cache_ref[s, row, HD:] = jnp.where(page >= 0, v_ref[token, :], empty)


def attention_of_pairs(info, slots, queries, start, keys, values, capacity):
    span = queries.shape[0]
    heads = queries.shape[1] // HD
    smem = pl.BlockSpec(memory_space=pltpu.SMEM)
    vmem = pl.BlockSpec(memory_space=pltpu.VMEM)
    cost = pl.CostEstimate(
        flops=8 * heads * span * span * HD,
        bytes_accessed=4 * queries.size * 2,
        transcendentals=2 * heads * span * span,
    )
    params = pltpu.CompilerParams(vmem_limit_bytes=VMEM_LIMIT)
    held = [pltpu.VMEM((2 * span, HD), jnp.bfloat16)] * 2
    state = pl.pallas_call(
        functools.partial(own_kernel, heads),
        in_specs=[smem] * 2 + [vmem] * 6,
        out_specs=[vmem] * 4,
        out_shape=[
            jax.ShapeDtypeStruct((heads, span, 1), jnp.float32),
            jax.ShapeDtypeStruct((heads, span, 1), jnp.float32),
            jax.ShapeDtypeStruct((heads, span, HD), jnp.float32),
            jax.ShapeDtypeStruct((2, capacity * PAGE, 2 * HD), jnp.bfloat16),
        ],
        scratch_shapes=held,
        compiler_params=params,
        cost_estimate=cost,
        name="attend_own",
    )(info, slots, queries, start, *keys[:2], *values[:2])
    return pl.pallas_call(
        functools.partial(far_kernel, heads),
        in_specs=[smem] * 2 + [vmem] * 10,
        out_specs=[vmem] * 2,
        out_shape=[
            jax.ShapeDtypeStruct(queries.shape, jnp.bfloat16),
            jax.ShapeDtypeStruct((4, capacity * PAGE, 2 * HD), jnp.bfloat16),
        ],
        scratch_shapes=held,
        compiler_params=params,
        cost_estimate=cost,
        name="attend_far",
    )(info, slots, queries, start, *keys[2:], *values[2:], *state)


def gathered(hidden, key_weight, value_weight, key_bias, value_bias):
    joined = jnp.concatenate([key_weight, value_weight], axis=1)
    joined = lax.all_gather(joined, "pre", axis=0, tiled=True)
    bias = jnp.concatenate([key_bias, value_bias]).astype(jnp.float32)
    local = jnp.dot(hidden, joined, preferred_element_type=jnp.float32) + bias
    both = lax.all_gather(local.astype(jnp.bfloat16), "pre", axis=0, tiled=True)
    return both[:, :HD], both[:, HD:]


def body(hidden, queries, key_weight, value_weight, key_bias, value_bias, segment_ids, page_owner):
    n_pre = lax.axis_size("pre")
    index = lax.axis_index("pre")
    span = hidden.shape[0]
    pages_dev = span // PAGE
    capacity = 2 * pages_dev // n_pre
    assert key_weight.shape[1] == HD

    own_segments = lax.dynamic_slice_in_dim(segment_ids, index * span, span)
    start = jnp.sum(
        (segment_ids[None, :] < own_segments[:, None]).astype(jnp.int32), axis=1, keepdims=True
    )
    info = jnp.stack([index, start[0, 0] // span]).astype(jnp.int32)
    arrays = (hidden, key_weight, value_weight, key_bias, value_bias)
    if n_pre == 4:
        keys, values, owners = line_of_four(*arrays, page_owner)
    else:
        owners = lax.all_gather(page_owner[:, 0], "pre")
        keys, values = gathered(*arrays)

    mine = (owners == index).astype(jnp.int32)
    rank = jnp.cumsum(mine, axis=1) - mine
    numbers = jnp.arange(n_pre * pages_dev, dtype=jnp.int32).reshape(n_pre, 1, pages_dev)
    wanted = (mine[:, None, :] == 1) & (
        rank[:, None, :] == jnp.arange(capacity, dtype=jnp.int32)[None, :, None]
    )
    slots = jnp.max(jnp.where(wanted, numbers, -1), axis=2)
    if n_pre == 4:
        low, high = slots[:2], jnp.where(slots[2:] < 0, -1, slots[2:] - 2 * pages_dev)
        slots = jnp.where(index < 2, jnp.stack([low, high]), jnp.stack([high, low]))
        mixed, cache = attention_of_pairs(
            info, slots.reshape(-1), queries, start, keys, values, capacity
        )
    else:
        slots = slots.reshape(-1)
        mixed, cache = attention(info, slots, queries, keys, values, start, n_pre, capacity)
    return (mixed, cache[None])


def solution(mesh):
    return jax.shard_map(
        body,
        mesh=mesh,
        in_specs=(
            P(("group", "pre"), None),
            P(("group", "pre"), ("dec", "tp")),
            P("pre", ("dec", "tp")),
            P("pre", ("dec", "tp")),
            P(("dec", "tp")),
            P(("dec", "tp")),
            P("group"),
            P(("group", "pre"), None),
        ),
        out_specs=(
            P(("group", "pre"), ("dec", "tp")),
            P(("group", "pre"), None, None, ("dec", "tp")),
        ),
        check_vma=False,
    )
```

```python
import functools
import math

import jax
import jax.numpy as jnp
from jax import lax
from jax.experimental import pallas as pl
from jax.experimental.pallas import tpu as pltpu
from jax.sharding import PartitionSpec as P

HD = 128
PAGE = 16
NEG = -1e30
KERNEL_VMEM = 48 * 1024 * 1024
PROMPTS = 4


def attention_kernel(heads, span, info, slots, q_ref, k_ref, v_ref, start_ref, out_ref, cache_ref, acc, top):
    index = info[0]
    first = info[1]
    factor = HD**-0.5 * math.log2(math.e)
    columns = lax.broadcasted_iota(jnp.int32, (span, span), 1)
    rows = lax.broadcasted_iota(jnp.int32, (span, span), 0)

    def block(j, diagonal):
        at = pl.multiple_of(j * span, span)
        keys = k_ref[pl.ds(at, span), :]
        values = jnp.concatenate(
            [v_ref[pl.ds(at, span), :], jnp.ones((span, HD), jnp.bfloat16)], axis=1
        )
        allowed = columns >= start_ref[...] - at
        if diagonal:
            allowed = allowed & (columns <= rows)
        for g in range(heads):
            scores = lax.dot_general(
                q_ref[:, g * HD : (g + 1) * HD],
                keys,
                (((1,), (1,)), ((), ())),
                preferred_element_type=jnp.float32,
            )
            scores = jnp.where(allowed, scores, NEG)
            peak = jnp.max(scores, axis=1, keepdims=True)
            if not diagonal:
                before = top[g]
                peak = jnp.maximum(peak, before)
            weights = jnp.exp2(scores * factor - peak * factor).astype(jnp.bfloat16)
            mixed = jnp.dot(weights, values, preferred_element_type=jnp.float32)
            if not diagonal:
                mixed = mixed + acc[g] * jnp.exp2((before - peak) * factor)
            top[g] = peak
            acc[g] = mixed

    block(index, True)

    @pl.loop(first, index)
    def _(j):
        block(j, False)

    for g in range(heads):
        mixed = acc[g]
        out_ref[:, g * HD : (g + 1) * HD] = (mixed[:, :HD] / mixed[:, HD:]).astype(out_ref.dtype)

    capacity = cache_ref.shape[1] // PAGE
    empty = jnp.zeros((PAGE, HD), cache_ref.dtype)
    for s in range(cache_ref.shape[0]):

        @pl.loop(0, capacity)
        def _(r):
            page = slots[s * capacity + r]
            token = pl.ds(pl.multiple_of(jnp.maximum(page, 0) * PAGE, PAGE), PAGE)
            row = pl.ds(pl.multiple_of(r * PAGE, PAGE), PAGE)
            cache_ref[s, row, :HD] = jnp.where(page >= 0, k_ref[token, :], empty)
            cache_ref[s, row, HD:] = jnp.where(page >= 0, v_ref[token, :], empty)


def attention(info, slots, queries, keys, values, start, n_pre, capacity):
    span = queries.shape[0]
    heads = queries.shape[1] // HD
    return pl.pallas_call(
        functools.partial(attention_kernel, heads, span),
        in_specs=[
            pl.BlockSpec(memory_space=pltpu.SMEM),
            pl.BlockSpec(memory_space=pltpu.SMEM),
            pl.BlockSpec(memory_space=pltpu.VMEM),
            pl.BlockSpec(memory_space=pltpu.VMEM),
            pl.BlockSpec(memory_space=pltpu.VMEM),
            pl.BlockSpec(memory_space=pltpu.VMEM),
        ],
        out_specs=[
            pl.BlockSpec(memory_space=pltpu.VMEM),
            pl.BlockSpec(memory_space=pltpu.VMEM),
        ],
        out_shape=[
            jax.ShapeDtypeStruct(queries.shape, jnp.bfloat16),
            jax.ShapeDtypeStruct((n_pre, capacity * PAGE, 2 * HD), jnp.bfloat16),
        ],
        scratch_shapes=[
            pltpu.VMEM((heads, span, 2 * HD), jnp.float32),
            pltpu.VMEM((heads, span, 1), jnp.float32),
        ],
        compiler_params=pltpu.CompilerParams(vmem_limit_bytes=KERNEL_VMEM),
        cost_estimate=pl.CostEstimate(
            flops=4 * heads * span * span * n_pre * HD,
            bytes_accessed=4 * queries.size * 2,
            transcendentals=heads * span * span * n_pre,
        ),
        name="attention",
    )(info, slots, queries, keys, values, start)


PIECES = 8


def chunk_copy(h_ref, chunk, h_buf, sem):
    depth = h_buf.shape[1]
    columns = pl.ds(pl.multiple_of(chunk * depth, depth), depth)
    return pltpu.make_async_copy(h_ref.at[:, columns], h_buf, sem)


def add_pieces(member, chunk, pieces, w_ref, acc_ref):
    share = pieces[0].shape[1]
    half = PIECES // 2
    for side in range(2):

        @pl.when(jnp.bitwise_xor(member // half, side) == lax.rem(chunk, 2))
        def _():
            total = acc_ref[...]
            for j in range(side * half, side * half + half):
                row = lax.rem(jnp.bitwise_xor(member, j), half) * share
                total += jnp.dot(
                    pieces[j][...],
                    w_ref[pl.ds(pl.multiple_of(row, share), share), :],
                    preferred_element_type=jnp.float32,
                )
            acc_ref[...] = total


def near_kernel(place, h_ref, kw_ref, vw_ref, out_ref, h_buf, sem):
    copy = chunk_copy(h_ref, place[0], h_buf, sem)
    copy.start()
    weight = jnp.concatenate([kw_ref[...], vw_ref[...]], axis=1)
    copy.wait()
    out_ref[...] = jnp.dot(h_buf[...], weight, preferred_element_type=jnp.float32)


def partial_kernel(place, h_ref, kw_ref, vw_ref, before_ref, owner_ref, out_ref, h_buf, sem):
    copy = chunk_copy(h_ref, place[0], h_buf, sem)
    copy.start()
    span = h_buf.shape[0]
    weight = jnp.concatenate([kw_ref[...], vw_ref[...]], axis=1)
    out_ref[span:, :HD] = owner_ref[...]
    out_ref[span:, HD:] = owner_ref[...]
    copy.wait()
    out_ref[:span] = before_ref[...] + jnp.dot(
        h_buf[...], weight, preferred_element_type=jnp.float32
    )


def facing_kernel(place, h_ref, kw_ref, vw_ref, *refs):
    pieces = refs[:PIECES]
    out_ref, h_buf, w_buf, sem = refs[PIECES:]
    copy = chunk_copy(h_ref, place[0], h_buf, sem)
    copy.start()
    span = h_buf.shape[0]
    w_buf[:, :HD] = kw_ref[...]
    w_buf[:, HD:] = vw_ref[...]
    out_ref[span:] = jnp.zeros((span, 2 * HD), jnp.float32)
    add_pieces(place[2], place[0], pieces, w_buf, out_ref.at[pl.ds(span, span)])
    copy.wait()
    out_ref[:span] = jnp.dot(h_buf[...], w_buf[...], preferred_element_type=jnp.float32)


def distant_kernel(column, place, h_ref, w_ref, near_ref, outer_ref, facing_ref, bias_ref, *refs):
    pieces = refs[:PIECES]
    out_ref, h_buf, acc, sem = refs[PIECES:]
    copy = chunk_copy(h_ref, place[0], h_buf, sem)
    copy.start()
    span = h_buf.shape[0]
    part = slice(column * HD, column * HD + HD)
    own_at = pl.multiple_of(place[1] * span, span)
    outer_at = pl.multiple_of((1 - place[1]) * span, span)
    bias = bias_ref[...].astype(jnp.float32)
    acc[...] = outer_ref[:span, part] + facing_ref[span:, part] + bias
    add_pieces(place[2], place[0], pieces, w_ref, acc)
    out_ref[pl.ds(outer_at, span), :] = acc[...].astype(jnp.bfloat16)
    own = near_ref[:span, part] + facing_ref[:span, part] + bias
    copy.wait()
    own += jnp.dot(h_buf[...], w_ref[...], preferred_element_type=jnp.float32)
    out_ref[pl.ds(own_at, span), :] = own.astype(jnp.bfloat16)
    if column == 0:
        mine, theirs = near_ref[span:, :HD], outer_ref[span:, :HD]
        lower = jnp.where(place[1] == 0, mine, theirs)
        upper = jnp.where(place[1] == 0, theirs, mine)
        out_ref[2 * span :] = jnp.concatenate([lower, upper], axis=0).astype(jnp.bfloat16)


ANY = pl.BlockSpec(memory_space=pl.ANY)
EXTRA = 8


def call_project(kernel, name, place, operands, rows, columns, kind, scratch):
    whole = [pl.BlockSpec(x.shape, lambda k, place: (0, 0)) for x in operands[1:]]
    return pl.pallas_call(
        kernel,
        grid_spec=pltpu.PrefetchScalarGridSpec(
            num_scalar_prefetch=1,
            grid=(1,),
            in_specs=[ANY] + whole,
            out_specs=pl.BlockSpec((rows, columns), lambda k, place: (0, 0)),
            scratch_shapes=scratch + [pltpu.SemaphoreType.DMA],
        ),
        out_shape=jax.ShapeDtypeStruct((rows, columns), kind),
        compiler_params=pltpu.CompilerParams(vmem_limit_bytes=KERNEL_VMEM),
        cost_estimate=pl.CostEstimate(flops=0, bytes_accessed=0, transcendentals=0),
        name=name,
    )(place, *operands)


INWARD = [(0, 1), (3, 2)]
ACROSS = [(1, 2), (2, 1)]
OUTWARD = [(1, 0), (2, 3)]
SWAP = [(0, 1), (1, 0), (2, 3), (3, 2)]


def line_of_four(hidden, key_weight, value_weight, key_bias, value_bias, page_owner):
    index = lax.axis_index("pre")
    member = lax.axis_index(("dec", "tp"))
    span, width = hidden.shape
    depth = key_weight.shape[0]
    share = width // 2 // PIECES
    facing = 3 - index
    near = jnp.bitwise_xor(index, 1)
    distant = jnp.bitwise_xor(facing, 1)
    second = (index < 2).astype(jnp.int32)

    def send(x, pairs):
        return lax.ppermute(x, "pre", pairs)

    def trade(x, apart):
        return lax.ppermute(x, ("dec", "tp"), [(m, m ^ apart) for m in range(PIECES)])

    mine = second * (width // 2) + member * share
    cut = lax.dynamic_slice_in_dim(hidden, mine, share, axis=1)
    tie = lax.optimization_barrier
    key_facing = send(key_weight, ACROSS)
    cut = send(cut, INWARD)
    cut, key_after = tie((cut, key_weight))
    key_swapped = send(key_after, SWAP)
    key_facing, value_after = tie((key_facing, value_weight))
    value_facing = send(value_after, ACROSS)
    key_swapped, value_after = tie((key_swapped, value_weight))
    value_swapped = send(value_after, SWAP)
    chips = [trade(cut, 2), trade(cut, 4), trade(cut, 6)]
    chips, value_facing = tie((chips, value_facing))
    chips = [cut] + chips
    mates = [trade(x, 1) for x in chips]
    pieces = [x for both in zip(chips, mates) for x in both]
    key_distant = send(key_swapped, ACROSS)
    value_distant = send(value_swapped, ACROSS)

    def place(chunk):
        return jnp.stack([chunk, second, member])

    block = pltpu.VMEM((span, depth), jnp.bfloat16)
    both = pltpu.VMEM((depth, 2 * HD), jnp.bfloat16)
    own_part = call_project(
        near_kernel,
        "near",
        index[None],
        [hidden, key_weight, value_weight],
        span,
        2 * HD,
        jnp.float32,
        [block],
    )
    faced = call_project(
        facing_kernel,
        "facing",
        place(facing),
        [hidden, key_facing, value_facing] + pieces,
        2 * span,
        2 * HD,
        jnp.float32,
        [block, both],
    )
    faced, own_part, key_distant = tie((faced, own_part, key_distant))
    owners = jnp.broadcast_to(page_owner.T.astype(jnp.float32), (EXTRA, page_owner.shape[0]))
    owners = jnp.pad(owners, ((0, 0), (0, HD - page_owner.shape[0])))
    own_part = call_project(
        partial_kernel,
        "partial",
        near[None],
        [hidden, key_swapped, value_swapped, own_part, owners],
        span + EXTRA,
        2 * HD,
        jnp.float32,
        [block],
    )
    outer_part = send(own_part, INWARD)

    def finish(column, weight, bias):
        pair = call_project(
            functools.partial(distant_kernel, column),
            "distant",
            place(distant),
            [hidden, weight, own_part, outer_part, faced, bias[None, :]] + pieces,
            2 * span + (2 * EXTRA if column == 0 else 0),
            HD,
            jnp.bfloat16,
            [block, pltpu.VMEM((span, HD), jnp.float32)],
        )
        out = send(pair, OUTWARD)
        across = send(pair, ACROSS)
        return pair, out, across, send(across, OUTWARD)

    keys = finish(0, key_distant, key_bias)
    values = finish(1, value_distant, value_bias)
    return keys, values


def softmax_step(q, keys, values, allowed, before):
    factor = HD**-0.5 * math.log2(math.e)
    scores = lax.dot_general(q, keys, (((1,), (1,)), ((), ())), preferred_element_type=jnp.float32)
    scores = jnp.where(allowed, scores, NEG)
    peak = jnp.max(scores, axis=1, keepdims=True)
    if before is not None:
        peak = jnp.maximum(peak, before[0])
    weights = jnp.exp2(scores * factor - peak * factor).astype(jnp.bfloat16)
    mixed = jnp.dot(weights, values, preferred_element_type=jnp.float32)
    total, mixed = mixed[:, HD:], mixed[:, :HD]
    if before is not None:
        shrink = jnp.exp2((before[0] - peak) * factor)
        total = total + before[1] * shrink
        mixed = mixed + before[2] * shrink
    return peak, total, mixed


def with_ones(values):
    return jnp.concatenate([values, jnp.ones_like(values)], axis=1)


def prompt_starts(seg_ref, first, span):
    seg = seg_ref[...]
    position = (lax.broadcasted_iota(jnp.int32, (span, 1), 0) + first).astype(jnp.float32)
    start = jnp.zeros((span, 1), jnp.float32)
    for v in range(1, PROMPTS):
        lower = jnp.where(seg < v, 1.0, 0.0)
        bound = jnp.sum(jnp.sum(lower, axis=1, keepdims=True), axis=0, keepdims=True)
        start = jnp.where(position >= bound, bound, start)
    return start.astype(jnp.int32)


def read_owners(held_k, span, listed, named, sem):
    listed[...] = held_k[2 * span :].astype(jnp.float32).astype(jnp.int32)
    copy = pltpu.make_async_copy(listed, named, sem)
    copy.start()
    return copy


def place_pages(index, span, named, held_k, held_v, cache_ref):
    cache_ref[...] = jnp.zeros(cache_ref.shape, cache_ref.dtype)
    for s in range(2):
        rank = jnp.int32(0)
        for p in range(span // PAGE):
            owned = named[s * EXTRA, p] == index
            tokens = pl.ds(s * span + p * PAGE, PAGE)
            at = pl.ds(pl.multiple_of(rank * PAGE, PAGE), PAGE)

            @pl.when(owned)
            def _():
                cache_ref[s, at, :HD] = held_k[tokens, :]
                cache_ref[s, at, HD:] = held_v[tokens, :]

            rank = rank + owned.astype(jnp.int32)


def own_kernel(
    heads,
    info,
    q_ref,
    seg_ref,
    k_in,
    k_out,
    v_in,
    v_out,
    top,
    total,
    mix,
    cache_ref,
    held_k,
    held_v,
    q_buf,
    listed,
    named,
    sems,
):
    copy = pltpu.make_async_copy(q_ref, q_buf, sems.at[0])
    copy.start()
    span = q_buf.shape[0]
    index = info[0]
    inner = (index == 1) | (index == 2)
    held_k[...] = jnp.where(inner, k_in[...], k_out[...])
    held_v[...] = jnp.where(inner, v_in[...], v_out[...])
    owners = read_owners(held_k, span, listed, named, sems.at[1])
    keys = held_k[: 2 * span]
    values = with_ones(held_v[...])
    columns = lax.broadcasted_iota(jnp.int32, (span, 2 * span), 1)
    rows = lax.broadcasted_iota(jnp.int32, (span, 2 * span), 0)
    start = prompt_starts(seg_ref, index * span, span)
    allowed = (columns <= rows + lax.rem(index, 2) * span) & (
        columns >= start - (index // 2) * 2 * span
    )
    copy.wait()
    for g in range(heads):
        q = q_buf[:, g * HD : (g + 1) * HD]
        peak, sums, mixed = softmax_step(q, keys, values, allowed, None)
        top[g] = peak
        total[g] = sums[:, :1]
        mix[g] = mixed
    owners.wait()
    place_pages(index, span, named, held_k, held_v, cache_ref)


def far_kernel(
    heads,
    info,
    q_ref,
    seg_ref,
    k_across,
    k_far,
    v_across,
    v_far,
    top,
    total,
    mix,
    own_cache,
    out_ref,
    cache_ref,
    held_k,
    held_v,
    q_buf,
    listed,
    named,
    sems,
):
    copy = pltpu.make_async_copy(q_ref, q_buf, sems.at[0])
    copy.start()
    span = q_buf.shape[0]
    index = info[0]
    inner = (index == 1) | (index == 2)
    held_k[...] = jnp.where(inner, k_across[...], k_far[...])
    held_v[...] = jnp.where(inner, v_across[...], v_far[...])
    cache_ref[pl.ds(index // 2 * 2, 2)] = own_cache[...]
    owners = read_owners(held_k, span, listed, named, sems.at[1])
    copy.wait()

    @pl.when(index < 2)
    def _():
        for g in range(heads):
            out_ref[:, g * HD : (g + 1) * HD] = (mix[g] / total[g]).astype(out_ref.dtype)

    @pl.when(index >= 2)
    def _():
        keys = held_k[: 2 * span]
        values = with_ones(held_v[...])
        columns = lax.broadcasted_iota(jnp.int32, (span, 2 * span), 1)
        allowed = columns >= prompt_starts(seg_ref, index * span, span)
        for g in range(heads):
            q = q_buf[:, g * HD : (g + 1) * HD]
            _, sums, mixed = softmax_step(q, keys, values, allowed, (top[g], total[g], mix[g]))
            out_ref[:, g * HD : (g + 1) * HD] = (mixed / sums).astype(out_ref.dtype)

    owners.wait()
    far_cache = cache_ref.at[pl.ds((1 - index // 2) * 2, 2)]
    place_pages(index, span, named, held_k, held_v, far_cache)


def attention_of_pairs(queries, segment_ids, keys, values, capacity):
    span = queries.shape[0]
    heads = queries.shape[1] // HD
    info = lax.axis_index("pre").astype(jnp.int32)[None]
    segments = segment_ids.reshape(-1, HD)
    smem = pl.BlockSpec(memory_space=pltpu.SMEM)
    vmem = pl.BlockSpec(memory_space=pltpu.VMEM)
    cost = pl.CostEstimate(flops=0, bytes_accessed=0, transcendentals=0)
    params = pltpu.CompilerParams(vmem_limit_bytes=KERNEL_VMEM)
    scratch = [
        pltpu.VMEM((2 * span + 2 * EXTRA, HD), jnp.bfloat16),
        pltpu.VMEM((2 * span, HD), jnp.bfloat16),
        pltpu.VMEM(queries.shape, jnp.bfloat16),
        pltpu.VMEM((2 * EXTRA, HD), jnp.int32),
        pltpu.SMEM((2 * EXTRA, HD), jnp.int32),
        pltpu.SemaphoreType.DMA((2,)),
    ]
    state = pl.pallas_call(
        functools.partial(own_kernel, heads),
        in_specs=[smem, ANY] + [vmem] * 5,
        out_specs=[vmem] * 4,
        out_shape=[
            jax.ShapeDtypeStruct((heads, span, 1), jnp.float32),
            jax.ShapeDtypeStruct((heads, span, 1), jnp.float32),
            jax.ShapeDtypeStruct((heads, span, HD), jnp.float32),
            jax.ShapeDtypeStruct((2, capacity * PAGE, 2 * HD), jnp.bfloat16),
        ],
        scratch_shapes=scratch,
        compiler_params=params,
        cost_estimate=cost,
        name="attend_own",
    )(info, queries, segments, *keys[:2], *values[:2])
    return pl.pallas_call(
        functools.partial(far_kernel, heads),
        in_specs=[smem, ANY] + [vmem] * 9,
        out_specs=[vmem] * 2,
        out_shape=[
            jax.ShapeDtypeStruct(queries.shape, jnp.bfloat16),
            jax.ShapeDtypeStruct((4, capacity * PAGE, 2 * HD), jnp.bfloat16),
        ],
        scratch_shapes=scratch,
        compiler_params=params,
        cost_estimate=cost,
        name="attend_far",
    )(info, queries, segments, *keys[2:], *values[2:], *state)


def gathered(hidden, key_weight, value_weight, key_bias, value_bias):
    joined = jnp.concatenate([key_weight, value_weight], axis=1)
    joined = lax.all_gather(joined, "pre", axis=0, tiled=True)
    bias = jnp.concatenate([key_bias, value_bias]).astype(jnp.float32)
    local = jnp.dot(hidden, joined, preferred_element_type=jnp.float32) + bias
    both = lax.all_gather(local.astype(jnp.bfloat16), "pre", axis=0, tiled=True)
    return both[:, :HD], both[:, HD:]


def body(hidden, queries, key_weight, value_weight, key_bias, value_bias, segment_ids, page_owner):
    n_pre = lax.axis_size("pre")
    index = lax.axis_index("pre")
    span = hidden.shape[0]
    pages_dev = span // PAGE
    capacity = 2 * pages_dev // n_pre
    assert key_weight.shape[1] == HD
    arrays = (hidden, key_weight, value_weight, key_bias, value_bias)
    if n_pre == 4:
        keys, values = line_of_four(*arrays, page_owner)
        mixed, cache = attention_of_pairs(queries, segment_ids, keys, values, capacity)
        return (mixed, cache[None])

    own_segments = lax.dynamic_slice_in_dim(segment_ids, index * span, span)
    start = jnp.sum(
        (segment_ids[None, :] < own_segments[:, None]).astype(jnp.int32), axis=1, keepdims=True
    )
    info = jnp.stack([index, start[0, 0] // span]).astype(jnp.int32)
    owners = lax.all_gather(page_owner[:, 0], "pre")
    keys, values = gathered(*arrays)
    mine = (owners == index).astype(jnp.int32)
    rank = jnp.cumsum(mine, axis=1) - mine
    numbers = jnp.arange(n_pre * pages_dev, dtype=jnp.int32).reshape(n_pre, 1, pages_dev)
    wanted = (mine[:, None, :] == 1) & (
        rank[:, None, :] == jnp.arange(capacity, dtype=jnp.int32)[None, :, None]
    )
    slots = jnp.max(jnp.where(wanted, numbers, -1), axis=2).reshape(-1)
    mixed, cache = attention(info, slots, queries, keys, values, start, n_pre, capacity)
    return (mixed, cache[None])


def solution(mesh):
    return jax.shard_map(
        body,
        mesh=mesh,
        in_specs=(
            P(("group", "pre"), None),
            P(("group", "pre"), ("dec", "tp")),
            P("pre", ("dec", "tp")),
            P("pre", ("dec", "tp")),
            P(("dec", "tp")),
            P(("dec", "tp")),
            P("group"),
            P(("group", "pre"), None),
        ),
        out_specs=(
            P(("group", "pre"), ("dec", "tp")),
            P(("group", "pre"), None, None, ("dec", "tp")),
        ),
        check_vma=False,
    )
```

```python
import functools
import math

import jax
import jax.numpy as jnp
from jax import lax
from jax.experimental import pallas as pl
from jax.experimental.pallas import tpu as pltpu
from jax.sharding import PartitionSpec as P

HD = 128
PAGE = 16
NEG = -1e30
KERNEL_VMEM = 24 * 1024 * 1024
PROMPTS = 4


def attention_kernel(heads, span, info, slots, q_ref, k_ref, v_ref, start_ref, out_ref, cache_ref, acc, top):
    index = info[0]
    first = info[1]
    factor = HD**-0.5 * math.log2(math.e)
    columns = lax.broadcasted_iota(jnp.int32, (span, span), 1)
    rows = lax.broadcasted_iota(jnp.int32, (span, span), 0)

    def block(j, diagonal):
        at = pl.multiple_of(j * span, span)
        keys = k_ref[pl.ds(at, span), :]
        values = jnp.concatenate(
            [v_ref[pl.ds(at, span), :], jnp.ones((span, HD), jnp.bfloat16)], axis=1
        )
        allowed = columns >= start_ref[...] - at
        if diagonal:
            allowed = allowed & (columns <= rows)
        for g in range(heads):
            scores = lax.dot_general(
                q_ref[:, g * HD : (g + 1) * HD],
                keys,
                (((1,), (1,)), ((), ())),
                preferred_element_type=jnp.float32,
            )
            scores = jnp.where(allowed, scores, NEG)
            peak = jnp.max(scores, axis=1, keepdims=True)
            if not diagonal:
                before = top[g]
                peak = jnp.maximum(peak, before)
            weights = jnp.exp2(scores * factor - peak * factor).astype(jnp.bfloat16)
            mixed = jnp.dot(weights, values, preferred_element_type=jnp.float32)
            if not diagonal:
                mixed = mixed + acc[g] * jnp.exp2((before - peak) * factor)
            top[g] = peak
            acc[g] = mixed

    block(index, True)

    @pl.loop(first, index)
    def _(j):
        block(j, False)

    for g in range(heads):
        mixed = acc[g]
        out_ref[:, g * HD : (g + 1) * HD] = (mixed[:, :HD] / mixed[:, HD:]).astype(out_ref.dtype)

    capacity = cache_ref.shape[1] // PAGE
    empty = jnp.zeros((PAGE, HD), cache_ref.dtype)
    for s in range(cache_ref.shape[0]):

        @pl.loop(0, capacity)
        def _(r):
            page = slots[s * capacity + r]
            token = pl.ds(pl.multiple_of(jnp.maximum(page, 0) * PAGE, PAGE), PAGE)
            row = pl.ds(pl.multiple_of(r * PAGE, PAGE), PAGE)
            cache_ref[s, row, :HD] = jnp.where(page >= 0, k_ref[token, :], empty)
            cache_ref[s, row, HD:] = jnp.where(page >= 0, v_ref[token, :], empty)


def attention(info, slots, queries, keys, values, start, n_pre, capacity):
    span = queries.shape[0]
    heads = queries.shape[1] // HD
    return pl.pallas_call(
        functools.partial(attention_kernel, heads, span),
        in_specs=[
            pl.BlockSpec(memory_space=pltpu.SMEM),
            pl.BlockSpec(memory_space=pltpu.SMEM),
            pl.BlockSpec(memory_space=pltpu.VMEM),
            pl.BlockSpec(memory_space=pltpu.VMEM),
            pl.BlockSpec(memory_space=pltpu.VMEM),
            pl.BlockSpec(memory_space=pltpu.VMEM),
        ],
        out_specs=[
            pl.BlockSpec(memory_space=pltpu.VMEM),
            pl.BlockSpec(memory_space=pltpu.VMEM),
        ],
        out_shape=[
            jax.ShapeDtypeStruct(queries.shape, jnp.bfloat16),
            jax.ShapeDtypeStruct((n_pre, capacity * PAGE, 2 * HD), jnp.bfloat16),
        ],
        scratch_shapes=[
            pltpu.VMEM((heads, span, 2 * HD), jnp.float32),
            pltpu.VMEM((heads, span, 1), jnp.float32),
        ],
        compiler_params=pltpu.CompilerParams(vmem_limit_bytes=KERNEL_VMEM),
        cost_estimate=pl.CostEstimate(
            flops=4 * heads * span * span * n_pre * HD,
            bytes_accessed=4 * queries.size * 2,
            transcendentals=heads * span * span * n_pre,
        ),
        name="attention",
    )(info, slots, queries, keys, values, start)


PIECES = 8


def chunk_copy(h_ref, chunk, h_buf, sem):
    depth = h_buf.shape[1]
    columns = pl.ds(pl.multiple_of(chunk * depth, depth), depth)
    return pltpu.make_async_copy(h_ref.at[:, columns], h_buf, sem)


def add_pieces(member, chunk, pieces, w_ref, acc_ref):
    share = pieces[0].shape[1]
    half = PIECES // 2
    for side in range(2):

        @pl.when(jnp.bitwise_xor(member // half, side) == lax.rem(chunk, 2))
        def _():
            total = acc_ref[...]
            for j in range(side * half, side * half + half):
                row = lax.rem(jnp.bitwise_xor(member, j), half) * share
                total += jnp.dot(
                    pieces[j][...],
                    w_ref[pl.ds(pl.multiple_of(row, share), share), :],
                    preferred_element_type=jnp.float32,
                )
            acc_ref[...] = total


def near_kernel(place, h_ref, kw_ref, vw_ref, out_ref, h_buf, w_buf, sems):
    copies = [
        chunk_copy(h_ref, place[0], h_buf, sems.at[0]),
        pltpu.make_async_copy(kw_ref, w_buf.at[:, pl.ds(0, HD)], sems.at[1]),
        pltpu.make_async_copy(vw_ref, w_buf.at[:, pl.ds(HD, HD)], sems.at[2]),
    ]
    for copy in copies:
        copy.start()
    for copy in copies:
        copy.wait()
    out_ref[...] = jnp.dot(h_buf[...], w_buf[...], preferred_element_type=jnp.float32)


def partial_kernel(place, h_ref, kw_ref, vw_ref, before_ref, owner_ref, out_ref, h_buf, sem):
    copy = chunk_copy(h_ref, place[0], h_buf, sem)
    copy.start()
    span = h_buf.shape[0]
    weight = jnp.concatenate([kw_ref[...], vw_ref[...]], axis=1)
    out_ref[span:, :HD] = owner_ref[...]
    out_ref[span:, HD:] = owner_ref[...]
    copy.wait()
    out_ref[:span] = before_ref[...] + jnp.dot(
        h_buf[...], weight, preferred_element_type=jnp.float32
    )


def facing_kernel(place, h_ref, kw_ref, vw_ref, *refs):
    pieces = refs[:PIECES]
    out_ref, h_buf, w_buf, sem = refs[PIECES:]
    copy = chunk_copy(h_ref, place[0], h_buf, sem)
    copy.start()
    span = h_buf.shape[0]
    w_buf[:, :HD] = kw_ref[...]
    w_buf[:, HD:] = vw_ref[...]
    out_ref[span:] = jnp.zeros((span, 2 * HD), jnp.float32)
    add_pieces(place[2], place[0], pieces, w_buf, out_ref.at[pl.ds(span, span)])
    copy.wait()
    out_ref[:span] = jnp.dot(h_buf[...], w_buf[...], preferred_element_type=jnp.float32)


def distant_kernel(column, place, h_ref, w_ref, near_ref, outer_ref, facing_ref, bias_ref, *refs):
    pieces = refs[:PIECES]
    out_ref, h_buf, acc, sem = refs[PIECES:]
    copy = chunk_copy(h_ref, place[0], h_buf, sem)
    copy.start()
    span = h_buf.shape[0]
    part = slice(column * HD, column * HD + HD)
    own_at = pl.multiple_of(place[1] * span, span)
    outer_at = pl.multiple_of((1 - place[1]) * span, span)
    bias = bias_ref[...].astype(jnp.float32)
    acc[...] = outer_ref[:span, part] + facing_ref[span:, part] + bias
    add_pieces(place[2], place[0], pieces, w_ref, acc)
    out_ref[pl.ds(outer_at, span), :] = acc[...].astype(jnp.bfloat16)
    own = near_ref[:span, part] + facing_ref[:span, part] + bias
    copy.wait()
    own += jnp.dot(h_buf[...], w_ref[...], preferred_element_type=jnp.float32)
    out_ref[pl.ds(own_at, span), :] = own.astype(jnp.bfloat16)
    if column == 0:
        mine, theirs = near_ref[span:, :HD], outer_ref[span:, :HD]
        lower = jnp.where(place[1] == 0, mine, theirs)
        upper = jnp.where(place[1] == 0, theirs, mine)
        out_ref[2 * span :] = jnp.concatenate([lower, upper], axis=0).astype(jnp.bfloat16)


EXTRA = 8
HELD = pl.BlockSpec(memory_space=pltpu.HBM)
FAST = pl.BlockSpec(memory_space=pltpu.VMEM)
SCALAR = pl.BlockSpec(memory_space=pltpu.SMEM)


def in_hbm(x):
    return pltpu.with_memory_space_constraint(x, pltpu.HBM)


def call_project(kernel, name, place, operands, rows, columns, kind, scratch, held=1, copies=()):
    return pl.pallas_call(
        kernel,
        in_specs=[SCALAR] + [HELD] * held + [FAST] * (len(operands) - held),
        out_specs=FAST,
        out_shape=jax.ShapeDtypeStruct((rows, columns), kind),
        scratch_shapes=scratch + [pltpu.SemaphoreType.DMA(copies)],
        compiler_params=pltpu.CompilerParams(vmem_limit_bytes=KERNEL_VMEM),
        cost_estimate=pl.CostEstimate(flops=0, bytes_accessed=0, transcendentals=0),
        name=name,
    )(place, *[in_hbm(x) for x in operands[:held]], *operands[held:])


INWARD = [(0, 1), (3, 2)]
ACROSS = [(1, 2), (2, 1)]
OUTWARD = [(1, 0), (2, 3)]
SWAP = [(0, 1), (1, 0), (2, 3), (3, 2)]


def line_of_four(hidden, key_weight, value_weight, key_bias, value_bias, page_owner):
    index = lax.axis_index("pre")
    member = lax.axis_index(("dec", "tp"))
    span, width = hidden.shape
    depth = key_weight.shape[0]
    share = width // 2 // PIECES
    facing = 3 - index
    near = jnp.bitwise_xor(index, 1)
    distant = jnp.bitwise_xor(facing, 1)
    second = (index < 2).astype(jnp.int32)

    def send(x, pairs):
        return lax.ppermute(x, "pre", pairs)

    def trade(x, apart):
        return lax.ppermute(x, ("dec", "tp"), [(m, m ^ apart) for m in range(PIECES)])

    mine = second * (width // 2) + member * share
    cut = lax.dynamic_slice_in_dim(hidden, mine, share, axis=1)
    tie = lax.optimization_barrier
    block = pltpu.VMEM((span, depth), jnp.bfloat16)
    both = pltpu.VMEM((depth, 2 * HD), jnp.bfloat16)
    own_part = call_project(
        near_kernel,
        "near",
        index[None],
        [hidden, key_weight, value_weight],
        span,
        2 * HD,
        jnp.float32,
        [block, both],
        held=3,
        copies=(3,),
    )
    cut = send(cut, INWARD)
    key_facing = send(key_weight, ACROSS)
    key_facing, value_after = tie((key_facing, value_weight))
    value_facing = send(value_after, ACROSS)
    cut, key_after, own_part = tie((cut, key_weight, own_part))
    key_swapped = send(key_after, SWAP)
    key_swapped, value_after = tie((key_swapped, value_weight))
    value_swapped = send(value_after, SWAP)
    chips = [cut, trade(cut, 2), trade(cut, 4), trade(cut, 6)]
    chips, value_facing = tie((chips, value_facing))
    mates = [trade(x, 1) for x in chips]
    pieces = [x for both_cores in zip(chips, mates) for x in both_cores]
    key_distant = send(key_swapped, ACROSS)
    value_distant = send(value_swapped, ACROSS)

    def place(chunk):
        return jnp.stack([chunk, second, member])

    faced = call_project(
        facing_kernel,
        "facing",
        place(facing),
        [hidden, key_facing, value_facing] + pieces,
        2 * span,
        2 * HD,
        jnp.float32,
        [block, both],
    )
    own_part, key_distant = tie((own_part, key_distant))
    owners = jnp.broadcast_to(page_owner.T.astype(jnp.float32), (EXTRA, page_owner.shape[0]))
    owners = jnp.pad(owners, ((0, 0), (0, HD - page_owner.shape[0])))
    own_part = call_project(
        partial_kernel,
        "partial",
        near[None],
        [hidden, key_swapped, value_swapped, own_part, owners],
        span + EXTRA,
        2 * HD,
        jnp.float32,
        [block],
    )
    outer_part = send(own_part, INWARD)

    def finish(column, weight, bias):
        return call_project(
            functools.partial(distant_kernel, column),
            "distant",
            place(distant),
            [hidden, weight, own_part, outer_part, faced, bias[None, :]] + pieces,
            2 * span + (2 * EXTRA if column == 0 else 0),
            HD,
            jnp.bfloat16,
            [block, pltpu.VMEM((span, HD), jnp.float32)],
        )

    keys = finish(0, key_distant, key_bias)
    keys_out, keys_across = send(keys, OUTWARD), send(keys, ACROSS)
    values = finish(1, value_distant, value_bias)
    values_across = send(values, ACROSS)
    keys_out, values_after = tie((keys_out, values))
    values_out = send(values_after, OUTWARD)
    keys_across, values_across = tie((keys_across, values_across))
    keys_far, values_far = send(keys_across, OUTWARD), send(values_across, OUTWARD)
    return (
        (keys, keys_out, keys_across, keys_far),
        (values, values_out, values_across, values_far),
    )


def softmax_step(q, keys, values, allowed, before):
    factor = HD**-0.5 * math.log2(math.e)
    scores = lax.dot_general(q, keys, (((1,), (1,)), ((), ())), preferred_element_type=jnp.float32)
    scores = jnp.where(allowed, scores, NEG)
    peak = jnp.max(scores, axis=1, keepdims=True)
    if before is not None:
        peak = jnp.maximum(peak, before[0])
    weights = jnp.exp2(scores * factor - peak * factor).astype(jnp.bfloat16)
    mixed = jnp.dot(weights, values, preferred_element_type=jnp.float32)
    total, mixed = mixed[:, HD:], mixed[:, :HD]
    if before is not None:
        shrink = jnp.exp2((before[0] - peak) * factor)
        total = total + before[1] * shrink
        mixed = mixed + before[2] * shrink
    return peak, total, mixed


def with_ones(values):
    return jnp.concatenate([values, jnp.ones_like(values)], axis=1)


def prompt_starts(seg_ref, first, span):
    seg = seg_ref[...]
    position = (lax.broadcasted_iota(jnp.int32, (span, 1), 0) + first).astype(jnp.float32)
    start = jnp.zeros((span, 1), jnp.float32)
    for v in range(1, PROMPTS):
        lower = jnp.where(seg < v, 1.0, 0.0)
        bound = jnp.sum(jnp.sum(lower, axis=1, keepdims=True), axis=0, keepdims=True)
        start = jnp.where(position >= bound, bound, start)
    return start.astype(jnp.int32)


def read_owners(held_k, span, listed, named, sem):
    listed[...] = held_k[2 * span :].astype(jnp.float32).astype(jnp.int32)
    copy = pltpu.make_async_copy(listed, named, sem)
    copy.start()
    return copy


def place_pages(index, span, named, held_k, held_v, cache_ref):
    cache_ref[...] = jnp.zeros(cache_ref.shape, cache_ref.dtype)
    for s in range(2):
        rank = jnp.int32(0)
        for p in range(span // PAGE):
            owned = named[s * EXTRA, p] == index
            tokens = pl.ds(s * span + p * PAGE, PAGE)
            at = pl.ds(pl.multiple_of(rank * PAGE, PAGE), PAGE)

            @pl.when(owned)
            def _():
                cache_ref[s, at, :HD] = held_k[tokens, :]
                cache_ref[s, at, HD:] = held_v[tokens, :]

            rank = rank + owned.astype(jnp.int32)


def own_kernel(
    heads,
    info,
    q_ref,
    seg_ref,
    k_in,
    k_out,
    v_in,
    v_out,
    top,
    total,
    mix,
    cache_ref,
    held_k,
    held_v,
    q_buf,
    listed,
    named,
    sems,
):
    copy = pltpu.make_async_copy(q_ref, q_buf, sems.at[0])
    copy.start()
    span = q_buf.shape[0]
    index = info[0]
    inner = (index == 1) | (index == 2)
    held_k[...] = jnp.where(inner, k_in[...], k_out[...])
    held_v[...] = jnp.where(inner, v_in[...], v_out[...])
    owners = read_owners(held_k, span, listed, named, sems.at[1])
    keys = held_k[: 2 * span]
    values = with_ones(held_v[...])
    columns = lax.broadcasted_iota(jnp.int32, (span, 2 * span), 1)
    rows = lax.broadcasted_iota(jnp.int32, (span, 2 * span), 0)
    start = prompt_starts(seg_ref, index * span, span)
    allowed = (columns <= rows + lax.rem(index, 2) * span) & (
        columns >= start - (index // 2) * 2 * span
    )
    copy.wait()
    for g in range(heads):
        q = q_buf[:, g * HD : (g + 1) * HD]
        peak, sums, mixed = softmax_step(q, keys, values, allowed, None)
        top[g] = peak
        total[g] = sums[:, :1]
        mix[g] = mixed
    owners.wait()
    place_pages(index, span, named, held_k, held_v, cache_ref)


def far_kernel(
    heads,
    info,
    q_ref,
    seg_ref,
    k_across,
    k_far,
    v_across,
    v_far,
    top,
    total,
    mix,
    own_cache,
    out_ref,
    cache_ref,
    held_k,
    held_v,
    q_buf,
    listed,
    named,
    sems,
):
    copy = pltpu.make_async_copy(q_ref, q_buf, sems.at[0])
    copy.start()
    span = q_buf.shape[0]
    index = info[0]
    inner = (index == 1) | (index == 2)
    held_k[...] = jnp.where(inner, k_across[...], k_far[...])
    held_v[...] = jnp.where(inner, v_across[...], v_far[...])
    cache_ref[pl.ds(index // 2 * 2, 2)] = own_cache[...]
    owners = read_owners(held_k, span, listed, named, sems.at[1])
    copy.wait()

    @pl.when(index < 2)
    def _():
        for g in range(heads):
            out_ref[:, g * HD : (g + 1) * HD] = (mix[g] / total[g]).astype(out_ref.dtype)

    @pl.when(index >= 2)
    def _():
        keys = held_k[: 2 * span]
        values = with_ones(held_v[...])
        columns = lax.broadcasted_iota(jnp.int32, (span, 2 * span), 1)
        allowed = columns >= prompt_starts(seg_ref, index * span, span)
        for g in range(heads):
            q = q_buf[:, g * HD : (g + 1) * HD]
            _, sums, mixed = softmax_step(q, keys, values, allowed, (top[g], total[g], mix[g]))
            out_ref[:, g * HD : (g + 1) * HD] = (mixed / sums).astype(out_ref.dtype)

    owners.wait()
    far_cache = cache_ref.at[pl.ds((1 - index // 2) * 2, 2)]
    place_pages(index, span, named, held_k, held_v, far_cache)


def attention_of_pairs(queries, segment_ids, keys, values, capacity):
    span = queries.shape[0]
    heads = queries.shape[1] // HD
    info = lax.axis_index("pre").astype(jnp.int32)[None]
    segments = segment_ids.reshape(-1, HD)
    scores = heads * span * 2 * span
    cost = pl.CostEstimate(flops=4 * scores * HD, bytes_accessed=8 * scores, transcendentals=scores)
    params = pltpu.CompilerParams(vmem_limit_bytes=KERNEL_VMEM)
    scratch = [
        pltpu.VMEM((2 * span + 2 * EXTRA, HD), jnp.bfloat16),
        pltpu.VMEM((2 * span, HD), jnp.bfloat16),
        pltpu.VMEM(queries.shape, jnp.bfloat16),
        pltpu.VMEM((2 * EXTRA, HD), jnp.int32),
        pltpu.SMEM((2 * EXTRA, HD), jnp.int32),
        pltpu.SemaphoreType.DMA((2,)),
    ]
    state = pl.pallas_call(
        functools.partial(own_kernel, heads),
        in_specs=[SCALAR, HELD] + [FAST] * 5,
        out_specs=[FAST] * 4,
        out_shape=[
            jax.ShapeDtypeStruct((heads, span, 1), jnp.float32),
            jax.ShapeDtypeStruct((heads, span, 1), jnp.float32),
            jax.ShapeDtypeStruct((heads, span, HD), jnp.float32),
            jax.ShapeDtypeStruct((2, capacity * PAGE, 2 * HD), jnp.bfloat16),
        ],
        scratch_shapes=scratch,
        compiler_params=params,
        cost_estimate=cost,
        name="attend_own",
    )(info, in_hbm(queries), segments, *keys[:2], *values[:2])
    return pl.pallas_call(
        functools.partial(far_kernel, heads),
        in_specs=[SCALAR, HELD] + [FAST] * 9,
        out_specs=[FAST] * 2,
        out_shape=[
            jax.ShapeDtypeStruct(queries.shape, jnp.bfloat16),
            jax.ShapeDtypeStruct((4, capacity * PAGE, 2 * HD), jnp.bfloat16),
        ],
        scratch_shapes=scratch,
        compiler_params=params,
        cost_estimate=cost,
        name="attend_far",
    )(info, in_hbm(queries), segments, *keys[2:], *values[2:], *state)


def gathered(hidden, key_weight, value_weight, key_bias, value_bias):
    joined = jnp.concatenate([key_weight, value_weight], axis=1)
    joined = lax.all_gather(joined, "pre", axis=0, tiled=True)
    bias = jnp.concatenate([key_bias, value_bias]).astype(jnp.float32)
    local = jnp.dot(hidden, joined, preferred_element_type=jnp.float32) + bias
    both = lax.all_gather(local.astype(jnp.bfloat16), "pre", axis=0, tiled=True)
    return both[:, :HD], both[:, HD:]


def body(hidden, queries, key_weight, value_weight, key_bias, value_bias, segment_ids, page_owner):
    n_pre = lax.axis_size("pre")
    index = lax.axis_index("pre")
    span = hidden.shape[0]
    pages_dev = span // PAGE
    capacity = 2 * pages_dev // n_pre
    assert key_weight.shape[1] == HD
    arrays = (hidden, key_weight, value_weight, key_bias, value_bias)
    if n_pre == 4:
        keys, values = line_of_four(*arrays, page_owner)
        mixed, cache = attention_of_pairs(queries, segment_ids, keys, values, capacity)
        return (mixed, cache[None])

    own_segments = lax.dynamic_slice_in_dim(segment_ids, index * span, span)
    start = jnp.sum(
        (segment_ids[None, :] < own_segments[:, None]).astype(jnp.int32), axis=1, keepdims=True
    )
    info = jnp.stack([index, start[0, 0] // span]).astype(jnp.int32)
    owners = lax.all_gather(page_owner[:, 0], "pre")
    keys, values = gathered(*arrays)
    mine = (owners == index).astype(jnp.int32)
    rank = jnp.cumsum(mine, axis=1) - mine
    numbers = jnp.arange(n_pre * pages_dev, dtype=jnp.int32).reshape(n_pre, 1, pages_dev)
    wanted = (mine[:, None, :] == 1) & (
        rank[:, None, :] == jnp.arange(capacity, dtype=jnp.int32)[None, :, None]
    )
    slots = jnp.max(jnp.where(wanted, numbers, -1), axis=2).reshape(-1)
    mixed, cache = attention(info, slots, queries, keys, values, start, n_pre, capacity)
    return (mixed, cache[None])


def solution(mesh):
    return jax.shard_map(
        body,
        mesh=mesh,
        in_specs=(
            P(("group", "pre"), None),
            P(("group", "pre"), ("dec", "tp")),
            P("pre", ("dec", "tp")),
            P("pre", ("dec", "tp")),
            P(("dec", "tp")),
            P(("dec", "tp")),
            P("group"),
            P(("group", "pre"), None),
        ),
        out_specs=(
            P(("group", "pre"), ("dec", "tp")),
            P(("group", "pre"), None, None, ("dec", "tp")),
        ),
        check_vma=False,
    )
```

```python
import functools
import math

import jax
import jax.numpy as jnp
from jax import lax
from jax.experimental import pallas as pl
from jax.experimental.pallas import tpu as pltpu
from jax.sharding import PartitionSpec as P

HD = 128
PAGE = 16
NEG = -1e30
KERNEL_VMEM = 16 * 1024 * 1024
PROMPTS = 4


def attention_kernel(heads, span, info, slots, q_ref, k_ref, v_ref, start_ref, out_ref, cache_ref, acc, top):
    index = info[0]
    first = info[1]
    factor = HD**-0.5 * math.log2(math.e)
    columns = lax.broadcasted_iota(jnp.int32, (span, span), 1)
    rows = lax.broadcasted_iota(jnp.int32, (span, span), 0)

    def block(j, diagonal):
        at = pl.multiple_of(j * span, span)
        keys = k_ref[pl.ds(at, span), :]
        values = jnp.concatenate(
            [v_ref[pl.ds(at, span), :], jnp.ones((span, HD), jnp.bfloat16)], axis=1
        )
        allowed = columns >= start_ref[...] - at
        if diagonal:
            allowed = allowed & (columns <= rows)
        for g in range(heads):
            scores = lax.dot_general(
                q_ref[:, g * HD : (g + 1) * HD],
                keys,
                (((1,), (1,)), ((), ())),
                preferred_element_type=jnp.float32,
            )
            scores = jnp.where(allowed, scores, NEG)
            peak = jnp.max(scores, axis=1, keepdims=True)
            if not diagonal:
                before = top[g]
                peak = jnp.maximum(peak, before)
            weights = jnp.exp2(scores * factor - peak * factor).astype(jnp.bfloat16)
            mixed = jnp.dot(weights, values, preferred_element_type=jnp.float32)
            if not diagonal:
                mixed = mixed + acc[g] * jnp.exp2((before - peak) * factor)
            top[g] = peak
            acc[g] = mixed

    block(index, True)

    @pl.loop(first, index)
    def _(j):
        block(j, False)

    for g in range(heads):
        mixed = acc[g]
        out_ref[:, g * HD : (g + 1) * HD] = (mixed[:, :HD] / mixed[:, HD:]).astype(out_ref.dtype)

    capacity = cache_ref.shape[1] // PAGE
    empty = jnp.zeros((PAGE, HD), cache_ref.dtype)
    for s in range(cache_ref.shape[0]):

        @pl.loop(0, capacity)
        def _(r):
            page = slots[s * capacity + r]
            token = pl.ds(pl.multiple_of(jnp.maximum(page, 0) * PAGE, PAGE), PAGE)
            row = pl.ds(pl.multiple_of(r * PAGE, PAGE), PAGE)
            cache_ref[s, row, :HD] = jnp.where(page >= 0, k_ref[token, :], empty)
            cache_ref[s, row, HD:] = jnp.where(page >= 0, v_ref[token, :], empty)


def attention(info, slots, queries, keys, values, start, n_pre, capacity):
    span = queries.shape[0]
    heads = queries.shape[1] // HD
    return pl.pallas_call(
        functools.partial(attention_kernel, heads, span),
        in_specs=[
            pl.BlockSpec(memory_space=pltpu.SMEM),
            pl.BlockSpec(memory_space=pltpu.SMEM),
            pl.BlockSpec(memory_space=pltpu.VMEM),
            pl.BlockSpec(memory_space=pltpu.VMEM),
            pl.BlockSpec(memory_space=pltpu.VMEM),
            pl.BlockSpec(memory_space=pltpu.VMEM),
        ],
        out_specs=[
            pl.BlockSpec(memory_space=pltpu.VMEM),
            pl.BlockSpec(memory_space=pltpu.VMEM),
        ],
        out_shape=[
            jax.ShapeDtypeStruct(queries.shape, jnp.bfloat16),
            jax.ShapeDtypeStruct((n_pre, capacity * PAGE, 2 * HD), jnp.bfloat16),
        ],
        scratch_shapes=[
            pltpu.VMEM((heads, span, 2 * HD), jnp.float32),
            pltpu.VMEM((heads, span, 1), jnp.float32),
        ],
        compiler_params=pltpu.CompilerParams(vmem_limit_bytes=KERNEL_VMEM),
        cost_estimate=pl.CostEstimate(
            flops=4 * heads * span * span * n_pre * HD,
            bytes_accessed=4 * queries.size * 2,
            transcendentals=heads * span * span * n_pre,
        ),
        name="attention",
    )(info, slots, queries, keys, values, start)


PIECES = 8


def chunk_copy(h_ref, chunk, h_buf, sem):
    depth = h_buf.shape[1]
    columns = pl.ds(pl.multiple_of(chunk * depth, depth), depth)
    return pltpu.make_async_copy(h_ref.at[:, columns], h_buf, sem)


def add_pieces(member, chunk, pieces, w_ref, acc_ref):
    share = pieces[0].shape[1]
    half = PIECES // 2
    for side in range(2):

        @pl.when(jnp.bitwise_xor(member // half, side) == lax.rem(chunk, 2))
        def _():
            total = acc_ref[...]
            for j in range(side * half, side * half + half):
                row = lax.rem(jnp.bitwise_xor(member, j), half) * share
                total += jnp.dot(
                    pieces[j][...],
                    w_ref[pl.ds(pl.multiple_of(row, share), share), :],
                    preferred_element_type=jnp.float32,
                )
            acc_ref[...] = total


def near_kernel(place, h_ref, kw_ref, vw_ref, out_ref, h_buf, w_buf, sems):
    copies = [
        chunk_copy(h_ref, place[0], h_buf, sems.at[0]),
        pltpu.make_async_copy(kw_ref, w_buf.at[:, pl.ds(0, HD)], sems.at[1]),
        pltpu.make_async_copy(vw_ref, w_buf.at[:, pl.ds(HD, HD)], sems.at[2]),
    ]
    for copy in copies:
        copy.start()
    for copy in copies:
        copy.wait()
    out_ref[...] = jnp.dot(h_buf[...], w_buf[...], preferred_element_type=jnp.float32)


def partial_kernel(column, place, h_ref, w_ref, before_ref, owner_ref, out_ref, h_buf, sem):
    copy = chunk_copy(h_ref, place[0], h_buf, sem)
    copy.start()
    span = h_buf.shape[0]
    part = slice(column * HD, column * HD + HD)
    if column == 0:
        out_ref[span:] = owner_ref[...]
    copy.wait()
    out_ref[:span] = before_ref[:, part] + jnp.dot(
        h_buf[...], w_ref[...], preferred_element_type=jnp.float32
    )


def facing_kernel(place, h_ref, kw_ref, vw_ref, *refs):
    pieces = refs[:PIECES]
    out_ref, h_buf, w_buf, sem = refs[PIECES:]
    copy = chunk_copy(h_ref, place[0], h_buf, sem)
    copy.start()
    span = h_buf.shape[0]
    w_buf[:, :HD] = kw_ref[...]
    w_buf[:, HD:] = vw_ref[...]
    out_ref[span:] = jnp.zeros((span, 2 * HD), jnp.float32)
    add_pieces(place[2], place[0], pieces, w_buf, out_ref.at[pl.ds(span, span)])
    copy.wait()
    out_ref[:span] = jnp.dot(h_buf[...], w_buf[...], preferred_element_type=jnp.float32)


def distant_kernel(column, place, h_ref, w_ref, near_ref, outer_ref, facing_ref, bias_ref, *refs):
    pieces = refs[:PIECES]
    out_ref, h_buf, acc, sem = refs[PIECES:]
    copy = chunk_copy(h_ref, place[0], h_buf, sem)
    copy.start()
    span = h_buf.shape[0]
    part = slice(column * HD, column * HD + HD)
    own_at = pl.multiple_of(place[1] * span, span)
    outer_at = pl.multiple_of((1 - place[1]) * span, span)
    bias = bias_ref[...].astype(jnp.float32)
    acc[...] = outer_ref[:span] + facing_ref[span:, part] + bias
    add_pieces(place[2], place[0], pieces, w_ref, acc)
    out_ref[pl.ds(outer_at, span), :] = acc[...].astype(jnp.bfloat16)
    own = near_ref[:span] + facing_ref[:span, part] + bias
    copy.wait()
    own += jnp.dot(h_buf[...], w_ref[...], preferred_element_type=jnp.float32)
    out_ref[pl.ds(own_at, span), :] = own.astype(jnp.bfloat16)
    if column == 0:
        mine, theirs = near_ref[span:], outer_ref[span:]
        lower = jnp.where(place[1] == 0, mine, theirs)
        upper = jnp.where(place[1] == 0, theirs, mine)
        out_ref[2 * span :] = jnp.concatenate([lower, upper], axis=0).astype(jnp.bfloat16)


EXTRA = 8
HELD = pl.BlockSpec(memory_space=pltpu.HBM)
FAST = pl.BlockSpec(memory_space=pltpu.VMEM)
SCALAR = pl.BlockSpec(memory_space=pltpu.SMEM)


def in_hbm(x):
    return pltpu.with_memory_space_constraint(x, pltpu.HBM)


def call_project(kernel, name, place, operands, rows, columns, kind, scratch, held=1, copies=()):
    return pl.pallas_call(
        kernel,
        in_specs=[SCALAR] + [HELD] * held + [FAST] * (len(operands) - held),
        out_specs=FAST,
        out_shape=jax.ShapeDtypeStruct((rows, columns), kind),
        scratch_shapes=scratch + [pltpu.SemaphoreType.DMA(copies)],
        compiler_params=pltpu.CompilerParams(vmem_limit_bytes=KERNEL_VMEM),
        cost_estimate=pl.CostEstimate(flops=0, bytes_accessed=0, transcendentals=0),
        name=name,
    )(place, *[in_hbm(x) for x in operands[:held]], *operands[held:])


INWARD = [(0, 1), (3, 2)]
ACROSS = [(1, 2), (2, 1)]
OUTWARD = [(1, 0), (2, 3)]
SWAP = [(0, 1), (1, 0), (2, 3), (3, 2)]


def line_of_four(hidden, key_weight, value_weight, key_bias, value_bias, page_owner):
    index = lax.axis_index("pre")
    member = lax.axis_index(("dec", "tp"))
    span, width = hidden.shape
    depth = key_weight.shape[0]
    share = width // 2 // PIECES
    facing = 3 - index
    near = jnp.bitwise_xor(index, 1)
    distant = jnp.bitwise_xor(facing, 1)
    second = (index < 2).astype(jnp.int32)

    def send(x, pairs):
        return lax.ppermute(x, "pre", pairs)

    def trade(x, apart):
        return lax.ppermute(x, ("dec", "tp"), [(m, m ^ apart) for m in range(PIECES)])

    mine = second * (width // 2) + member * share
    cut = lax.dynamic_slice_in_dim(hidden, mine, share, axis=1)
    tie = lax.optimization_barrier
    block = pltpu.VMEM((span, depth), jnp.bfloat16)
    both = pltpu.VMEM((depth, 2 * HD), jnp.bfloat16)
    key_facing = send(key_weight, ACROSS)
    cut = send(cut, INWARD)
    own_part = call_project(
        near_kernel,
        "near",
        index[None],
        [hidden, key_weight, value_weight],
        span,
        2 * HD,
        jnp.float32,
        [block, both],
        held=3,
        copies=(3,),
    )
    cut, key_facing, key_after, value_after, own_part = tie(
        (cut, key_facing, key_weight, value_weight, own_part)
    )
    value_facing = send(value_after, ACROSS)
    key_swapped = send(key_after, SWAP)
    value_swapped = send(value_after, SWAP)
    chips = [cut, trade(cut, 2), trade(cut, 4), trade(cut, 6)]
    key_swapped, value_facing = tie((key_swapped, value_facing))
    key_distant = send(key_swapped, ACROSS)
    value_distant = send(value_swapped, ACROSS)
    chips[2], key_distant = tie((chips[2], key_distant))
    mates = [trade(x, 1) for x in chips]
    pieces = [x for both_cores in zip(chips, mates) for x in both_cores]

    def place(chunk):
        return jnp.stack([chunk, second, member])

    owners = jnp.broadcast_to(page_owner.T.astype(jnp.float32), (EXTRA, page_owner.shape[0]))
    owners = jnp.pad(owners, ((0, 0), (0, HD - page_owner.shape[0])))

    def begin(column, weight):
        part = call_project(
            functools.partial(partial_kernel, column),
            "partial",
            near[None],
            [hidden, weight, own_part, owners],
            span + (EXTRA if column == 0 else 0),
            HD,
            jnp.float32,
            [block],
        )
        return part, send(part, INWARD)

    def finish(column, weight, parts, bias):
        return call_project(
            functools.partial(distant_kernel, column),
            "distant",
            place(distant),
            [hidden, weight, *parts, faced, bias[None, :]] + pieces,
            2 * span + (2 * EXTRA if column == 0 else 0),
            HD,
            jnp.bfloat16,
            [block, pltpu.VMEM((span, HD), jnp.float32)],
        )

    key_parts = begin(0, key_swapped)
    value_parts = begin(1, value_swapped)
    faced = call_project(
        facing_kernel,
        "facing",
        place(facing),
        [hidden, key_facing, value_facing] + pieces,
        2 * span,
        2 * HD,
        jnp.float32,
        [block, both],
    )
    keys = finish(0, key_distant, key_parts, key_bias)
    keys_out, keys_across = send(keys, OUTWARD), send(keys, ACROSS)
    values = finish(1, value_distant, value_parts, value_bias)
    values_across = send(values, ACROSS)
    keys_out, values_after = tie((keys_out, values))
    values_out = send(values_after, OUTWARD)
    keys_far, values_far = send(keys_across, OUTWARD), send(values_across, OUTWARD)
    return (
        (keys, keys_out, keys_across, keys_far),
        (values, values_out, values_across, values_far),
    )


def head_of(x, g):
    return x[:, g * HD : (g + 1) * HD]


def attend(q_ref, heads, keys, values, allowed, before, store):
    factor = HD**-0.5 * math.log2(math.e)

    def scores_of(g):
        return lax.dot_general(
            head_of(q_ref, g), keys, (((1,), (1,)), ((), ())), preferred_element_type=jnp.float32
        )

    following = scores_of(0)
    for g in range(heads):
        scores = jnp.where(allowed, following, NEG)
        if g + 1 < heads:
            following = scores_of(g + 1)
        peak = jnp.max(scores, axis=1, keepdims=True)
        if before is not None:
            top, total, mix = before(g)
            peak = jnp.maximum(peak, top)
        weights = jnp.exp2(scores * factor - peak * factor).astype(jnp.bfloat16)
        mixed = jnp.dot(weights, values, preferred_element_type=jnp.float32)
        sums, mixed = mixed[:, HD:], mixed[:, :HD]
        if before is not None:
            shrink = jnp.exp2((top - peak) * factor)
            sums = sums + total * shrink
            mixed = mixed + mix * shrink
        store(g, peak, sums, mixed)


def with_ones(values):
    return jnp.concatenate([values, jnp.ones_like(values)], axis=1)


def prompt_starts(seg_ref, first, span):
    seg = seg_ref[...]
    position = (lax.broadcasted_iota(jnp.int32, (span, 1), 0) + first).astype(jnp.float32)
    start = jnp.zeros((span, 1), jnp.float32)
    for v in range(1, PROMPTS):
        lower = jnp.where(seg < v, 1.0, 0.0)
        bound = jnp.sum(jnp.sum(lower, axis=1, keepdims=True), axis=0, keepdims=True)
        start = jnp.where(position >= bound, bound, start)
    return start.astype(jnp.int32)


def read_owners(held_k, span, listed, named, sem):
    listed[...] = held_k[2 * span :].astype(jnp.float32).astype(jnp.int32)
    copy = pltpu.make_async_copy(listed, named, sem)
    copy.start()
    return copy


def place_pages(index, span, named, held_k, held_v, cache_ref, laid):
    rows = cache_ref.shape[1]
    row = lax.broadcasted_iota(jnp.int32, (rows, 2 * HD), 0)
    for s in range(2):
        rank = jnp.int32(0)
        for p in range(span // PAGE):
            tokens = pl.ds(s * span + p * PAGE, PAGE)
            at = pl.ds(pl.multiple_of(rank * PAGE, PAGE), PAGE)
            laid[s, at, :HD] = held_k[tokens, :]
            laid[s, at, HD:] = held_v[tokens, :]
            rank = rank + (named[s * EXTRA, p] == index).astype(jnp.int32)
        cache_ref[s] = jnp.where(row < rank * PAGE, laid[s, :rows], 0)


def own_kernel(
    heads,
    info,
    q_ref,
    seg_ref,
    k_in,
    k_out,
    v_in,
    v_out,
    top,
    total,
    mix,
    cache_ref,
    held_k,
    held_v,
    q_buf,
    listed,
    named,
    laid,
    sems,
):
    copy = pltpu.make_async_copy(q_ref, q_buf, sems.at[0])
    copy.start()
    span = q_buf.shape[0]
    index = info[0]
    inner = (index == 1) | (index == 2)
    held_k[...] = jnp.where(inner, k_in[...], k_out[...])
    held_v[...] = jnp.where(inner, v_in[...], v_out[...])
    owners = read_owners(held_k, span, listed, named, sems.at[1])
    keys = held_k[: 2 * span]
    values = with_ones(held_v[...])
    columns = lax.broadcasted_iota(jnp.int32, (span, 2 * span), 1)
    rows = lax.broadcasted_iota(jnp.int32, (span, 2 * span), 0)
    start = prompt_starts(seg_ref, index * span, span)
    allowed = (columns <= rows + lax.rem(index, 2) * span) & (
        columns >= start - (index // 2) * 2 * span
    )
    copy.wait()

    def store(g, peak, sums, mixed):
        top[g] = peak
        total[g] = sums[:, :1]
        mix[g] = mixed

    attend(q_buf, heads, keys, values, allowed, None, store)
    owners.wait()
    place_pages(index, span, named, held_k, held_v, cache_ref, laid)


def far_kernel(
    heads,
    info,
    q_ref,
    seg_ref,
    k_across,
    k_far,
    v_across,
    v_far,
    top,
    total,
    mix,
    own_cache,
    out_ref,
    cache_ref,
    held_k,
    held_v,
    q_buf,
    listed,
    named,
    laid,
    sems,
):
    copy = pltpu.make_async_copy(q_ref, q_buf, sems.at[0])
    copy.start()
    span = q_buf.shape[0]
    index = info[0]
    inner = (index == 1) | (index == 2)
    held_k[...] = jnp.where(inner, k_across[...], k_far[...])
    held_v[...] = jnp.where(inner, v_across[...], v_far[...])
    cache_ref[pl.ds(index // 2 * 2, 2)] = own_cache[...]
    owners = read_owners(held_k, span, listed, named, sems.at[1])
    copy.wait()

    @pl.when(index < 2)
    def _():
        for g in range(heads):
            out_ref[:, g * HD : (g + 1) * HD] = (mix[g] / total[g]).astype(out_ref.dtype)

    @pl.when(index >= 2)
    def _():
        keys = held_k[: 2 * span]
        values = with_ones(held_v[...])
        columns = lax.broadcasted_iota(jnp.int32, (span, 2 * span), 1)
        allowed = columns >= prompt_starts(seg_ref, index * span, span)

        def store(g, peak, sums, mixed):
            out_ref[:, g * HD : (g + 1) * HD] = (mixed / sums).astype(out_ref.dtype)

        attend(q_buf, heads, keys, values, allowed, lambda g: (top[g], total[g], mix[g]), store)

    owners.wait()
    far_cache = cache_ref.at[pl.ds((1 - index // 2) * 2, 2)]
    place_pages(index, span, named, held_k, held_v, far_cache, laid)


def attention_of_pairs(queries, segment_ids, keys, values, capacity):
    span = queries.shape[0]
    heads = queries.shape[1] // HD
    info = lax.axis_index("pre").astype(jnp.int32)[None]
    segments = segment_ids.reshape(-1, HD)
    scores = heads * span * 2 * span
    cost = pl.CostEstimate(flops=4 * scores * HD, bytes_accessed=8 * scores, transcendentals=scores)
    params = pltpu.CompilerParams(vmem_limit_bytes=KERNEL_VMEM)
    scratch = [
        pltpu.VMEM((2 * span + 2 * EXTRA, HD), jnp.bfloat16),
        pltpu.VMEM((2 * span, HD), jnp.bfloat16),
        pltpu.VMEM(queries.shape, jnp.bfloat16),
        pltpu.VMEM((2 * EXTRA, HD), jnp.int32),
        pltpu.SMEM((2 * EXTRA, HD), jnp.int32),
        pltpu.VMEM((2, (capacity + 1) * PAGE, 2 * HD), jnp.bfloat16),
        pltpu.SemaphoreType.DMA((2,)),
    ]
    state = pl.pallas_call(
        functools.partial(own_kernel, heads),
        in_specs=[SCALAR, HELD] + [FAST] * 5,
        out_specs=[FAST] * 4,
        out_shape=[
            jax.ShapeDtypeStruct((heads, span, 1), jnp.float32),
            jax.ShapeDtypeStruct((heads, span, 1), jnp.float32),
            jax.ShapeDtypeStruct((heads, span, HD), jnp.float32),
            jax.ShapeDtypeStruct((2, capacity * PAGE, 2 * HD), jnp.bfloat16),
        ],
        scratch_shapes=scratch,
        compiler_params=params,
        cost_estimate=cost,
        name="attend_own",
    )(info, in_hbm(queries), segments, *keys[:2], *values[:2])
    return pl.pallas_call(
        functools.partial(far_kernel, heads),
        in_specs=[SCALAR, HELD] + [FAST] * 9,
        out_specs=[FAST] * 2,
        out_shape=[
            jax.ShapeDtypeStruct(queries.shape, jnp.bfloat16),
            jax.ShapeDtypeStruct((4, capacity * PAGE, 2 * HD), jnp.bfloat16),
        ],
        scratch_shapes=scratch,
        compiler_params=params,
        cost_estimate=cost,
        name="attend_far",
    )(info, in_hbm(queries), segments, *keys[2:], *values[2:], *state)


def gathered(hidden, key_weight, value_weight, key_bias, value_bias):
    joined = jnp.concatenate([key_weight, value_weight], axis=1)
    joined = lax.all_gather(joined, "pre", axis=0, tiled=True)
    bias = jnp.concatenate([key_bias, value_bias]).astype(jnp.float32)
    local = jnp.dot(hidden, joined, preferred_element_type=jnp.float32) + bias
    both = lax.all_gather(local.astype(jnp.bfloat16), "pre", axis=0, tiled=True)
    return both[:, :HD], both[:, HD:]


def body(hidden, queries, key_weight, value_weight, key_bias, value_bias, segment_ids, page_owner):
    n_pre = lax.axis_size("pre")
    index = lax.axis_index("pre")
    span = hidden.shape[0]
    pages_dev = span // PAGE
    capacity = 2 * pages_dev // n_pre
    assert key_weight.shape[1] == HD
    arrays = (hidden, key_weight, value_weight, key_bias, value_bias)
    if n_pre == 4:
        keys, values = line_of_four(*arrays, page_owner)
        mixed, cache = attention_of_pairs(queries, segment_ids, keys, values, capacity)
        return (mixed, cache[None])

    own_segments = lax.dynamic_slice_in_dim(segment_ids, index * span, span)
    start = jnp.sum(
        (segment_ids[None, :] < own_segments[:, None]).astype(jnp.int32), axis=1, keepdims=True
    )
    info = jnp.stack([index, start[0, 0] // span]).astype(jnp.int32)
    owners = lax.all_gather(page_owner[:, 0], "pre")
    keys, values = gathered(*arrays)
    mine = (owners == index).astype(jnp.int32)
    rank = jnp.cumsum(mine, axis=1) - mine
    numbers = jnp.arange(n_pre * pages_dev, dtype=jnp.int32).reshape(n_pre, 1, pages_dev)
    wanted = (mine[:, None, :] == 1) & (
        rank[:, None, :] == jnp.arange(capacity, dtype=jnp.int32)[None, :, None]
    )
    slots = jnp.max(jnp.where(wanted, numbers, -1), axis=2).reshape(-1)
    mixed, cache = attention(info, slots, queries, keys, values, start, n_pre, capacity)
    return (mixed, cache[None])


def solution(mesh):
    return jax.shard_map(
        body,
        mesh=mesh,
        in_specs=(
            P(("group", "pre"), None),
            P(("group", "pre"), ("dec", "tp")),
            P("pre", ("dec", "tp")),
            P("pre", ("dec", "tp")),
            P(("dec", "tp")),
            P(("dec", "tp")),
            P("group"),
            P(("group", "pre"), None),
        ),
        out_specs=(
            P(("group", "pre"), ("dec", "tp")),
            P(("group", "pre"), None, None, ("dec", "tp")),
        ),
        check_vma=False,
    )
```

```python
import functools
import math

import jax
import jax.numpy as jnp
from jax import lax
from jax.experimental import pallas as pl
from jax.experimental.pallas import tpu as pltpu
from jax.sharding import PartitionSpec as P

HD = 128
PAGE = 16
NEG = -1e30
KERNEL_VMEM = 16 * 1024 * 1024
PROMPTS = 4


def attention_kernel(heads, span, info, slots, q_ref, k_ref, v_ref, start_ref, out_ref, cache_ref, acc, top):
    index = info[0]
    first = info[1]
    factor = HD**-0.5 * math.log2(math.e)
    columns = lax.broadcasted_iota(jnp.int32, (span, span), 1)
    rows = lax.broadcasted_iota(jnp.int32, (span, span), 0)

    def block(j, diagonal):
        at = pl.multiple_of(j * span, span)
        keys = k_ref[pl.ds(at, span), :]
        values = jnp.concatenate(
            [v_ref[pl.ds(at, span), :], jnp.ones((span, HD), jnp.bfloat16)], axis=1
        )
        allowed = columns >= start_ref[...] - at
        if diagonal:
            allowed = allowed & (columns <= rows)
        for g in range(heads):
            scores = lax.dot_general(
                q_ref[:, g * HD : (g + 1) * HD],
                keys,
                (((1,), (1,)), ((), ())),
                preferred_element_type=jnp.float32,
            )
            scores = jnp.where(allowed, scores, NEG)
            peak = jnp.max(scores, axis=1, keepdims=True)
            if not diagonal:
                before = top[g]
                peak = jnp.maximum(peak, before)
            weights = jnp.exp2(scores * factor - peak * factor).astype(jnp.bfloat16)
            mixed = jnp.dot(weights, values, preferred_element_type=jnp.float32)
            if not diagonal:
                mixed = mixed + acc[g] * jnp.exp2((before - peak) * factor)
            top[g] = peak
            acc[g] = mixed

    block(index, True)

    @pl.loop(first, index)
    def _(j):
        block(j, False)

    for g in range(heads):
        mixed = acc[g]
        out_ref[:, g * HD : (g + 1) * HD] = (mixed[:, :HD] / mixed[:, HD:]).astype(out_ref.dtype)

    capacity = cache_ref.shape[1] // PAGE
    empty = jnp.zeros((PAGE, HD), cache_ref.dtype)
    for s in range(cache_ref.shape[0]):

        @pl.loop(0, capacity)
        def _(r):
            page = slots[s * capacity + r]
            token = pl.ds(pl.multiple_of(jnp.maximum(page, 0) * PAGE, PAGE), PAGE)
            row = pl.ds(pl.multiple_of(r * PAGE, PAGE), PAGE)
            cache_ref[s, row, :HD] = jnp.where(page >= 0, k_ref[token, :], empty)
            cache_ref[s, row, HD:] = jnp.where(page >= 0, v_ref[token, :], empty)


def attention(info, slots, queries, keys, values, start, n_pre, capacity):
    span = queries.shape[0]
    heads = queries.shape[1] // HD
    return pl.pallas_call(
        functools.partial(attention_kernel, heads, span),
        in_specs=[
            pl.BlockSpec(memory_space=pltpu.SMEM),
            pl.BlockSpec(memory_space=pltpu.SMEM),
            pl.BlockSpec(memory_space=pltpu.VMEM),
            pl.BlockSpec(memory_space=pltpu.VMEM),
            pl.BlockSpec(memory_space=pltpu.VMEM),
            pl.BlockSpec(memory_space=pltpu.VMEM),
        ],
        out_specs=[
            pl.BlockSpec(memory_space=pltpu.VMEM),
            pl.BlockSpec(memory_space=pltpu.VMEM),
        ],
        out_shape=[
            jax.ShapeDtypeStruct(queries.shape, jnp.bfloat16),
            jax.ShapeDtypeStruct((n_pre, capacity * PAGE, 2 * HD), jnp.bfloat16),
        ],
        scratch_shapes=[
            pltpu.VMEM((heads, span, 2 * HD), jnp.float32),
            pltpu.VMEM((heads, span, 1), jnp.float32),
        ],
        compiler_params=pltpu.CompilerParams(vmem_limit_bytes=KERNEL_VMEM),
        cost_estimate=pl.CostEstimate(
            flops=4 * heads * span * span * n_pre * HD,
            bytes_accessed=4 * queries.size * 2,
            transcendentals=heads * span * span * n_pre,
        ),
        name="attention",
    )(info, slots, queries, keys, values, start)


PIECES = 8
PARTS = 4


def add_pieces(member, chunk, pieces, w_ref, acc_ref):
    share = pieces[0].shape[1]
    half = PIECES // 2
    for side in range(2):

        @pl.when(jnp.bitwise_xor(member // half, side) == lax.rem(chunk, 2))
        def _():
            total = acc_ref[...]
            for j in range(side * half, side * half + half):
                row = lax.rem(jnp.bitwise_xor(member, j), half) * share
                total += jnp.dot(
                    pieces[j][...],
                    w_ref[pl.ds(pl.multiple_of(row, share), share), :],
                    preferred_element_type=jnp.float32,
                )
            acc_ref[...] = total


def chunk_copies(h_ref, chunk, h_buf, sems):
    depth = h_buf.shape[1]
    part = depth // PARTS
    copies = []
    for t in range(PARTS):
        columns = pl.ds(pl.multiple_of(chunk * depth + t * part, part), part)
        to = h_buf.at[:, pl.ds(t * part, part)]
        copies.append(pltpu.make_async_copy(h_ref.at[:, columns], to, sems.at[t]))
        copies[t].start()
    return copies


def chunk_product(copies, h_buf, w_ref):
    part = h_buf.shape[1] // PARTS
    total = None
    for t, copy in enumerate(copies):
        copy.wait()
        at = slice(t * part, t * part + part)
        product = jnp.dot(h_buf[:, at], w_ref[at, :], preferred_element_type=jnp.float32)
        total = product if total is None else total + product
    return total


def weight_copies(kw_ref, vw_ref, w_buf, sems):
    copies = [
        pltpu.make_async_copy(kw_ref, w_buf.at[:, pl.ds(0, HD)], sems.at[PARTS]),
        pltpu.make_async_copy(vw_ref, w_buf.at[:, pl.ds(HD, HD)], sems.at[PARTS + 1]),
    ]
    for copy in copies:
        copy.start()
    return copies


def near_kernel(place, h_ref, kw_ref, vw_ref, out_ref, h_buf, w_buf, sems):
    weights = weight_copies(kw_ref, vw_ref, w_buf, sems)
    copies = chunk_copies(h_ref, place[0], h_buf, sems)
    for copy in weights:
        copy.wait()
    out_ref[...] = chunk_product(copies, h_buf, w_buf)


def partial_kernel(column, place, h_ref, w_ref, before_ref, owner_ref, out_ref, h_buf, sems):
    copies = chunk_copies(h_ref, place[0], h_buf, sems)
    span = h_buf.shape[0]
    part = slice(column * HD, column * HD + HD)
    if column == 0:
        out_ref[span:] = owner_ref[...]
    out_ref[:span] = before_ref[:, part] + chunk_product(copies, h_buf, w_ref)


def facing_kernel(place, h_ref, kw_ref, vw_ref, *refs):
    pieces = refs[:PIECES]
    out_ref, h_buf, w_buf, sems = refs[PIECES:]
    span = h_buf.shape[0]

    @pl.when(place[3] == 1)
    def _():
        weights = weight_copies(kw_ref, vw_ref, w_buf, sems)
        copies = chunk_copies(h_ref, place[0], h_buf, sems)
        for copy in weights:
            copy.wait()
        out_ref[span:] = jnp.zeros((span, 2 * HD), jnp.float32)
        add_pieces(place[2], place[0], pieces, w_buf, out_ref.at[pl.ds(span, span)])
        out_ref[:span] = chunk_product(copies, h_buf, w_buf)


def distant_kernel(column, place, h_ref, w_ref, near_ref, outer_ref, facing_ref, bias_ref, *refs):
    pieces = refs[:PIECES]
    out_ref, h_buf, acc, sems = refs[PIECES:]
    span = h_buf.shape[0]
    part = slice(column * HD, column * HD + HD)

    @pl.when(place[3] == 1)
    def _():
        copies = chunk_copies(h_ref, place[0], h_buf, sems)
        own_at = pl.multiple_of(place[1] * span, span)
        outer_at = pl.multiple_of((1 - place[1]) * span, span)
        bias = bias_ref[...].astype(jnp.float32)
        acc[...] = outer_ref[:span] + facing_ref[span:, part] + bias
        add_pieces(place[2], place[0], pieces, w_ref, acc)
        out_ref[pl.ds(outer_at, span), :] = acc[...].astype(jnp.bfloat16)
        own = near_ref[:span] + facing_ref[:span, part] + bias
        own += chunk_product(copies, h_buf, w_ref)
        out_ref[pl.ds(own_at, span), :] = own.astype(jnp.bfloat16)
        if column == 0:
            mine, theirs = near_ref[span:], outer_ref[span:]
            lower = jnp.where(place[1] == 0, mine, theirs)
            upper = jnp.where(place[1] == 0, theirs, mine)
            out_ref[2 * span :] = jnp.concatenate([lower, upper], axis=0).astype(jnp.bfloat16)


EXTRA = 8
HELD = pl.BlockSpec(memory_space=pltpu.HBM)
FAST = pl.BlockSpec(memory_space=pltpu.VMEM)
SCALAR = pl.BlockSpec(memory_space=pltpu.SMEM)


def in_hbm(x):
    return pltpu.with_memory_space_constraint(x, pltpu.HBM)


def call_project(kernel, name, operands, in_specs, shapes, scratch=()):
    many = isinstance(shapes, list)
    return pl.pallas_call(
        kernel,
        in_specs=in_specs,
        out_specs=[FAST] * len(shapes) if many else FAST,
        out_shape=shapes,
        scratch_shapes=list(scratch),
        compiler_params=pltpu.CompilerParams(vmem_limit_bytes=KERNEL_VMEM),
        cost_estimate=pl.CostEstimate(flops=0, bytes_accessed=0, transcendentals=0),
        name=name,
    )(*operands)


INWARD = [(0, 1), (3, 2)]
ACROSS = [(1, 2), (2, 1)]
OUTWARD = [(1, 0), (2, 3)]
SWAP = [(0, 1), (1, 0), (2, 3), (3, 2)]


def line_of_four(hidden, key_weight, value_weight, key_bias, value_bias, page_owner):
    index = lax.axis_index("pre")
    member = lax.axis_index(("dec", "tp"))
    span, width = hidden.shape
    depth = key_weight.shape[0]
    share = width // 2 // PIECES
    facing = 3 - index
    near = jnp.bitwise_xor(index, 1)
    distant = jnp.bitwise_xor(facing, 1)
    second = (index < 2).astype(jnp.int32)
    inner = ((index == 1) | (index == 2)).astype(jnp.int32)
    tie = lax.optimization_barrier

    def send(x, pairs):
        return lax.ppermute(x, "pre", pairs)

    def trade(x, apart):
        pairs = [(p * PIECES + m, p * PIECES + (m ^ apart)) for p in (1, 2) for m in range(PIECES)]
        return lax.ppermute(x, ("pre", "dec", "tp"), pairs)

    def place(chunk):
        return jnp.stack([chunk, second, member, inner])

    def f32(rows, columns):
        return jax.ShapeDtypeStruct((rows, columns), jnp.float32)

    def bf16(rows, columns):
        return jax.ShapeDtypeStruct((rows, columns), jnp.bfloat16)

    mine = second * (width // 2) + member * share
    cut = lax.dynamic_slice_in_dim(hidden, mine, share, axis=1)
    both = pltpu.VMEM((depth, 2 * HD), jnp.bfloat16)
    key_facing = send(key_weight, ACROSS)
    cut = send(cut, INWARD)
    block = [pltpu.VMEM((span, depth), jnp.bfloat16)]
    parts = [pltpu.SemaphoreType.DMA((PARTS,))]
    held = in_hbm(hidden)
    own_part = call_project(
        near_kernel,
        "near",
        [index[None], held, in_hbm(key_weight), in_hbm(value_weight)],
        [SCALAR] + [HELD] * 3,
        f32(span, 2 * HD),
        block + [both, pltpu.SemaphoreType.DMA((PARTS + 2,))],
    )
    cut, key_facing, key_after, value_after, own_part = tie(
        (cut, key_facing, key_weight, value_weight, own_part)
    )
    value_facing = send(value_after, ACROSS)
    key_swapped = send(key_after, SWAP)
    value_swapped = send(value_after, SWAP)
    chips = [cut, trade(cut, 2), trade(cut, 4), trade(cut, 6)]
    key_swapped, value_facing = tie((key_swapped, value_facing))
    key_distant = send(key_swapped, ACROSS)
    owners = jnp.broadcast_to(page_owner.T.astype(jnp.float32), (EXTRA, page_owner.shape[0]))
    owners = jnp.pad(owners, ((0, 0), (0, HD - page_owner.shape[0])))

    def begin(column, weight):
        return call_project(
            functools.partial(partial_kernel, column),
            "partial",
            [near[None], held, weight, own_part, owners],
            [SCALAR, HELD] + [FAST] * 3,
            f32(span + (EXTRA if column == 0 else 0), HD),
            block + parts,
        )

    key_part = begin(0, key_swapped)
    key_part, value_swapped = tie((key_part, value_swapped))
    value_distant = send(value_swapped, ACROSS)
    value_part = begin(1, value_swapped)
    key_outer, value_outer = send(key_part, INWARD), send(value_part, INWARD)
    chips[2], key_distant = tie((chips[2], key_distant))
    mates = [trade(x, 1) for x in chips]
    pieces = [x for both_cores in zip(chips, mates) for x in both_cores]
    faced = call_project(
        facing_kernel,
        "facing",
        [place(facing), held, in_hbm(key_facing), in_hbm(value_facing)] + pieces,
        [SCALAR] + [HELD] * 3 + [FAST] * PIECES,
        f32(2 * span, 2 * HD),
        block + [both, pltpu.SemaphoreType.DMA((PARTS + 2,))],
    )

    def finish(column, weight, part, outer, bias):
        return call_project(
            functools.partial(distant_kernel, column),
            "distant",
            [place(distant), held, weight, part, outer, faced, bias[None, :]] + pieces,
            [SCALAR, HELD] + [FAST] * (5 + PIECES),
            bf16(2 * span + (2 * EXTRA if column == 0 else 0), HD),
            block + [pltpu.VMEM((span, HD), jnp.float32)] + parts,
        )

    keys = finish(0, key_distant, key_part, key_outer, key_bias)
    keys_out, keys_across = send(keys, OUTWARD), send(keys, ACROSS)
    values = finish(1, value_distant, value_part, value_outer, value_bias)
    values_across = send(values, ACROSS)
    keys_out, values_after = tie((keys_out, values))
    values_out = send(values_after, OUTWARD)
    keys_far, values_far = send(keys_across, OUTWARD), send(values_across, OUTWARD)
    return (
        (keys, keys_out, keys_across, keys_far),
        (values, values_out, values_across, values_far),
    )


def head_of(x, g):
    return x[:, g * HD : (g + 1) * HD]


def attend(q_ref, heads, keys, values, allowed, before, store):
    factor = HD**-0.5 * math.log2(math.e)

    def scores_of(g):
        return lax.dot_general(
            head_of(q_ref, g), keys, (((1,), (1,)), ((), ())), preferred_element_type=jnp.float32
        )

    following = scores_of(0)
    for g in range(heads):
        scores = jnp.where(allowed, following, NEG)
        if g + 1 < heads:
            following = scores_of(g + 1)
        peak = jnp.max(scores, axis=1, keepdims=True)
        if before is not None:
            top, total, mix = before(g)
            peak = jnp.maximum(peak, top)
        weights = jnp.exp2(scores * factor - peak * factor).astype(jnp.bfloat16)
        mixed = jnp.dot(weights, values, preferred_element_type=jnp.float32)
        sums, mixed = mixed[:, HD:], mixed[:, :HD]
        if before is not None:
            shrink = jnp.exp2((top - peak) * factor)
            sums = sums + total * shrink
            mixed = mixed + mix * shrink
        store(g, peak, sums, mixed)


def with_ones(values):
    return jnp.concatenate([values, jnp.ones_like(values)], axis=1)


def prompt_starts(seg_ref, first, span):
    seg = seg_ref[...]
    position = (lax.broadcasted_iota(jnp.int32, (span, 1), 0) + first).astype(jnp.float32)
    start = jnp.zeros((span, 1), jnp.float32)
    for v in range(1, PROMPTS):
        lower = jnp.where(seg < v, 1.0, 0.0)
        bound = jnp.sum(jnp.sum(lower, axis=1, keepdims=True), axis=0, keepdims=True)
        start = jnp.where(position >= bound, bound, start)
    return start.astype(jnp.int32)


def read_owners(held_k, span, listed, named, sem):
    listed[...] = held_k[2 * span :].astype(jnp.float32).astype(jnp.int32)
    copy = pltpu.make_async_copy(listed, named, sem)
    copy.start()
    return copy


def place_pages(index, span, named, held_k, held_v, cache_ref, laid):
    rows = cache_ref.shape[1]
    row = lax.broadcasted_iota(jnp.int32, (rows, 2 * HD), 0)
    for s in range(2):
        rank = jnp.int32(0)
        for p in range(span // PAGE):
            tokens = pl.ds(s * span + p * PAGE, PAGE)
            at = pl.ds(pl.multiple_of(rank * PAGE, PAGE), PAGE)
            laid[s, at, :HD] = held_k[tokens, :]
            laid[s, at, HD:] = held_v[tokens, :]
            rank = rank + (named[s * EXTRA, p] == index).astype(jnp.int32)
        cache_ref[s] = jnp.where(row < rank * PAGE, laid[s, :rows], 0)


def own_kernel(
    heads,
    info,
    q_ref,
    seg_ref,
    k_in,
    k_out,
    v_in,
    v_out,
    top,
    total,
    mix,
    cache_ref,
    held_k,
    held_v,
    q_buf,
    listed,
    named,
    laid,
    sems,
):
    copy = pltpu.make_async_copy(q_ref, q_buf, sems.at[0])
    copy.start()
    span = q_buf.shape[0]
    index = info[0]
    inner = (index == 1) | (index == 2)
    held_k[...] = jnp.where(inner, k_in[...], k_out[...])
    held_v[...] = jnp.where(inner, v_in[...], v_out[...])
    owners = read_owners(held_k, span, listed, named, sems.at[1])
    keys = held_k[: 2 * span]
    values = with_ones(held_v[...])
    columns = lax.broadcasted_iota(jnp.int32, (span, 2 * span), 1)
    rows = lax.broadcasted_iota(jnp.int32, (span, 2 * span), 0)
    start = prompt_starts(seg_ref, index * span, span)
    allowed = (columns <= rows + lax.rem(index, 2) * span) & (
        columns >= start - (index // 2) * 2 * span
    )
    copy.wait()

    def store(g, peak, sums, mixed):
        top[g] = peak
        total[g] = sums[:, :1]
        mix[g] = mixed

    attend(q_buf, heads, keys, values, allowed, None, store)
    owners.wait()
    place_pages(index, span, named, held_k, held_v, cache_ref, laid)


def far_kernel(
    heads,
    info,
    q_ref,
    seg_ref,
    k_across,
    k_far,
    v_across,
    v_far,
    top,
    total,
    mix,
    own_cache,
    out_ref,
    cache_ref,
    held_k,
    held_v,
    q_buf,
    listed,
    named,
    laid,
    sems,
    out_buf,
    far_cache,
):
    copy = pltpu.make_async_copy(q_ref, q_buf, sems.at[0])
    copy.start()
    span = q_buf.shape[0]
    index = info[0]
    inner = (index == 1) | (index == 2)
    held_k[...] = jnp.where(inner, k_across[...], k_far[...])
    held_v[...] = jnp.where(inner, v_across[...], v_far[...])
    owners = read_owners(held_k, span, listed, named, sems.at[1])
    own_at, far_at = index // 2 * 2, (1 - index // 2) * 2
    leaving = [pltpu.make_async_copy(own_cache, cache_ref.at[pl.ds(own_at, 2)], sems.at[2])]
    leaving[0].start()
    copy.wait()

    def leave(g):
        columns = pl.ds(g * HD, HD)
        return pltpu.make_async_copy(out_buf.at[:, columns], out_ref.at[:, columns], sems.at[4 + g])

    def place_far():
        owners.wait()
        place_pages(index, span, named, held_k, held_v, far_cache, laid)
        return pltpu.make_async_copy(far_cache, cache_ref.at[pl.ds(far_at, 2)], sems.at[3])

    @pl.when(index < 2)
    def _():
        for g in range(heads):
            out_buf[:, g * HD : (g + 1) * HD] = (mix[g] / total[g]).astype(out_buf.dtype)
            leave(g).start()
        place_far().start()

    @pl.when(index >= 2)
    def _():
        keys = held_k[: 2 * span]
        values = with_ones(held_v[...])
        columns = lax.broadcasted_iota(jnp.int32, (span, 2 * span), 1)
        allowed = columns >= prompt_starts(seg_ref, index * span, span)

        def store(g, peak, sums, mixed):
            out_buf[:, g * HD : (g + 1) * HD] = (mixed / sums).astype(out_buf.dtype)
            leave(g).start()
            if g == heads // 2:
                place_far().start()

        attend(q_buf, heads, keys, values, allowed, lambda g: (top[g], total[g], mix[g]), store)

    for g in range(heads):
        leave(g).wait()
    leaving[0].wait()
    pltpu.make_async_copy(far_cache, cache_ref.at[pl.ds(far_at, 2)], sems.at[3]).wait()


def attention_of_pairs(queries, segment_ids, keys, values, capacity):
    span = queries.shape[0]
    heads = queries.shape[1] // HD
    info = lax.axis_index("pre").astype(jnp.int32)[None]
    segments = segment_ids.reshape(-1, HD)
    scores = heads * span * 2 * span
    cost = pl.CostEstimate(flops=4 * scores * HD, bytes_accessed=8 * scores, transcendentals=scores)
    params = pltpu.CompilerParams(vmem_limit_bytes=KERNEL_VMEM)
    scratch = [
        pltpu.VMEM((2 * span + 2 * EXTRA, HD), jnp.bfloat16),
        pltpu.VMEM((2 * span, HD), jnp.bfloat16),
        pltpu.VMEM(queries.shape, jnp.bfloat16),
        pltpu.VMEM((2 * EXTRA, HD), jnp.int32),
        pltpu.SMEM((2 * EXTRA, HD), jnp.int32),
        pltpu.VMEM((2, (capacity + 1) * PAGE, 2 * HD), jnp.bfloat16),
        pltpu.SemaphoreType.DMA((4 + heads,)),
    ]
    state = pl.pallas_call(
        functools.partial(own_kernel, heads),
        in_specs=[SCALAR, HELD] + [FAST] * 5,
        out_specs=[FAST] * 4,
        out_shape=[
            jax.ShapeDtypeStruct((heads, span, 1), jnp.float32),
            jax.ShapeDtypeStruct((heads, span, 1), jnp.float32),
            jax.ShapeDtypeStruct((heads, span, HD), jnp.float32),
            jax.ShapeDtypeStruct((2, capacity * PAGE, 2 * HD), jnp.bfloat16),
        ],
        scratch_shapes=scratch,
        compiler_params=params,
        cost_estimate=cost,
        name="attend_own",
    )(info, in_hbm(queries), segments, *keys[:2], *values[:2])
    return pl.pallas_call(
        functools.partial(far_kernel, heads),
        in_specs=[SCALAR, HELD] + [FAST] * 9,
        out_specs=[HELD] * 2,
        out_shape=[
            jax.ShapeDtypeStruct(queries.shape, jnp.bfloat16),
            jax.ShapeDtypeStruct((4, capacity * PAGE, 2 * HD), jnp.bfloat16),
        ],
        scratch_shapes=scratch
        + [
            pltpu.VMEM(queries.shape, jnp.bfloat16),
            pltpu.VMEM((2, capacity * PAGE, 2 * HD), jnp.bfloat16),
        ],
        compiler_params=params,
        cost_estimate=cost,
        name="attend_far",
    )(info, in_hbm(queries), segments, *keys[2:], *values[2:], *state)


def gathered(hidden, key_weight, value_weight, key_bias, value_bias):
    joined = jnp.concatenate([key_weight, value_weight], axis=1)
    joined = lax.all_gather(joined, "pre", axis=0, tiled=True)
    bias = jnp.concatenate([key_bias, value_bias]).astype(jnp.float32)
    local = jnp.dot(hidden, joined, preferred_element_type=jnp.float32) + bias
    both = lax.all_gather(local.astype(jnp.bfloat16), "pre", axis=0, tiled=True)
    return both[:, :HD], both[:, HD:]


def body(hidden, queries, key_weight, value_weight, key_bias, value_bias, segment_ids, page_owner):
    n_pre = lax.axis_size("pre")
    index = lax.axis_index("pre")
    span = hidden.shape[0]
    pages_dev = span // PAGE
    capacity = 2 * pages_dev // n_pre
    assert key_weight.shape[1] == HD
    arrays = (hidden, key_weight, value_weight, key_bias, value_bias)
    if n_pre == 4:
        keys, values = line_of_four(*arrays, page_owner)
        mixed, cache = attention_of_pairs(queries, segment_ids, keys, values, capacity)
        return (mixed, cache[None])

    own_segments = lax.dynamic_slice_in_dim(segment_ids, index * span, span)
    start = jnp.sum(
        (segment_ids[None, :] < own_segments[:, None]).astype(jnp.int32), axis=1, keepdims=True
    )
    info = jnp.stack([index, start[0, 0] // span]).astype(jnp.int32)
    owners = lax.all_gather(page_owner[:, 0], "pre")
    keys, values = gathered(*arrays)
    mine = (owners == index).astype(jnp.int32)
    rank = jnp.cumsum(mine, axis=1) - mine
    numbers = jnp.arange(n_pre * pages_dev, dtype=jnp.int32).reshape(n_pre, 1, pages_dev)
    wanted = (mine[:, None, :] == 1) & (
        rank[:, None, :] == jnp.arange(capacity, dtype=jnp.int32)[None, :, None]
    )
    slots = jnp.max(jnp.where(wanted, numbers, -1), axis=2).reshape(-1)
    mixed, cache = attention(info, slots, queries, keys, values, start, n_pre, capacity)
    return (mixed, cache[None])


def solution(mesh):
    return jax.shard_map(
        body,
        mesh=mesh,
        in_specs=(
            P(("group", "pre"), None),
            P(("group", "pre"), ("dec", "tp")),
            P("pre", ("dec", "tp")),
            P("pre", ("dec", "tp")),
            P(("dec", "tp")),
            P(("dec", "tp")),
            P("group"),
            P(("group", "pre"), None),
        ),
        out_specs=(
            P(("group", "pre"), ("dec", "tp")),
            P(("group", "pre"), None, None, ("dec", "tp")),
        ),
        check_vma=False,
    )
```

```python
import functools
import math

import jax
import jax.numpy as jnp
from jax import lax
from jax.experimental import pallas as pl
from jax.experimental.pallas import tpu as pltpu
from jax.sharding import PartitionSpec as P

HD = 128
PAGE = 16
NEG = -1e30
KERNEL_VMEM = 16 * 1024 * 1024
PROMPTS = 4


def attention_kernel(heads, span, info, slots, q_ref, k_ref, v_ref, start_ref, out_ref, cache_ref, acc, top):
    index = info[0]
    first = info[1]
    factor = HD**-0.5 * math.log2(math.e)
    columns = lax.broadcasted_iota(jnp.int32, (span, span), 1)
    rows = lax.broadcasted_iota(jnp.int32, (span, span), 0)

    def block(j, diagonal):
        at = pl.multiple_of(j * span, span)
        keys = k_ref[pl.ds(at, span), :]
        values = jnp.concatenate(
            [v_ref[pl.ds(at, span), :], jnp.ones((span, HD), jnp.bfloat16)], axis=1
        )
        allowed = columns >= start_ref[...] - at
        if diagonal:
            allowed = allowed & (columns <= rows)
        for g in range(heads):
            scores = lax.dot_general(
                q_ref[:, g * HD : (g + 1) * HD],
                keys,
                (((1,), (1,)), ((), ())),
                preferred_element_type=jnp.float32,
            )
            scores = jnp.where(allowed, scores, NEG)
            peak = jnp.max(scores, axis=1, keepdims=True)
            if not diagonal:
                before = top[g]
                peak = jnp.maximum(peak, before)
            weights = jnp.exp2(scores * factor - peak * factor).astype(jnp.bfloat16)
            mixed = jnp.dot(weights, values, preferred_element_type=jnp.float32)
            if not diagonal:
                mixed = mixed + acc[g] * jnp.exp2((before - peak) * factor)
            top[g] = peak
            acc[g] = mixed

    block(index, True)

    @pl.loop(first, index)
    def _(j):
        block(j, False)

    for g in range(heads):
        mixed = acc[g]
        out_ref[:, g * HD : (g + 1) * HD] = (mixed[:, :HD] / mixed[:, HD:]).astype(out_ref.dtype)

    capacity = cache_ref.shape[1] // PAGE
    empty = jnp.zeros((PAGE, HD), cache_ref.dtype)
    for s in range(cache_ref.shape[0]):

        @pl.loop(0, capacity)
        def _(r):
            page = slots[s * capacity + r]
            token = pl.ds(pl.multiple_of(jnp.maximum(page, 0) * PAGE, PAGE), PAGE)
            row = pl.ds(pl.multiple_of(r * PAGE, PAGE), PAGE)
            cache_ref[s, row, :HD] = jnp.where(page >= 0, k_ref[token, :], empty)
            cache_ref[s, row, HD:] = jnp.where(page >= 0, v_ref[token, :], empty)


def attention(info, slots, queries, keys, values, start, n_pre, capacity):
    span = queries.shape[0]
    heads = queries.shape[1] // HD
    return pl.pallas_call(
        functools.partial(attention_kernel, heads, span),
        in_specs=[
            pl.BlockSpec(memory_space=pltpu.SMEM),
            pl.BlockSpec(memory_space=pltpu.SMEM),
            pl.BlockSpec(memory_space=pltpu.VMEM),
            pl.BlockSpec(memory_space=pltpu.VMEM),
            pl.BlockSpec(memory_space=pltpu.VMEM),
            pl.BlockSpec(memory_space=pltpu.VMEM),
        ],
        out_specs=[
            pl.BlockSpec(memory_space=pltpu.VMEM),
            pl.BlockSpec(memory_space=pltpu.VMEM),
        ],
        out_shape=[
            jax.ShapeDtypeStruct(queries.shape, jnp.bfloat16),
            jax.ShapeDtypeStruct((n_pre, capacity * PAGE, 2 * HD), jnp.bfloat16),
        ],
        scratch_shapes=[
            pltpu.VMEM((heads, span, 2 * HD), jnp.float32),
            pltpu.VMEM((heads, span, 1), jnp.float32),
        ],
        compiler_params=pltpu.CompilerParams(vmem_limit_bytes=KERNEL_VMEM),
        cost_estimate=pl.CostEstimate(
            flops=4 * heads * span * span * n_pre * HD,
            bytes_accessed=4 * queries.size * 2,
            transcendentals=heads * span * span * n_pre,
        ),
        name="attention",
    )(info, slots, queries, keys, values, start)


PIECES = 8


def chunk_copy(h_ref, chunk, h_buf, sem):
    depth = h_buf.shape[1]
    columns = pl.ds(pl.multiple_of(chunk * depth, depth), depth)
    return pltpu.make_async_copy(h_ref.at[:, columns], h_buf, sem)


def add_pieces(member, chunk, pieces, w_ref, acc_ref):
    share = pieces[0].shape[1]
    half = PIECES // 2
    for side in range(2):

        @pl.when(jnp.bitwise_xor(member // half, side) == lax.rem(chunk, 2))
        def _():
            total = acc_ref[...]
            for j in range(side * half, side * half + half):
                row = lax.rem(jnp.bitwise_xor(member, j), half) * share
                total += jnp.dot(
                    pieces[j][...],
                    w_ref[pl.ds(pl.multiple_of(row, share), share), :],
                    preferred_element_type=jnp.float32,
                )
            acc_ref[...] = total


def near_kernel(place, h_ref, kw_ref, vw_ref, out_ref, h_buf, w_buf, sems):
    copies = [
        chunk_copy(h_ref, place[0], h_buf, sems.at[0]),
        pltpu.make_async_copy(kw_ref, w_buf.at[:, pl.ds(0, HD)], sems.at[1]),
        pltpu.make_async_copy(vw_ref, w_buf.at[:, pl.ds(HD, HD)], sems.at[2]),
    ]
    for copy in copies:
        copy.start()
    for copy in copies:
        copy.wait()
    out_ref[...] = jnp.dot(h_buf[...], w_buf[...], preferred_element_type=jnp.float32)


def partial_kernel(column, place, h_ref, w_ref, before_ref, owner_ref, out_ref, h_buf, sem):
    copy = chunk_copy(h_ref, place[0], h_buf, sem)
    copy.start()
    span = h_buf.shape[0]
    part = slice(column * HD, column * HD + HD)
    if column == 0:
        out_ref[span:] = owner_ref[...]
    copy.wait()
    out_ref[:span] = before_ref[:, part] + jnp.dot(
        h_buf[...], w_ref[...], preferred_element_type=jnp.float32
    )


def facing_kernel(place, h_ref, kw_ref, vw_ref, *refs):
    pieces = refs[:PIECES]
    out_ref, h_buf, w_buf, sems = refs[PIECES:]
    span = h_buf.shape[0]

    @pl.when(place[3] == 1)
    def _():
        copies = [
            pltpu.make_async_copy(kw_ref, w_buf.at[:, pl.ds(0, HD)], sems.at[0]),
            pltpu.make_async_copy(vw_ref, w_buf.at[:, pl.ds(HD, HD)], sems.at[1]),
            chunk_copy(h_ref, place[0], h_buf, sems.at[2]),
        ]
        for copy in copies:
            copy.start()
        for copy in copies[:2]:
            copy.wait()
        out_ref[span:] = jnp.zeros((span, 2 * HD), jnp.float32)
        add_pieces(place[2], place[0], pieces, w_buf, out_ref.at[pl.ds(span, span)])
        copies[2].wait()
        out_ref[:span] = jnp.dot(h_buf[...], w_buf[...], preferred_element_type=jnp.float32)


def distant_kernel(column, place, h_ref, w_ref, near_ref, outer_ref, facing_ref, bias_ref, *refs):
    pieces = refs[:PIECES]
    out_ref, h_buf, acc, sem = refs[PIECES:]
    span = h_buf.shape[0]
    part = slice(column * HD, column * HD + HD)

    @pl.when(place[3] == 1)
    def _():
        copy = chunk_copy(h_ref, place[0], h_buf, sem)
        copy.start()
        own_at = pl.multiple_of(place[1] * span, span)
        outer_at = pl.multiple_of((1 - place[1]) * span, span)
        bias = bias_ref[...].astype(jnp.float32)
        acc[...] = outer_ref[:span] + facing_ref[span:, part] + bias
        add_pieces(place[2], place[0], pieces, w_ref, acc)
        out_ref[pl.ds(outer_at, span), :] = acc[...].astype(jnp.bfloat16)
        own = near_ref[:span] + facing_ref[:span, part] + bias
        copy.wait()
        own += jnp.dot(h_buf[...], w_ref[...], preferred_element_type=jnp.float32)
        out_ref[pl.ds(own_at, span), :] = own.astype(jnp.bfloat16)
        if column == 0:
            mine, theirs = near_ref[span:], outer_ref[span:]
            lower = jnp.where(place[1] == 0, mine, theirs)
            upper = jnp.where(place[1] == 0, theirs, mine)
            out_ref[2 * span :] = jnp.concatenate([lower, upper], axis=0).astype(jnp.bfloat16)


EXTRA = 8
HELD = pl.BlockSpec(memory_space=pltpu.HBM)
FAST = pl.BlockSpec(memory_space=pltpu.VMEM)
SCALAR = pl.BlockSpec(memory_space=pltpu.SMEM)


def in_hbm(x):
    return pltpu.with_memory_space_constraint(x, pltpu.HBM)


def call_project(kernel, name, place, operands, rows, columns, kind, scratch, held=1, copies=()):
    return pl.pallas_call(
        kernel,
        in_specs=[SCALAR] + [HELD] * held + [FAST] * (len(operands) - held),
        out_specs=FAST,
        out_shape=jax.ShapeDtypeStruct((rows, columns), kind),
        scratch_shapes=scratch + [pltpu.SemaphoreType.DMA(copies)],
        compiler_params=pltpu.CompilerParams(vmem_limit_bytes=KERNEL_VMEM),
        cost_estimate=pl.CostEstimate(flops=0, bytes_accessed=0, transcendentals=0),
        name=name,
    )(place, *[in_hbm(x) for x in operands[:held]], *operands[held:])


INWARD = [(0, 1), (3, 2)]
ACROSS = [(1, 2), (2, 1)]
OUTWARD = [(1, 0), (2, 3)]
SWAP = [(0, 1), (1, 0), (2, 3), (3, 2)]


def line_of_four(hidden, key_weight, value_weight, key_bias, value_bias, page_owner):
    index = lax.axis_index("pre")
    member = lax.axis_index(("dec", "tp"))
    span, width = hidden.shape
    depth = key_weight.shape[0]
    share = width // 2 // PIECES
    facing = 3 - index
    near = jnp.bitwise_xor(index, 1)
    distant = jnp.bitwise_xor(facing, 1)
    second = (index < 2).astype(jnp.int32)
    inner = ((index == 1) | (index == 2)).astype(jnp.int32)

    def send(x, pairs):
        return lax.ppermute(x, "pre", pairs)

    def trade(x, apart):
        return lax.ppermute(x, ("dec", "tp"), [(m, m ^ apart) for m in range(PIECES)])

    mine = second * (width // 2) + member * share
    cut = lax.dynamic_slice_in_dim(hidden, mine, share, axis=1)
    tie = lax.optimization_barrier
    block = pltpu.VMEM((span, depth), jnp.bfloat16)
    both = pltpu.VMEM((depth, 2 * HD), jnp.bfloat16)
    key_facing = send(key_weight, ACROSS)
    cut = send(cut, INWARD)
    own_part = call_project(
        near_kernel,
        "near",
        index[None],
        [hidden, key_weight, value_weight],
        span,
        2 * HD,
        jnp.float32,
        [block, both],
        held=3,
        copies=(3,),
    )
    cut, key_facing, key_after, value_after, own_part = tie(
        (cut, key_facing, key_weight, value_weight, own_part)
    )
    value_facing = send(value_after, ACROSS)
    key_swapped = send(key_after, SWAP)
    value_swapped = send(value_after, SWAP)
    chips = [cut, trade(cut, 2), trade(cut, 4), trade(cut, 6)]
    key_swapped, value_facing = tie((key_swapped, value_facing))
    key_distant = send(key_swapped, ACROSS)
    value_distant = send(value_swapped, ACROSS)
    owners = jnp.broadcast_to(page_owner.T.astype(jnp.float32), (EXTRA, page_owner.shape[0]))
    owners = jnp.pad(owners, ((0, 0), (0, HD - page_owner.shape[0])))

    def begin(column, weight):
        part = call_project(
            functools.partial(partial_kernel, column),
            "partial",
            near[None],
            [hidden, weight, own_part, owners],
            span + (EXTRA if column == 0 else 0),
            HD,
            jnp.float32,
            [block],
        )
        return part, send(part, INWARD)

    key_part, key_outer = begin(0, key_swapped)
    chips[2], key_distant, key_outer = tie((chips[2], key_distant, key_outer))
    mates = [trade(x, 1) for x in chips]
    pieces = [x for both_cores in zip(chips, mates) for x in both_cores]

    def place(chunk):
        return jnp.stack([chunk, second, member, inner])

    def finish(column, weight, parts, bias):
        return call_project(
            functools.partial(distant_kernel, column),
            "distant",
            place(distant),
            [hidden, weight, *parts, faced, bias[None, :]] + pieces,
            2 * span + (2 * EXTRA if column == 0 else 0),
            HD,
            jnp.bfloat16,
            [block, pltpu.VMEM((span, HD), jnp.float32)],
        )

    value_parts = begin(1, value_swapped)
    faced = call_project(
        facing_kernel,
        "facing",
        place(facing),
        [hidden, key_facing, value_facing] + pieces,
        2 * span,
        2 * HD,
        jnp.float32,
        [block, both],
        held=3,
        copies=(3,),
    )
    keys = finish(0, key_distant, (key_part, key_outer), key_bias)
    keys_out, keys_across = send(keys, OUTWARD), send(keys, ACROSS)
    values = finish(1, value_distant, value_parts, value_bias)
    values_across = send(values, ACROSS)
    keys_out, values_after = tie((keys_out, values))
    values_out = send(values_after, OUTWARD)
    keys_far, values_far = send(keys_across, OUTWARD), send(values_across, OUTWARD)
    return (
        (keys, keys_out, keys_across, keys_far),
        (values, values_out, values_across, values_far),
    )


def head_of(x, g):
    return x[:, g * HD : (g + 1) * HD]


def attend(q_ref, heads, keys, values, allowed, before, store):
    factor = HD**-0.5 * math.log2(math.e)

    def scores_of(g):
        return lax.dot_general(
            head_of(q_ref, g), keys, (((1,), (1,)), ((), ())), preferred_element_type=jnp.float32
        )

    following = scores_of(0)
    for g in range(heads):
        scores = jnp.where(allowed, following, NEG)
        if g + 1 < heads:
            following = scores_of(g + 1)
        peak = jnp.max(scores, axis=1, keepdims=True)
        if before is not None:
            top, total, mix = before(g)
            peak = jnp.maximum(peak, top)
        weights = jnp.exp2(scores * factor - peak * factor).astype(jnp.bfloat16)
        mixed = jnp.dot(weights, values, preferred_element_type=jnp.float32)
        sums, mixed = mixed[:, HD:], mixed[:, :HD]
        if before is not None:
            shrink = jnp.exp2((top - peak) * factor)
            sums = sums + total * shrink
            mixed = mixed + mix * shrink
        store(g, peak, sums, mixed)


def with_ones(values):
    return jnp.concatenate([values, jnp.ones_like(values)], axis=1)


def prompt_starts(seg_ref, first, span):
    seg = seg_ref[...]
    position = (lax.broadcasted_iota(jnp.int32, (span, 1), 0) + first).astype(jnp.float32)
    start = jnp.zeros((span, 1), jnp.float32)
    for v in range(1, PROMPTS):
        lower = jnp.where(seg < v, 1.0, 0.0)
        bound = jnp.sum(jnp.sum(lower, axis=1, keepdims=True), axis=0, keepdims=True)
        start = jnp.where(position >= bound, bound, start)
    return start.astype(jnp.int32)


def read_owners(held_k, span, listed, named, sem):
    listed[...] = held_k[2 * span :].astype(jnp.float32).astype(jnp.int32)
    copy = pltpu.make_async_copy(listed, named, sem)
    copy.start()
    return copy


def place_pages(index, span, named, held_k, held_v, cache_ref, laid):
    rows = cache_ref.shape[1]
    row = lax.broadcasted_iota(jnp.int32, (rows, 2 * HD), 0)
    for s in range(2):
        rank = jnp.int32(0)
        for p in range(span // PAGE):
            tokens = pl.ds(s * span + p * PAGE, PAGE)
            at = pl.ds(pl.multiple_of(rank * PAGE, PAGE), PAGE)
            laid[s, at, :HD] = held_k[tokens, :]
            laid[s, at, HD:] = held_v[tokens, :]
            rank = rank + (named[s * EXTRA, p] == index).astype(jnp.int32)
        cache_ref[s] = jnp.where(row < rank * PAGE, laid[s, :rows], 0)


def own_kernel(
    heads,
    info,
    q_ref,
    seg_ref,
    k_in,
    k_out,
    v_in,
    v_out,
    top,
    total,
    mix,
    cache_ref,
    held_k,
    held_v,
    q_buf,
    listed,
    named,
    laid,
    sems,
):
    copy = pltpu.make_async_copy(q_ref, q_buf, sems.at[0])
    copy.start()
    span = q_buf.shape[0]
    index = info[0]
    inner = (index == 1) | (index == 2)
    held_k[...] = jnp.where(inner, k_in[...], k_out[...])
    held_v[...] = jnp.where(inner, v_in[...], v_out[...])
    owners = read_owners(held_k, span, listed, named, sems.at[1])
    keys = held_k[: 2 * span]
    values = with_ones(held_v[...])
    columns = lax.broadcasted_iota(jnp.int32, (span, 2 * span), 1)
    rows = lax.broadcasted_iota(jnp.int32, (span, 2 * span), 0)
    start = prompt_starts(seg_ref, index * span, span)
    allowed = (columns <= rows + lax.rem(index, 2) * span) & (
        columns >= start - (index // 2) * 2 * span
    )
    copy.wait()

    def store(g, peak, sums, mixed):
        top[g] = peak
        total[g] = sums[:, :1]
        mix[g] = mixed

    attend(q_buf, heads, keys, values, allowed, None, store)
    owners.wait()
    place_pages(index, span, named, held_k, held_v, cache_ref, laid)


def far_kernel(
    heads,
    info,
    q_ref,
    seg_ref,
    k_across,
    k_far,
    v_across,
    v_far,
    top,
    total,
    mix,
    own_cache,
    out_ref,
    cache_ref,
    held_k,
    held_v,
    q_buf,
    listed,
    named,
    laid,
    sems,
    out_buf,
    far_cache,
):
    copy = pltpu.make_async_copy(q_ref, q_buf, sems.at[0])
    copy.start()
    span = q_buf.shape[0]
    index = info[0]
    inner = (index == 1) | (index == 2)
    held_k[...] = jnp.where(inner, k_across[...], k_far[...])
    held_v[...] = jnp.where(inner, v_across[...], v_far[...])
    owners = read_owners(held_k, span, listed, named, sems.at[1])
    own_at, far_at = index // 2 * 2, (1 - index // 2) * 2
    leaving = [pltpu.make_async_copy(own_cache, cache_ref.at[pl.ds(own_at, 2)], sems.at[2])]
    leaving[0].start()
    copy.wait()

    def leave(g):
        columns = pl.ds(g * HD, HD)
        return pltpu.make_async_copy(out_buf.at[:, columns], out_ref.at[:, columns], sems.at[4 + g])

    def place_far():
        owners.wait()
        place_pages(index, span, named, held_k, held_v, far_cache, laid)
        return pltpu.make_async_copy(far_cache, cache_ref.at[pl.ds(far_at, 2)], sems.at[3])

    @pl.when(index < 2)
    def _():
        for g in range(heads):
            out_buf[:, g * HD : (g + 1) * HD] = (mix[g] / total[g]).astype(out_buf.dtype)
            leave(g).start()
        place_far().start()

    @pl.when(index >= 2)
    def _():
        keys = held_k[: 2 * span]
        values = with_ones(held_v[...])
        columns = lax.broadcasted_iota(jnp.int32, (span, 2 * span), 1)
        allowed = columns >= prompt_starts(seg_ref, index * span, span)

        def store(g, peak, sums, mixed):
            out_buf[:, g * HD : (g + 1) * HD] = (mixed / sums).astype(out_buf.dtype)
            leave(g).start()
            if g == heads // 2:
                place_far().start()

        attend(q_buf, heads, keys, values, allowed, lambda g: (top[g], total[g], mix[g]), store)

    for g in range(heads):
        leave(g).wait()
    leaving[0].wait()
    pltpu.make_async_copy(far_cache, cache_ref.at[pl.ds(far_at, 2)], sems.at[3]).wait()


def attention_of_pairs(queries, segment_ids, keys, values, capacity):
    span = queries.shape[0]
    heads = queries.shape[1] // HD
    info = lax.axis_index("pre").astype(jnp.int32)[None]
    segments = segment_ids.reshape(-1, HD)
    scores = heads * span * 2 * span
    cost = pl.CostEstimate(flops=4 * scores * HD, bytes_accessed=8 * scores, transcendentals=scores)
    params = pltpu.CompilerParams(vmem_limit_bytes=KERNEL_VMEM)
    scratch = [
        pltpu.VMEM((2 * span + 2 * EXTRA, HD), jnp.bfloat16),
        pltpu.VMEM((2 * span, HD), jnp.bfloat16),
        pltpu.VMEM(queries.shape, jnp.bfloat16),
        pltpu.VMEM((2 * EXTRA, HD), jnp.int32),
        pltpu.SMEM((2 * EXTRA, HD), jnp.int32),
        pltpu.VMEM((2, (capacity + 1) * PAGE, 2 * HD), jnp.bfloat16),
        pltpu.SemaphoreType.DMA((4 + heads,)),
    ]
    state = pl.pallas_call(
        functools.partial(own_kernel, heads),
        in_specs=[SCALAR, HELD] + [FAST] * 5,
        out_specs=[FAST] * 4,
        out_shape=[
            jax.ShapeDtypeStruct((heads, span, 1), jnp.float32),
            jax.ShapeDtypeStruct((heads, span, 1), jnp.float32),
            jax.ShapeDtypeStruct((heads, span, HD), jnp.float32),
            jax.ShapeDtypeStruct((2, capacity * PAGE, 2 * HD), jnp.bfloat16),
        ],
        scratch_shapes=scratch,
        compiler_params=params,
        cost_estimate=cost,
        name="attend_own",
    )(info, in_hbm(queries), segments, *keys[:2], *values[:2])
    return pl.pallas_call(
        functools.partial(far_kernel, heads),
        in_specs=[SCALAR, HELD] + [FAST] * 9,
        out_specs=[HELD] * 2,
        out_shape=[
            jax.ShapeDtypeStruct(queries.shape, jnp.bfloat16),
            jax.ShapeDtypeStruct((4, capacity * PAGE, 2 * HD), jnp.bfloat16),
        ],
        scratch_shapes=scratch
        + [
            pltpu.VMEM(queries.shape, jnp.bfloat16),
            pltpu.VMEM((2, capacity * PAGE, 2 * HD), jnp.bfloat16),
        ],
        compiler_params=params,
        cost_estimate=cost,
        name="attend_far",
    )(info, in_hbm(queries), segments, *keys[2:], *values[2:], *state)


def gathered(hidden, key_weight, value_weight, key_bias, value_bias):
    joined = jnp.concatenate([key_weight, value_weight], axis=1)
    joined = lax.all_gather(joined, "pre", axis=0, tiled=True)
    bias = jnp.concatenate([key_bias, value_bias]).astype(jnp.float32)
    local = jnp.dot(hidden, joined, preferred_element_type=jnp.float32) + bias
    both = lax.all_gather(local.astype(jnp.bfloat16), "pre", axis=0, tiled=True)
    return both[:, :HD], both[:, HD:]


def body(hidden, queries, key_weight, value_weight, key_bias, value_bias, segment_ids, page_owner):
    n_pre = lax.axis_size("pre")
    index = lax.axis_index("pre")
    span = hidden.shape[0]
    pages_dev = span // PAGE
    capacity = 2 * pages_dev // n_pre
    assert key_weight.shape[1] == HD
    arrays = (hidden, key_weight, value_weight, key_bias, value_bias)
    if n_pre == 4:
        keys, values = line_of_four(*arrays, page_owner)
        mixed, cache = attention_of_pairs(queries, segment_ids, keys, values, capacity)
        return (mixed, cache[None])

    own_segments = lax.dynamic_slice_in_dim(segment_ids, index * span, span)
    start = jnp.sum(
        (segment_ids[None, :] < own_segments[:, None]).astype(jnp.int32), axis=1, keepdims=True
    )
    info = jnp.stack([index, start[0, 0] // span]).astype(jnp.int32)
    owners = lax.all_gather(page_owner[:, 0], "pre")
    keys, values = gathered(*arrays)
    mine = (owners == index).astype(jnp.int32)
    rank = jnp.cumsum(mine, axis=1) - mine
    numbers = jnp.arange(n_pre * pages_dev, dtype=jnp.int32).reshape(n_pre, 1, pages_dev)
    wanted = (mine[:, None, :] == 1) & (
        rank[:, None, :] == jnp.arange(capacity, dtype=jnp.int32)[None, :, None]
    )
    slots = jnp.max(jnp.where(wanted, numbers, -1), axis=2).reshape(-1)
    mixed, cache = attention(info, slots, queries, keys, values, start, n_pre, capacity)
    return (mixed, cache[None])


def solution(mesh):
    return jax.shard_map(
        body,
        mesh=mesh,
        in_specs=(
            P(("group", "pre"), None),
            P(("group", "pre"), ("dec", "tp")),
            P("pre", ("dec", "tp")),
            P("pre", ("dec", "tp")),
            P(("dec", "tp")),
            P(("dec", "tp")),
            P("group"),
            P(("group", "pre"), None),
        ),
        out_specs=(
            P(("group", "pre"), ("dec", "tp")),
            P(("group", "pre"), None, None, ("dec", "tp")),
        ),
        check_vma=False,
    )
```

```python
import functools
import math

import jax
import jax.numpy as jnp
from jax import lax
from jax.experimental import pallas as pl
from jax.experimental.pallas import tpu as pltpu
from jax.sharding import PartitionSpec as P

HD = 128
PAGE = 16
NEG = -1e30
KERNEL_VMEM = 16 * 1024 * 1024
PROMPTS = 4


def attention_kernel(heads, span, info, slots, q_ref, k_ref, v_ref, start_ref, out_ref, cache_ref, acc, top):
    index = info[0]
    first = info[1]
    factor = HD**-0.5 * math.log2(math.e)
    columns = lax.broadcasted_iota(jnp.int32, (span, span), 1)
    rows = lax.broadcasted_iota(jnp.int32, (span, span), 0)

    def block(j, diagonal):
        at = pl.multiple_of(j * span, span)
        keys = k_ref[pl.ds(at, span), :]
        values = jnp.concatenate(
            [v_ref[pl.ds(at, span), :], jnp.ones((span, HD), jnp.bfloat16)], axis=1
        )
        allowed = columns >= start_ref[...] - at
        if diagonal:
            allowed = allowed & (columns <= rows)
        for g in range(heads):
            scores = lax.dot_general(
                q_ref[:, g * HD : (g + 1) * HD],
                keys,
                (((1,), (1,)), ((), ())),
                preferred_element_type=jnp.float32,
            )
            scores = jnp.where(allowed, scores, NEG)
            peak = jnp.max(scores, axis=1, keepdims=True)
            if not diagonal:
                before = top[g]
                peak = jnp.maximum(peak, before)
            weights = jnp.exp2(scores * factor - peak * factor).astype(jnp.bfloat16)
            mixed = jnp.dot(weights, values, preferred_element_type=jnp.float32)
            if not diagonal:
                mixed = mixed + acc[g] * jnp.exp2((before - peak) * factor)
            top[g] = peak
            acc[g] = mixed

    block(index, True)

    @pl.loop(first, index)
    def _(j):
        block(j, False)

    for g in range(heads):
        mixed = acc[g]
        out_ref[:, g * HD : (g + 1) * HD] = (mixed[:, :HD] / mixed[:, HD:]).astype(out_ref.dtype)

    capacity = cache_ref.shape[1] // PAGE
    empty = jnp.zeros((PAGE, HD), cache_ref.dtype)
    for s in range(cache_ref.shape[0]):

        @pl.loop(0, capacity)
        def _(r):
            page = slots[s * capacity + r]
            token = pl.ds(pl.multiple_of(jnp.maximum(page, 0) * PAGE, PAGE), PAGE)
            row = pl.ds(pl.multiple_of(r * PAGE, PAGE), PAGE)
            cache_ref[s, row, :HD] = jnp.where(page >= 0, k_ref[token, :], empty)
            cache_ref[s, row, HD:] = jnp.where(page >= 0, v_ref[token, :], empty)


def attention(info, slots, queries, keys, values, start, n_pre, capacity):
    span = queries.shape[0]
    heads = queries.shape[1] // HD
    return pl.pallas_call(
        functools.partial(attention_kernel, heads, span),
        in_specs=[
            pl.BlockSpec(memory_space=pltpu.SMEM),
            pl.BlockSpec(memory_space=pltpu.SMEM),
            pl.BlockSpec(memory_space=pltpu.VMEM),
            pl.BlockSpec(memory_space=pltpu.VMEM),
            pl.BlockSpec(memory_space=pltpu.VMEM),
            pl.BlockSpec(memory_space=pltpu.VMEM),
        ],
        out_specs=[
            pl.BlockSpec(memory_space=pltpu.VMEM),
            pl.BlockSpec(memory_space=pltpu.VMEM),
        ],
        out_shape=[
            jax.ShapeDtypeStruct(queries.shape, jnp.bfloat16),
            jax.ShapeDtypeStruct((n_pre, capacity * PAGE, 2 * HD), jnp.bfloat16),
        ],
        scratch_shapes=[
            pltpu.VMEM((heads, span, 2 * HD), jnp.float32),
            pltpu.VMEM((heads, span, 1), jnp.float32),
        ],
        compiler_params=pltpu.CompilerParams(vmem_limit_bytes=KERNEL_VMEM),
        cost_estimate=pl.CostEstimate(
            flops=4 * heads * span * span * n_pre * HD,
            bytes_accessed=4 * queries.size * 2,
            transcendentals=heads * span * span * n_pre,
        ),
        name="attention",
    )(info, slots, queries, keys, values, start)


PIECES = 8


def chunk_copy(h_ref, chunk, h_buf, sem):
    depth = h_buf.shape[1]
    columns = pl.ds(pl.multiple_of(chunk * depth, depth), depth)
    return pltpu.make_async_copy(h_ref.at[:, columns], h_buf, sem)


def add_pieces(member, chunk, pieces, w_ref, acc_ref):
    share = pieces[0].shape[1]
    half = PIECES // 2
    for side in range(2):

        @pl.when(jnp.bitwise_xor(member // half, side) == lax.rem(chunk, 2))
        def _():
            total = acc_ref[...]
            for j in range(side * half, side * half + half):
                row = lax.rem(jnp.bitwise_xor(member, j), half) * share
                total += jnp.dot(
                    pieces[j][...],
                    w_ref[pl.ds(pl.multiple_of(row, share), share), :],
                    preferred_element_type=jnp.float32,
                )
            acc_ref[...] = total


def near_kernel(place, h_ref, kw_ref, vw_ref, out_ref, h_buf, w_buf, sems):
    copies = [
        chunk_copy(h_ref, place[0], h_buf, sems.at[0]),
        pltpu.make_async_copy(kw_ref, w_buf.at[:, pl.ds(0, HD)], sems.at[1]),
        pltpu.make_async_copy(vw_ref, w_buf.at[:, pl.ds(HD, HD)], sems.at[2]),
    ]
    for copy in copies:
        copy.start()
    for copy in copies:
        copy.wait()
    out_ref[...] = jnp.dot(h_buf[...], w_buf[...], preferred_element_type=jnp.float32)


def partial_kernel(
    column, place, h_ref, w_ref, before_ref, owner_ref, out_ref, h_buf, w_buf, sems
):
    copies = [
        pltpu.make_async_copy(w_ref, w_buf, sems.at[0]),
        chunk_copy(h_ref, place[0], h_buf, sems.at[1]),
    ]
    for copy in copies:
        copy.start()
    span = h_buf.shape[0]
    part = slice(column * HD, column * HD + HD)
    if column == 0:
        out_ref[span:] = owner_ref[...]
    for copy in copies:
        copy.wait()
    out_ref[:span] = before_ref[:, part] + jnp.dot(
        h_buf[...], w_buf[...], preferred_element_type=jnp.float32
    )


def facing_kernel(place, h_ref, kw_ref, vw_ref, *refs):
    pieces = refs[:PIECES]
    out_ref, h_buf, w_buf, sems = refs[PIECES:]
    span = h_buf.shape[0]

    @pl.when(place[3] == 1)
    def _():
        copies = [
            pltpu.make_async_copy(kw_ref, w_buf.at[:, pl.ds(0, HD)], sems.at[0]),
            pltpu.make_async_copy(vw_ref, w_buf.at[:, pl.ds(HD, HD)], sems.at[1]),
            chunk_copy(h_ref, place[0], h_buf, sems.at[2]),
        ]
        for copy in copies:
            copy.start()
        for copy in copies[:2]:
            copy.wait()
        out_ref[span:] = jnp.zeros((span, 2 * HD), jnp.float32)
        add_pieces(place[2], place[0], pieces, w_buf, out_ref.at[pl.ds(span, span)])
        copies[2].wait()
        out_ref[:span] = jnp.dot(h_buf[...], w_buf[...], preferred_element_type=jnp.float32)


def distant_kernel(column, place, h_ref, w_ref, near_ref, outer_ref, facing_ref, bias_ref, *refs):
    pieces = refs[:PIECES]
    out_ref, h_buf, w_buf, acc, *parts, sems = refs[PIECES:]
    near, outer = parts or (near_ref, outer_ref)
    span = h_buf.shape[0]
    part = slice(column * HD, column * HD + HD)

    @pl.when(place[3] == 1)
    def _():
        copies = [
            pltpu.make_async_copy(w_ref, w_buf, sems.at[0]),
            chunk_copy(h_ref, place[0], h_buf, sems.at[1]),
        ]
        if parts:
            copies.append(pltpu.make_async_copy(outer_ref, outer, sems.at[2]))
            copies.append(pltpu.make_async_copy(near_ref, near, sems.at[3]))
        for copy in copies:
            copy.start()
        for copy in copies[2:]:
            copy.wait()
        own_at = pl.multiple_of(place[1] * span, span)
        outer_at = pl.multiple_of((1 - place[1]) * span, span)
        bias = bias_ref[...].astype(jnp.float32)
        acc[...] = outer[:span] + facing_ref[span:, part] + bias
        copies[0].wait()
        add_pieces(place[2], place[0], pieces, w_buf, acc)
        out_ref[pl.ds(outer_at, span), :] = acc[...].astype(jnp.bfloat16)
        own = near[:span] + facing_ref[:span, part] + bias
        copies[1].wait()
        own += jnp.dot(h_buf[...], w_buf[...], preferred_element_type=jnp.float32)
        out_ref[pl.ds(own_at, span), :] = own.astype(jnp.bfloat16)
        if column == 0:
            mine, theirs = near[span:], outer[span:]
            lower = jnp.where(place[1] == 0, mine, theirs)
            upper = jnp.where(place[1] == 0, theirs, mine)
            out_ref[2 * span :] = jnp.concatenate([lower, upper], axis=0).astype(jnp.bfloat16)


EXTRA = 8
HELD = pl.BlockSpec(memory_space=pltpu.HBM)
FAST = pl.BlockSpec(memory_space=pltpu.VMEM)
SCALAR = pl.BlockSpec(memory_space=pltpu.SMEM)


def in_hbm(x):
    return pltpu.with_memory_space_constraint(x, pltpu.HBM)


def call_project(kernel, name, place, operands, rows, columns, kind, scratch, held=1, copies=()):
    return pl.pallas_call(
        kernel,
        in_specs=[SCALAR] + [HELD] * held + [FAST] * (len(operands) - held),
        out_specs=FAST,
        out_shape=jax.ShapeDtypeStruct((rows, columns), kind),
        scratch_shapes=scratch + [pltpu.SemaphoreType.DMA(copies)],
        compiler_params=pltpu.CompilerParams(vmem_limit_bytes=KERNEL_VMEM),
        cost_estimate=pl.CostEstimate(flops=0, bytes_accessed=0, transcendentals=0),
        name=name,
    )(place, *[in_hbm(x) for x in operands[:held]], *operands[held:])


INWARD = [(0, 1), (3, 2)]
ACROSS = [(1, 2), (2, 1)]
OUTWARD = [(1, 0), (2, 3)]
SWAP = [(0, 1), (1, 0), (2, 3), (3, 2)]


def line_of_four(hidden, key_weight, value_weight, key_bias, value_bias, page_owner):
    index = lax.axis_index("pre")
    member = lax.axis_index(("dec", "tp"))
    span, width = hidden.shape
    depth = key_weight.shape[0]
    share = width // 2 // PIECES
    facing = 3 - index
    near = jnp.bitwise_xor(index, 1)
    distant = jnp.bitwise_xor(facing, 1)
    second = (index < 2).astype(jnp.int32)
    inner = ((index == 1) | (index == 2)).astype(jnp.int32)

    def send(x, pairs):
        return lax.ppermute(x, "pre", pairs)

    def trade(x, apart):
        return lax.ppermute(x, ("dec", "tp"), [(m, m ^ apart) for m in range(PIECES)])

    mine = second * (width // 2) + member * share
    cut = lax.dynamic_slice_in_dim(hidden, mine, share, axis=1)
    tie = lax.optimization_barrier
    block = pltpu.VMEM((span, depth), jnp.bfloat16)
    both = pltpu.VMEM((depth, 2 * HD), jnp.bfloat16)
    single = pltpu.VMEM((depth, HD), jnp.bfloat16)
    key_facing = send(key_weight, ACROSS)
    cut = send(cut, INWARD)
    own_part = call_project(
        near_kernel,
        "near",
        index[None],
        [hidden, key_weight, value_weight],
        span,
        2 * HD,
        jnp.float32,
        [block, both],
        held=3,
        copies=(3,),
    )
    cut, key_facing, key_after, value_after, own_part = tie(
        (cut, key_facing, key_weight, value_weight, own_part)
    )
    value_facing = send(value_after, ACROSS)
    key_swapped = send(key_after, SWAP)
    value_swapped = send(value_after, SWAP)
    chips = [cut, trade(cut, 2), trade(cut, 4), trade(cut, 6)]
    key_swapped, value_facing = tie((key_swapped, value_facing))
    key_distant = send(key_swapped, ACROSS)
    value_distant = send(value_swapped, ACROSS)
    owners = jnp.broadcast_to(page_owner.T.astype(jnp.float32), (EXTRA, page_owner.shape[0]))
    owners = jnp.pad(owners, ((0, 0), (0, HD - page_owner.shape[0])))

    def begin(column, weight):
        part = call_project(
            functools.partial(partial_kernel, column),
            "partial",
            near[None],
            [hidden, weight, own_part, owners],
            span + (EXTRA if column == 0 else 0),
            HD,
            jnp.float32,
            [block, single],
            held=2,
            copies=(2,),
        )
        return part, send(part, INWARD)

    key_part, key_outer = begin(0, key_swapped)
    chips[2], key_distant, key_outer = tie((chips[2], key_distant, key_outer))
    mates = [trade(x, 1) for x in chips]
    pieces = [x for both_cores in zip(chips, mates) for x in both_cores]

    def place(chunk):
        return jnp.stack([chunk, second, member, inner])

    def finish(column, weight, parts, bias):
        return call_project(
            functools.partial(distant_kernel, column),
            "distant",
            place(distant),
            [hidden, weight, *parts, faced, bias[None, :]] + pieces,
            2 * span + (2 * EXTRA if column == 0 else 0),
            HD,
            jnp.bfloat16,
            [block, single, pltpu.VMEM((span, HD), jnp.float32)]
            + [pltpu.VMEM(x.shape, jnp.float32) for x in parts if column == 0],
            held=4 if column == 0 else 2,
            copies=(4,),
        )

    value_parts = begin(1, value_swapped)
    faced = call_project(
        facing_kernel,
        "facing",
        place(facing),
        [hidden, key_facing, value_facing] + pieces,
        2 * span,
        2 * HD,
        jnp.float32,
        [block, both],
        held=3,
        copies=(3,),
    )
    keys = finish(0, key_distant, (key_part, key_outer), key_bias)
    keys_out, keys_across = send(keys, OUTWARD), send(keys, ACROSS)
    values = finish(1, value_distant, value_parts, value_bias)
    values_across = send(values, ACROSS)
    keys_out, values_after = tie((keys_out, values))
    values_out = send(values_after, OUTWARD)
    keys_far, values_far = send(keys_across, OUTWARD), send(values_across, OUTWARD)
    return (
        (keys, keys_out, keys_across, keys_far),
        (values, values_out, values_across, values_far),
    )


def head_of(x, g):
    return x[:, g * HD : (g + 1) * HD]


def attend(q_ref, heads, keys, values, allowed, before, store):
    factor = HD**-0.5 * math.log2(math.e)

    def scores_of(g):
        return lax.dot_general(
            head_of(q_ref, g), keys, (((1,), (1,)), ((), ())), preferred_element_type=jnp.float32
        )

    following = scores_of(0)
    for g in range(heads):
        scores = jnp.where(allowed, following, NEG)
        if g + 1 < heads:
            following = scores_of(g + 1)
        peak = jnp.max(scores, axis=1, keepdims=True)
        if before is not None:
            top, total, mix = before(g)
            peak = jnp.maximum(peak, top)
        weights = jnp.exp2(scores * factor - peak * factor).astype(jnp.bfloat16)
        mixed = jnp.dot(weights, values, preferred_element_type=jnp.float32)
        sums, mixed = mixed[:, HD:], mixed[:, :HD]
        if before is not None:
            shrink = jnp.exp2((top - peak) * factor)
            sums = sums + total * shrink
            mixed = mixed + mix * shrink
        store(g, peak, sums, mixed)


def with_ones(values):
    return jnp.concatenate([values, jnp.ones_like(values)], axis=1)


def prompt_starts(seg_ref, first, span):
    seg = seg_ref[...]
    position = (lax.broadcasted_iota(jnp.int32, (span, 1), 0) + first).astype(jnp.float32)
    start = jnp.zeros((span, 1), jnp.float32)
    for v in range(1, PROMPTS):
        lower = jnp.where(seg < v, 1.0, 0.0)
        bound = jnp.sum(jnp.sum(lower, axis=1, keepdims=True), axis=0, keepdims=True)
        start = jnp.where(position >= bound, bound, start)
    return start.astype(jnp.int32)


def read_owners(held_k, span, listed, named, sem):
    listed[...] = held_k[2 * span :].astype(jnp.float32).astype(jnp.int32)
    copy = pltpu.make_async_copy(listed, named, sem)
    copy.start()
    return copy


def place_pages(index, span, named, held_k, held_v, cache_ref, laid):
    rows = cache_ref.shape[1]
    row = lax.broadcasted_iota(jnp.int32, (rows, 2 * HD), 0)
    for s in range(2):
        rank = jnp.int32(0)
        for p in range(span // PAGE):
            tokens = pl.ds(s * span + p * PAGE, PAGE)
            at = pl.ds(pl.multiple_of(rank * PAGE, PAGE), PAGE)
            laid[s, at, :HD] = held_k[tokens, :]
            laid[s, at, HD:] = held_v[tokens, :]
            rank = rank + (named[s * EXTRA, p] == index).astype(jnp.int32)
        cache_ref[s] = jnp.where(row < rank * PAGE, laid[s, :rows], 0)


def own_kernel(
    heads,
    info,
    q_ref,
    seg_ref,
    k_in,
    k_out,
    v_in,
    v_out,
    top,
    total,
    mix,
    cache_ref,
    held_k,
    held_v,
    q_buf,
    listed,
    named,
    laid,
    sems,
):
    copy = pltpu.make_async_copy(q_ref, q_buf, sems.at[0])
    copy.start()
    span = q_buf.shape[0]
    index = info[0]
    inner = (index == 1) | (index == 2)
    held_k[...] = jnp.where(inner, k_in[...], k_out[...])
    held_v[...] = jnp.where(inner, v_in[...], v_out[...])
    owners = read_owners(held_k, span, listed, named, sems.at[1])
    keys = held_k[: 2 * span]
    values = with_ones(held_v[...])
    columns = lax.broadcasted_iota(jnp.int32, (span, 2 * span), 1)
    rows = lax.broadcasted_iota(jnp.int32, (span, 2 * span), 0)
    start = prompt_starts(seg_ref, index * span, span)
    allowed = (columns <= rows + lax.rem(index, 2) * span) & (
        columns >= start - (index // 2) * 2 * span
    )
    copy.wait()

    def store(g, peak, sums, mixed):
        top[g] = peak
        total[g] = sums[:, :1]
        mix[g] = mixed

    attend(q_buf, heads, keys, values, allowed, None, store)
    owners.wait()
    place_pages(index, span, named, held_k, held_v, cache_ref, laid)


def far_kernel(
    heads,
    info,
    q_ref,
    seg_ref,
    k_across,
    k_far,
    v_across,
    v_far,
    top,
    total,
    mix,
    own_cache,
    out_ref,
    cache_ref,
    held_k,
    held_v,
    q_buf,
    listed,
    named,
    laid,
    sems,
    out_buf,
    far_cache,
):
    copy = pltpu.make_async_copy(q_ref, q_buf, sems.at[0])
    copy.start()
    span = q_buf.shape[0]
    index = info[0]
    inner = (index == 1) | (index == 2)
    held_k[...] = jnp.where(inner, k_across[...], k_far[...])
    held_v[...] = jnp.where(inner, v_across[...], v_far[...])
    owners = read_owners(held_k, span, listed, named, sems.at[1])
    own_at, far_at = index // 2 * 2, (1 - index // 2) * 2
    leaving = [pltpu.make_async_copy(own_cache, cache_ref.at[pl.ds(own_at, 2)], sems.at[2])]
    leaving[0].start()
    copy.wait()

    def leave(g):
        columns = pl.ds(g * HD, HD)
        return pltpu.make_async_copy(out_buf.at[:, columns], out_ref.at[:, columns], sems.at[4 + g])

    def place_far():
        owners.wait()
        place_pages(index, span, named, held_k, held_v, far_cache, laid)
        return pltpu.make_async_copy(far_cache, cache_ref.at[pl.ds(far_at, 2)], sems.at[3])

    @pl.when(index < 2)
    def _():
        for g in range(heads):
            out_buf[:, g * HD : (g + 1) * HD] = (mix[g] / total[g]).astype(out_buf.dtype)
            leave(g).start()
        place_far().start()

    @pl.when(index >= 2)
    def _():
        keys = held_k[: 2 * span]
        values = with_ones(held_v[...])
        columns = lax.broadcasted_iota(jnp.int32, (span, 2 * span), 1)
        allowed = columns >= prompt_starts(seg_ref, index * span, span)

        def store(g, peak, sums, mixed):
            out_buf[:, g * HD : (g + 1) * HD] = (mixed / sums).astype(out_buf.dtype)
            leave(g).start()
            if g == heads // 2:
                place_far().start()

        attend(q_buf, heads, keys, values, allowed, lambda g: (top[g], total[g], mix[g]), store)

    for g in range(heads):
        leave(g).wait()
    leaving[0].wait()
    pltpu.make_async_copy(far_cache, cache_ref.at[pl.ds(far_at, 2)], sems.at[3]).wait()


def attention_of_pairs(queries, segment_ids, keys, values, capacity):
    span = queries.shape[0]
    heads = queries.shape[1] // HD
    info = lax.axis_index("pre").astype(jnp.int32)[None]
    segments = segment_ids.reshape(-1, HD)
    scores = heads * span * 2 * span
    cost = pl.CostEstimate(flops=4 * scores * HD, bytes_accessed=8 * scores, transcendentals=scores)
    params = pltpu.CompilerParams(vmem_limit_bytes=KERNEL_VMEM)
    scratch = [
        pltpu.VMEM((2 * span + 2 * EXTRA, HD), jnp.bfloat16),
        pltpu.VMEM((2 * span, HD), jnp.bfloat16),
        pltpu.VMEM(queries.shape, jnp.bfloat16),
        pltpu.VMEM((2 * EXTRA, HD), jnp.int32),
        pltpu.SMEM((2 * EXTRA, HD), jnp.int32),
        pltpu.VMEM((2, (capacity + 1) * PAGE, 2 * HD), jnp.bfloat16),
        pltpu.SemaphoreType.DMA((4 + heads,)),
    ]
    state = pl.pallas_call(
        functools.partial(own_kernel, heads),
        in_specs=[SCALAR, HELD] + [FAST] * 5,
        out_specs=[FAST] * 4,
        out_shape=[
            jax.ShapeDtypeStruct((heads, span, 1), jnp.float32),
            jax.ShapeDtypeStruct((heads, span, 1), jnp.float32),
            jax.ShapeDtypeStruct((heads, span, HD), jnp.float32),
            jax.ShapeDtypeStruct((2, capacity * PAGE, 2 * HD), jnp.bfloat16),
        ],
        scratch_shapes=scratch,
        compiler_params=params,
        cost_estimate=cost,
        name="attend_own",
    )(info, in_hbm(queries), segments, *keys[:2], *values[:2])
    return pl.pallas_call(
        functools.partial(far_kernel, heads),
        in_specs=[SCALAR, HELD] + [FAST] * 9,
        out_specs=[HELD] * 2,
        out_shape=[
            jax.ShapeDtypeStruct(queries.shape, jnp.bfloat16),
            jax.ShapeDtypeStruct((4, capacity * PAGE, 2 * HD), jnp.bfloat16),
        ],
        scratch_shapes=scratch
        + [
            pltpu.VMEM(queries.shape, jnp.bfloat16),
            pltpu.VMEM((2, capacity * PAGE, 2 * HD), jnp.bfloat16),
        ],
        compiler_params=params,
        cost_estimate=cost,
        name="attend_far",
    )(info, in_hbm(queries), segments, *keys[2:], *values[2:], *state)


def gathered(hidden, key_weight, value_weight, key_bias, value_bias):
    joined = jnp.concatenate([key_weight, value_weight], axis=1)
    joined = lax.all_gather(joined, "pre", axis=0, tiled=True)
    bias = jnp.concatenate([key_bias, value_bias]).astype(jnp.float32)
    local = jnp.dot(hidden, joined, preferred_element_type=jnp.float32) + bias
    both = lax.all_gather(local.astype(jnp.bfloat16), "pre", axis=0, tiled=True)
    return both[:, :HD], both[:, HD:]


def body(hidden, queries, key_weight, value_weight, key_bias, value_bias, segment_ids, page_owner):
    n_pre = lax.axis_size("pre")
    index = lax.axis_index("pre")
    span = hidden.shape[0]
    pages_dev = span // PAGE
    capacity = 2 * pages_dev // n_pre
    assert key_weight.shape[1] == HD
    arrays = (hidden, key_weight, value_weight, key_bias, value_bias)
    if n_pre == 4:
        keys, values = line_of_four(*arrays, page_owner)
        mixed, cache = attention_of_pairs(queries, segment_ids, keys, values, capacity)
        return (mixed, cache[None])

    own_segments = lax.dynamic_slice_in_dim(segment_ids, index * span, span)
    start = jnp.sum(
        (segment_ids[None, :] < own_segments[:, None]).astype(jnp.int32), axis=1, keepdims=True
    )
    info = jnp.stack([index, start[0, 0] // span]).astype(jnp.int32)
    owners = lax.all_gather(page_owner[:, 0], "pre")
    keys, values = gathered(*arrays)
    mine = (owners == index).astype(jnp.int32)
    rank = jnp.cumsum(mine, axis=1) - mine
    numbers = jnp.arange(n_pre * pages_dev, dtype=jnp.int32).reshape(n_pre, 1, pages_dev)
    wanted = (mine[:, None, :] == 1) & (
        rank[:, None, :] == jnp.arange(capacity, dtype=jnp.int32)[None, :, None]
    )
    slots = jnp.max(jnp.where(wanted, numbers, -1), axis=2).reshape(-1)
    mixed, cache = attention(info, slots, queries, keys, values, start, n_pre, capacity)
    return (mixed, cache[None])


def solution(mesh):
    return jax.shard_map(
        body,
        mesh=mesh,
        in_specs=(
            P(("group", "pre"), None),
            P(("group", "pre"), ("dec", "tp")),
            P("pre", ("dec", "tp")),
            P("pre", ("dec", "tp")),
            P(("dec", "tp")),
            P(("dec", "tp")),
            P("group"),
            P(("group", "pre"), None),
        ),
        out_specs=(
            P(("group", "pre"), ("dec", "tp")),
            P(("group", "pre"), None, None, ("dec", "tp")),
        ),
        check_vma=False,
    )
```

```python
import functools
import math

import jax
import jax.numpy as jnp
from jax import lax
from jax.experimental import pallas as pl
from jax.experimental.pallas import tpu as pltpu
from jax.sharding import PartitionSpec as P

HD = 128
PAGE = 16
NEG = -1e30
KERNEL_VMEM = 16 * 1024 * 1024
PROMPTS = 4


def attention_kernel(heads, span, info, slots, q_ref, k_ref, v_ref, start_ref, out_ref, cache_ref, acc, top):
    index = info[0]
    first = info[1]
    factor = HD**-0.5 * math.log2(math.e)
    columns = lax.broadcasted_iota(jnp.int32, (span, span), 1)
    rows = lax.broadcasted_iota(jnp.int32, (span, span), 0)

    def block(j, diagonal):
        at = pl.multiple_of(j * span, span)
        keys = k_ref[pl.ds(at, span), :]
        values = jnp.concatenate(
            [v_ref[pl.ds(at, span), :], jnp.ones((span, HD), jnp.bfloat16)], axis=1
        )
        allowed = columns >= start_ref[...] - at
        if diagonal:
            allowed = allowed & (columns <= rows)
        for g in range(heads):
            scores = lax.dot_general(
                q_ref[:, g * HD : (g + 1) * HD],
                keys,
                (((1,), (1,)), ((), ())),
                preferred_element_type=jnp.float32,
            )
            scores = jnp.where(allowed, scores, NEG)
            peak = jnp.max(scores, axis=1, keepdims=True)
            if not diagonal:
                before = top[g]
                peak = jnp.maximum(peak, before)
            weights = jnp.exp2(scores * factor - peak * factor).astype(jnp.bfloat16)
            mixed = jnp.dot(weights, values, preferred_element_type=jnp.float32)
            if not diagonal:
                mixed = mixed + acc[g] * jnp.exp2((before - peak) * factor)
            top[g] = peak
            acc[g] = mixed

    block(index, True)

    @pl.loop(first, index)
    def _(j):
        block(j, False)

    for g in range(heads):
        mixed = acc[g]
        out_ref[:, g * HD : (g + 1) * HD] = (mixed[:, :HD] / mixed[:, HD:]).astype(out_ref.dtype)

    capacity = cache_ref.shape[1] // PAGE
    empty = jnp.zeros((PAGE, HD), cache_ref.dtype)
    for s in range(cache_ref.shape[0]):

        @pl.loop(0, capacity)
        def _(r):
            page = slots[s * capacity + r]
            token = pl.ds(pl.multiple_of(jnp.maximum(page, 0) * PAGE, PAGE), PAGE)
            row = pl.ds(pl.multiple_of(r * PAGE, PAGE), PAGE)
            cache_ref[s, row, :HD] = jnp.where(page >= 0, k_ref[token, :], empty)
            cache_ref[s, row, HD:] = jnp.where(page >= 0, v_ref[token, :], empty)


def attention(info, slots, queries, keys, values, start, n_pre, capacity):
    span = queries.shape[0]
    heads = queries.shape[1] // HD
    return pl.pallas_call(
        functools.partial(attention_kernel, heads, span),
        in_specs=[
            pl.BlockSpec(memory_space=pltpu.SMEM),
            pl.BlockSpec(memory_space=pltpu.SMEM),
            pl.BlockSpec(memory_space=pltpu.VMEM),
            pl.BlockSpec(memory_space=pltpu.VMEM),
            pl.BlockSpec(memory_space=pltpu.VMEM),
            pl.BlockSpec(memory_space=pltpu.VMEM),
        ],
        out_specs=[
            pl.BlockSpec(memory_space=pltpu.VMEM),
            pl.BlockSpec(memory_space=pltpu.VMEM),
        ],
        out_shape=[
            jax.ShapeDtypeStruct(queries.shape, jnp.bfloat16),
            jax.ShapeDtypeStruct((n_pre, capacity * PAGE, 2 * HD), jnp.bfloat16),
        ],
        scratch_shapes=[
            pltpu.VMEM((heads, span, 2 * HD), jnp.float32),
            pltpu.VMEM((heads, span, 1), jnp.float32),
        ],
        compiler_params=pltpu.CompilerParams(vmem_limit_bytes=KERNEL_VMEM),
        cost_estimate=pl.CostEstimate(
            flops=4 * heads * span * span * n_pre * HD,
            bytes_accessed=4 * queries.size * 2,
            transcendentals=heads * span * span * n_pre,
        ),
        name="attention",
    )(info, slots, queries, keys, values, start)


PIECES = 8


def chunk_copy(h_ref, chunk, h_buf, sem):
    depth = h_buf.shape[1]
    columns = pl.ds(pl.multiple_of(chunk * depth, depth), depth)
    return pltpu.make_async_copy(h_ref.at[:, columns], h_buf, sem)


def add_pieces(member, chunk, pieces, w_ref, acc_ref):
    share = pieces[0].shape[1]
    half = PIECES // 2
    for side in range(2):

        @pl.when(jnp.bitwise_xor(member // half, side) == lax.rem(chunk, 2))
        def _():
            total = acc_ref[...]
            for j in range(side * half, side * half + half):
                row = lax.rem(jnp.bitwise_xor(member, j), half) * share
                total += jnp.dot(
                    pieces[j][...],
                    w_ref[pl.ds(pl.multiple_of(row, share), share), :],
                    preferred_element_type=jnp.float32,
                )
            acc_ref[...] = total


def near_kernel(place, h_ref, kw_ref, vw_ref, out_ref, h_buf, w_buf, sems):
    copies = [
        chunk_copy(h_ref, place[0], h_buf, sems.at[0]),
        pltpu.make_async_copy(kw_ref, w_buf.at[:, pl.ds(0, HD)], sems.at[1]),
        pltpu.make_async_copy(vw_ref, w_buf.at[:, pl.ds(HD, HD)], sems.at[2]),
    ]
    for copy in copies:
        copy.start()
    for copy in copies:
        copy.wait()
    out_ref[...] = jnp.dot(h_buf[...], w_buf[...], preferred_element_type=jnp.float32)


def partial_kernel(
    column, place, h_ref, w_ref, before_ref, owner_ref, out_ref, h_buf, w_buf, sems
):
    copies = [
        pltpu.make_async_copy(w_ref, w_buf, sems.at[0]),
        chunk_copy(h_ref, place[0], h_buf, sems.at[1]),
    ]
    for copy in copies:
        copy.start()
    span = h_buf.shape[0]
    part = slice(column * HD, column * HD + HD)
    if column == 0:
        out_ref[span:] = owner_ref[...]
    for copy in copies:
        copy.wait()
    out_ref[:span] = before_ref[:, part] + jnp.dot(
        h_buf[...], w_buf[...], preferred_element_type=jnp.float32
    )


def facing_kernel(place, h_ref, kw_ref, vw_ref, *refs):
    pieces = refs[:PIECES]
    out_ref, h_buf, w_buf, sems = refs[PIECES:]
    span = h_buf.shape[0]

    @pl.when(place[3] == 1)
    def _():
        copies = [
            pltpu.make_async_copy(kw_ref, w_buf.at[:, pl.ds(0, HD)], sems.at[0]),
            pltpu.make_async_copy(vw_ref, w_buf.at[:, pl.ds(HD, HD)], sems.at[1]),
            chunk_copy(h_ref, place[0], h_buf, sems.at[2]),
        ]
        for copy in copies:
            copy.start()
        for copy in copies[:2]:
            copy.wait()
        out_ref[span:] = jnp.zeros((span, 2 * HD), jnp.float32)
        add_pieces(place[2], place[0], pieces, w_buf, out_ref.at[pl.ds(span, span)])
        copies[2].wait()
        out_ref[:span] = jnp.dot(h_buf[...], w_buf[...], preferred_element_type=jnp.float32)


def distant_kernel(column, place, h_ref, w_ref, near_ref, outer_ref, facing_ref, bias_ref, *refs):
    pieces = refs[:PIECES]
    out_ref, h_buf, w_buf, acc, *parts, sems = refs[PIECES:]
    near, outer = parts or (near_ref, outer_ref)
    span = h_buf.shape[0]
    part = slice(column * HD, column * HD + HD)

    @pl.when(place[3] == 1)
    def _():
        copies = [
            pltpu.make_async_copy(w_ref, w_buf, sems.at[0]),
            chunk_copy(h_ref, place[0], h_buf, sems.at[1]),
        ]
        if parts:
            copies.append(pltpu.make_async_copy(outer_ref, outer, sems.at[2]))
            copies.append(pltpu.make_async_copy(near_ref, near, sems.at[3]))
        for copy in copies:
            copy.start()
        for copy in copies[2:]:
            copy.wait()
        own_at = pl.multiple_of(place[1] * span, span)
        outer_at = pl.multiple_of((1 - place[1]) * span, span)
        bias = bias_ref[...].astype(jnp.float32)
        acc[...] = outer[:span] + facing_ref[span:, part] + bias
        copies[0].wait()
        add_pieces(place[2], place[0], pieces, w_buf, acc)
        out_ref[pl.ds(outer_at, span), :] = acc[...].astype(jnp.bfloat16)
        own = near[:span] + facing_ref[:span, part] + bias
        copies[1].wait()
        own += jnp.dot(h_buf[...], w_buf[...], preferred_element_type=jnp.float32)
        out_ref[pl.ds(own_at, span), :] = own.astype(jnp.bfloat16)
        if column == 0:
            mine, theirs = near[span:], outer[span:]
            lower = jnp.where(place[1] == 0, mine, theirs)
            upper = jnp.where(place[1] == 0, theirs, mine)
            out_ref[2 * span :] = jnp.concatenate([lower, upper], axis=0).astype(jnp.bfloat16)


EXTRA = 8
HELD = pl.BlockSpec(memory_space=pltpu.HBM)
FAST = pl.BlockSpec(memory_space=pltpu.VMEM)
SCALAR = pl.BlockSpec(memory_space=pltpu.SMEM)


def in_hbm(x):
    return pltpu.with_memory_space_constraint(x, pltpu.HBM)


def call_project(kernel, name, place, operands, rows, columns, kind, scratch, held=1, copies=()):
    return pl.pallas_call(
        kernel,
        in_specs=[SCALAR] + [HELD] * held + [FAST] * (len(operands) - held),
        out_specs=FAST,
        out_shape=jax.ShapeDtypeStruct((rows, columns), kind),
        scratch_shapes=scratch + [pltpu.SemaphoreType.DMA(copies)],
        compiler_params=pltpu.CompilerParams(vmem_limit_bytes=KERNEL_VMEM),
        cost_estimate=pl.CostEstimate(flops=0, bytes_accessed=0, transcendentals=0),
        name=name,
    )(place, *[in_hbm(x) for x in operands[:held]], *operands[held:])


INWARD = [(0, 1), (3, 2)]
ACROSS = [(1, 2), (2, 1)]
OUTWARD = [(1, 0), (2, 3)]
LEAP = [(1, 3), (2, 0)]
SWAP = [(0, 1), (1, 0), (2, 3), (3, 2)]


def line_of_four(hidden, key_weight, value_weight, key_bias, value_bias, page_owner):
    index = lax.axis_index("pre")
    member = lax.axis_index(("dec", "tp"))
    span, width = hidden.shape
    depth = key_weight.shape[0]
    share = width // 2 // PIECES
    facing = 3 - index
    near = jnp.bitwise_xor(index, 1)
    distant = jnp.bitwise_xor(facing, 1)
    second = (index < 2).astype(jnp.int32)
    inner = ((index == 1) | (index == 2)).astype(jnp.int32)

    def send(x, pairs):
        return lax.ppermute(x, "pre", pairs)

    def trade(x, apart):
        return lax.ppermute(x, ("dec", "tp"), [(m, m ^ apart) for m in range(PIECES)])

    mine = second * (width // 2) + member * share
    cut = lax.dynamic_slice_in_dim(hidden, mine, share, axis=1)
    tie = lax.optimization_barrier
    block = pltpu.VMEM((span, depth), jnp.bfloat16)
    both = pltpu.VMEM((depth, 2 * HD), jnp.bfloat16)
    single = pltpu.VMEM((depth, HD), jnp.bfloat16)
    key_facing = send(key_weight, ACROSS)
    cut = send(cut, INWARD)
    own_part = call_project(
        near_kernel,
        "near",
        index[None],
        [hidden, key_weight, value_weight],
        span,
        2 * HD,
        jnp.float32,
        [block, both],
        held=3,
        copies=(3,),
    )
    cut, key_facing, key_after, value_after, own_part = tie(
        (cut, key_facing, key_weight, value_weight, own_part)
    )
    value_facing = send(value_after, ACROSS)
    key_swapped = send(key_after, SWAP)
    value_swapped = send(value_after, SWAP)
    chips = [cut, trade(cut, 2), trade(cut, 4), trade(cut, 6)]
    key_swapped, value_facing = tie((key_swapped, value_facing))
    key_distant = send(key_swapped, ACROSS)
    value_distant = send(value_swapped, ACROSS)
    owners = jnp.broadcast_to(page_owner.T.astype(jnp.float32), (EXTRA, page_owner.shape[0]))
    owners = jnp.pad(owners, ((0, 0), (0, HD - page_owner.shape[0])))

    def begin(column, weight):
        part = call_project(
            functools.partial(partial_kernel, column),
            "partial",
            near[None],
            [hidden, weight, own_part, owners],
            span + (EXTRA if column == 0 else 0),
            HD,
            jnp.float32,
            [block, single],
            held=2,
            copies=(2,),
        )
        return part, send(part, INWARD)

    key_part, key_outer = begin(0, key_swapped)
    chips[2], key_distant, key_outer = tie((chips[2], key_distant, key_outer))
    mates = [trade(x, 1) for x in chips]
    pieces = [x for both_cores in zip(chips, mates) for x in both_cores]

    def place(chunk):
        return jnp.stack([chunk, second, member, inner])

    def finish(column, weight, parts, bias):
        return call_project(
            functools.partial(distant_kernel, column),
            "distant",
            place(distant),
            [hidden, weight, *parts, faced, bias[None, :]] + pieces,
            2 * span + (2 * EXTRA if column == 0 else 0),
            HD,
            jnp.bfloat16,
            [block, single, pltpu.VMEM((span, HD), jnp.float32)]
            + [pltpu.VMEM(x.shape, jnp.float32) for x in parts if column == 0],
            held=4 if column == 0 else 2,
            copies=(4,),
        )

    value_parts = begin(1, value_swapped)
    faced = call_project(
        facing_kernel,
        "facing",
        place(facing),
        [hidden, key_facing, value_facing] + pieces,
        2 * span,
        2 * HD,
        jnp.float32,
        [block, both],
        held=3,
        copies=(3,),
    )
    keys = finish(0, key_distant, (key_part, key_outer), key_bias)
    keys_far, keys_out, keys_across = send(keys, LEAP), send(keys, OUTWARD), send(keys, ACROSS)
    values = finish(1, value_distant, value_parts, value_bias)
    values_across = send(values, ACROSS)
    keys_out, values_after = tie((keys_out, values))
    values_out = send(values_after, OUTWARD)
    values_across, keys_far = tie((values_across, keys_far))
    values_far = send(values_across, OUTWARD)
    return (
        (keys, keys_out, keys_across, keys_far),
        (values, values_out, values_across, values_far),
    )


def head_of(x, g):
    return x[:, g * HD : (g + 1) * HD]


def attend(q_ref, heads, keys, values, allowed, before, store):
    factor = HD**-0.5 * math.log2(math.e)

    def scores_of(g):
        return lax.dot_general(
            head_of(q_ref, g), keys, (((1,), (1,)), ((), ())), preferred_element_type=jnp.float32
        )

    following = scores_of(0)
    for g in range(heads):
        scores = jnp.where(allowed, following, NEG)
        if g + 1 < heads:
            following = scores_of(g + 1)
        peak = jnp.max(scores, axis=1, keepdims=True)
        if before is not None:
            top, total, mix = before(g)
            peak = jnp.maximum(peak, top)
        weights = jnp.exp2(scores * factor - peak * factor).astype(jnp.bfloat16)
        mixed = jnp.dot(weights, values, preferred_element_type=jnp.float32)
        sums, mixed = mixed[:, HD:], mixed[:, :HD]
        if before is not None:
            shrink = jnp.exp2((top - peak) * factor)
            sums = sums + total * shrink
            mixed = mixed + mix * shrink
        store(g, peak, sums, mixed)


def with_ones(values):
    return jnp.concatenate([values, jnp.ones_like(values)], axis=1)


def prompt_starts(seg_ref, first, span):
    seg = seg_ref[...]
    position = (lax.broadcasted_iota(jnp.int32, (span, 1), 0) + first).astype(jnp.float32)
    start = jnp.zeros((span, 1), jnp.float32)
    for v in range(1, PROMPTS):
        lower = jnp.where(seg < v, 1.0, 0.0)
        bound = jnp.sum(jnp.sum(lower, axis=1, keepdims=True), axis=0, keepdims=True)
        start = jnp.where(position >= bound, bound, start)
    return start.astype(jnp.int32)


def read_owners(held_k, span, listed, named, sem):
    listed[...] = held_k[2 * span :].astype(jnp.float32).astype(jnp.int32)
    copy = pltpu.make_async_copy(listed, named, sem)
    copy.start()
    return copy


def place_pages(index, span, named, held_k, held_v, cache_ref, laid):
    rows = cache_ref.shape[1]
    row = lax.broadcasted_iota(jnp.int32, (rows, 2 * HD), 0)
    for s in range(2):
        rank = jnp.int32(0)
        for p in range(span // PAGE):
            tokens = pl.ds(s * span + p * PAGE, PAGE)
            at = pl.ds(pl.multiple_of(rank * PAGE, PAGE), PAGE)
            laid[s, at, :HD] = held_k[tokens, :]
            laid[s, at, HD:] = held_v[tokens, :]
            rank = rank + (named[s * EXTRA, p] == index).astype(jnp.int32)
        cache_ref[s] = jnp.where(row < rank * PAGE, laid[s, :rows], 0)


def own_kernel(
    heads,
    info,
    q_ref,
    seg_ref,
    k_in,
    k_out,
    v_in,
    v_out,
    top,
    total,
    mix,
    cache_ref,
    held_k,
    held_v,
    q_buf,
    listed,
    named,
    laid,
    sems,
):
    copy = pltpu.make_async_copy(q_ref, q_buf, sems.at[0])
    copy.start()
    span = q_buf.shape[0]
    index = info[0]
    inner = (index == 1) | (index == 2)
    held_k[...] = jnp.where(inner, k_in[...], k_out[...])
    held_v[...] = jnp.where(inner, v_in[...], v_out[...])
    owners = read_owners(held_k, span, listed, named, sems.at[1])
    keys = held_k[: 2 * span]
    values = with_ones(held_v[...])
    columns = lax.broadcasted_iota(jnp.int32, (span, 2 * span), 1)
    rows = lax.broadcasted_iota(jnp.int32, (span, 2 * span), 0)
    start = prompt_starts(seg_ref, index * span, span)
    allowed = (columns <= rows + lax.rem(index, 2) * span) & (
        columns >= start - (index // 2) * 2 * span
    )
    copy.wait()

    def store(g, peak, sums, mixed):
        top[g] = peak
        total[g] = sums[:, :1]
        mix[g] = mixed

    attend(q_buf, heads, keys, values, allowed, None, store)
    owners.wait()
    place_pages(index, span, named, held_k, held_v, cache_ref, laid)


def far_kernel(
    heads,
    info,
    q_ref,
    seg_ref,
    k_across,
    k_far,
    v_across,
    v_far,
    top,
    total,
    mix,
    own_cache,
    out_ref,
    cache_ref,
    held_k,
    held_v,
    q_buf,
    listed,
    named,
    laid,
    sems,
    out_buf,
    far_cache,
):
    copy = pltpu.make_async_copy(q_ref, q_buf, sems.at[0])
    copy.start()
    span = q_buf.shape[0]
    index = info[0]
    inner = (index == 1) | (index == 2)
    held_k[...] = jnp.where(inner, k_across[...], k_far[...])
    held_v[...] = jnp.where(inner, v_across[...], v_far[...])
    owners = read_owners(held_k, span, listed, named, sems.at[1])
    own_at, far_at = index // 2 * 2, (1 - index // 2) * 2
    leaving = [pltpu.make_async_copy(own_cache, cache_ref.at[pl.ds(own_at, 2)], sems.at[2])]
    leaving[0].start()
    copy.wait()

    def leave(g):
        columns = pl.ds(g * HD, HD)
        return pltpu.make_async_copy(out_buf.at[:, columns], out_ref.at[:, columns], sems.at[4 + g])

    def place_far():
        owners.wait()
        place_pages(index, span, named, held_k, held_v, far_cache, laid)
        return pltpu.make_async_copy(far_cache, cache_ref.at[pl.ds(far_at, 2)], sems.at[3])

    @pl.when(index < 2)
    def _():
        for g in range(heads):
            out_buf[:, g * HD : (g + 1) * HD] = (mix[g] / total[g]).astype(out_buf.dtype)
            leave(g).start()
        place_far().start()

    @pl.when(index >= 2)
    def _():
        keys = held_k[: 2 * span]
        values = with_ones(held_v[...])
        columns = lax.broadcasted_iota(jnp.int32, (span, 2 * span), 1)
        allowed = columns >= prompt_starts(seg_ref, index * span, span)

        def store(g, peak, sums, mixed):
            out_buf[:, g * HD : (g + 1) * HD] = (mixed / sums).astype(out_buf.dtype)
            leave(g).start()
            if g == heads // 2:
                place_far().start()

        attend(q_buf, heads, keys, values, allowed, lambda g: (top[g], total[g], mix[g]), store)

    for g in range(heads):
        leave(g).wait()
    leaving[0].wait()
    pltpu.make_async_copy(far_cache, cache_ref.at[pl.ds(far_at, 2)], sems.at[3]).wait()


def attention_of_pairs(queries, segment_ids, keys, values, capacity):
    span = queries.shape[0]
    heads = queries.shape[1] // HD
    info = lax.axis_index("pre").astype(jnp.int32)[None]
    segments = segment_ids.reshape(-1, HD)
    scores = heads * span * 2 * span
    cost = pl.CostEstimate(flops=4 * scores * HD, bytes_accessed=8 * scores, transcendentals=scores)
    params = pltpu.CompilerParams(vmem_limit_bytes=KERNEL_VMEM)
    scratch = [
        pltpu.VMEM((2 * span + 2 * EXTRA, HD), jnp.bfloat16),
        pltpu.VMEM((2 * span, HD), jnp.bfloat16),
        pltpu.VMEM(queries.shape, jnp.bfloat16),
        pltpu.VMEM((2 * EXTRA, HD), jnp.int32),
        pltpu.SMEM((2 * EXTRA, HD), jnp.int32),
        pltpu.VMEM((2, (capacity + 1) * PAGE, 2 * HD), jnp.bfloat16),
        pltpu.SemaphoreType.DMA((4 + heads,)),
    ]
    state = pl.pallas_call(
        functools.partial(own_kernel, heads),
        in_specs=[SCALAR, HELD] + [FAST] * 5,
        out_specs=[FAST] * 4,
        out_shape=[
            jax.ShapeDtypeStruct((heads, span, 1), jnp.float32),
            jax.ShapeDtypeStruct((heads, span, 1), jnp.float32),
            jax.ShapeDtypeStruct((heads, span, HD), jnp.float32),
            jax.ShapeDtypeStruct((2, capacity * PAGE, 2 * HD), jnp.bfloat16),
        ],
        scratch_shapes=scratch,
        compiler_params=params,
        cost_estimate=cost,
        name="attend_own",
    )(info, in_hbm(queries), segments, *keys[:2], *values[:2])
    return pl.pallas_call(
        functools.partial(far_kernel, heads),
        in_specs=[SCALAR, HELD] + [FAST] * 9,
        out_specs=[HELD] * 2,
        out_shape=[
            jax.ShapeDtypeStruct(queries.shape, jnp.bfloat16),
            jax.ShapeDtypeStruct((4, capacity * PAGE, 2 * HD), jnp.bfloat16),
        ],
        scratch_shapes=scratch
        + [
            pltpu.VMEM(queries.shape, jnp.bfloat16),
            pltpu.VMEM((2, capacity * PAGE, 2 * HD), jnp.bfloat16),
        ],
        compiler_params=params,
        cost_estimate=cost,
        name="attend_far",
    )(info, in_hbm(queries), segments, *keys[2:], *values[2:], *state)


def gathered(hidden, key_weight, value_weight, key_bias, value_bias):
    joined = jnp.concatenate([key_weight, value_weight], axis=1)
    joined = lax.all_gather(joined, "pre", axis=0, tiled=True)
    bias = jnp.concatenate([key_bias, value_bias]).astype(jnp.float32)
    local = jnp.dot(hidden, joined, preferred_element_type=jnp.float32) + bias
    both = lax.all_gather(local.astype(jnp.bfloat16), "pre", axis=0, tiled=True)
    return both[:, :HD], both[:, HD:]


def body(hidden, queries, key_weight, value_weight, key_bias, value_bias, segment_ids, page_owner):
    n_pre = lax.axis_size("pre")
    index = lax.axis_index("pre")
    span = hidden.shape[0]
    pages_dev = span // PAGE
    capacity = 2 * pages_dev // n_pre
    assert key_weight.shape[1] == HD
    arrays = (hidden, key_weight, value_weight, key_bias, value_bias)
    if n_pre == 4:
        keys, values = line_of_four(*arrays, page_owner)
        mixed, cache = attention_of_pairs(queries, segment_ids, keys, values, capacity)
        return (mixed, cache[None])

    own_segments = lax.dynamic_slice_in_dim(segment_ids, index * span, span)
    start = jnp.sum(
        (segment_ids[None, :] < own_segments[:, None]).astype(jnp.int32), axis=1, keepdims=True
    )
    info = jnp.stack([index, start[0, 0] // span]).astype(jnp.int32)
    owners = lax.all_gather(page_owner[:, 0], "pre")
    keys, values = gathered(*arrays)
    mine = (owners == index).astype(jnp.int32)
    rank = jnp.cumsum(mine, axis=1) - mine
    numbers = jnp.arange(n_pre * pages_dev, dtype=jnp.int32).reshape(n_pre, 1, pages_dev)
    wanted = (mine[:, None, :] == 1) & (
        rank[:, None, :] == jnp.arange(capacity, dtype=jnp.int32)[None, :, None]
    )
    slots = jnp.max(jnp.where(wanted, numbers, -1), axis=2).reshape(-1)
    mixed, cache = attention(info, slots, queries, keys, values, start, n_pre, capacity)
    return (mixed, cache[None])


def solution(mesh):
    return jax.shard_map(
        body,
        mesh=mesh,
        in_specs=(
            P(("group", "pre"), None),
            P(("group", "pre"), ("dec", "tp")),
            P("pre", ("dec", "tp")),
            P("pre", ("dec", "tp")),
            P(("dec", "tp")),
            P(("dec", "tp")),
            P("group"),
            P(("group", "pre"), None),
        ),
        out_specs=(
            P(("group", "pre"), ("dec", "tp")),
            P(("group", "pre"), None, None, ("dec", "tp")),
        ),
        check_vma=False,
    )
```

```python
import functools
import math

import jax
import jax.numpy as jnp
from jax import lax
from jax.experimental import pallas as pl
from jax.experimental.pallas import tpu as pltpu
from jax.sharding import PartitionSpec as P

HD = 128
PAGE = 16
NEG = -1e30
KERNEL_VMEM = 16 * 1024 * 1024
PROMPTS = 4


def attention_kernel(heads, span, info, slots, q_ref, k_ref, v_ref, start_ref, out_ref, cache_ref, acc, top):
    index = info[0]
    first = info[1]
    factor = HD**-0.5 * math.log2(math.e)
    columns = lax.broadcasted_iota(jnp.int32, (span, span), 1)
    rows = lax.broadcasted_iota(jnp.int32, (span, span), 0)

    def block(j, diagonal):
        at = pl.multiple_of(j * span, span)
        keys = k_ref[pl.ds(at, span), :]
        values = jnp.concatenate(
            [v_ref[pl.ds(at, span), :], jnp.ones((span, HD), jnp.bfloat16)], axis=1
        )
        allowed = columns >= start_ref[...] - at
        if diagonal:
            allowed = allowed & (columns <= rows)
        for g in range(heads):
            scores = lax.dot_general(
                q_ref[:, g * HD : (g + 1) * HD],
                keys,
                (((1,), (1,)), ((), ())),
                preferred_element_type=jnp.float32,
            )
            scores = jnp.where(allowed, scores, NEG)
            peak = jnp.max(scores, axis=1, keepdims=True)
            if not diagonal:
                before = top[g]
                peak = jnp.maximum(peak, before)
            weights = jnp.exp2(scores * factor - peak * factor).astype(jnp.bfloat16)
            mixed = jnp.dot(weights, values, preferred_element_type=jnp.float32)
            if not diagonal:
                mixed = mixed + acc[g] * jnp.exp2((before - peak) * factor)
            top[g] = peak
            acc[g] = mixed

    block(index, True)

    @pl.loop(first, index)
    def _(j):
        block(j, False)

    for g in range(heads):
        mixed = acc[g]
        out_ref[:, g * HD : (g + 1) * HD] = (mixed[:, :HD] / mixed[:, HD:]).astype(out_ref.dtype)

    capacity = cache_ref.shape[1] // PAGE
    empty = jnp.zeros((PAGE, HD), cache_ref.dtype)
    for s in range(cache_ref.shape[0]):

        @pl.loop(0, capacity)
        def _(r):
            page = slots[s * capacity + r]
            token = pl.ds(pl.multiple_of(jnp.maximum(page, 0) * PAGE, PAGE), PAGE)
            row = pl.ds(pl.multiple_of(r * PAGE, PAGE), PAGE)
            cache_ref[s, row, :HD] = jnp.where(page >= 0, k_ref[token, :], empty)
            cache_ref[s, row, HD:] = jnp.where(page >= 0, v_ref[token, :], empty)


def attention(info, slots, queries, keys, values, start, n_pre, capacity):
    span = queries.shape[0]
    heads = queries.shape[1] // HD
    return pl.pallas_call(
        functools.partial(attention_kernel, heads, span),
        in_specs=[
            pl.BlockSpec(memory_space=pltpu.SMEM),
            pl.BlockSpec(memory_space=pltpu.SMEM),
            pl.BlockSpec(memory_space=pltpu.VMEM),
            pl.BlockSpec(memory_space=pltpu.VMEM),
            pl.BlockSpec(memory_space=pltpu.VMEM),
            pl.BlockSpec(memory_space=pltpu.VMEM),
        ],
        out_specs=[
            pl.BlockSpec(memory_space=pltpu.VMEM),
            pl.BlockSpec(memory_space=pltpu.VMEM),
        ],
        out_shape=[
            jax.ShapeDtypeStruct(queries.shape, jnp.bfloat16),
            jax.ShapeDtypeStruct((n_pre, capacity * PAGE, 2 * HD), jnp.bfloat16),
        ],
        scratch_shapes=[
            pltpu.VMEM((heads, span, 2 * HD), jnp.float32),
            pltpu.VMEM((heads, span, 1), jnp.float32),
        ],
        compiler_params=pltpu.CompilerParams(vmem_limit_bytes=KERNEL_VMEM),
        cost_estimate=pl.CostEstimate(
            flops=4 * heads * span * span * n_pre * HD,
            bytes_accessed=4 * queries.size * 2,
            transcendentals=heads * span * span * n_pre,
        ),
        name="attention",
    )(info, slots, queries, keys, values, start)


PIECES = 8


def chunk_copy(h_ref, chunk, h_buf, sem):
    depth = h_buf.shape[1]
    columns = pl.ds(pl.multiple_of(chunk * depth, depth), depth)
    return pltpu.make_async_copy(h_ref.at[:, columns], h_buf, sem)


def add_pieces(member, chunk, pieces, w_ref, acc_ref):
    share = pieces[0].shape[1]
    half = PIECES // 2
    for side in range(2):

        @pl.when(jnp.bitwise_xor(member // half, side) == lax.rem(chunk, 2))
        def _():
            total = acc_ref[...]
            for j in range(side * half, side * half + half):
                row = lax.rem(jnp.bitwise_xor(member, j), half) * share
                total += jnp.dot(
                    pieces[j][...],
                    w_ref[pl.ds(pl.multiple_of(row, share), share), :],
                    preferred_element_type=jnp.float32,
                )
            acc_ref[...] = total


def near_kernel(place, h_ref, kw_ref, vw_ref, out_ref, h_buf, w_buf, sems):
    copies = [
        chunk_copy(h_ref, place[0], h_buf, sems.at[0]),
        pltpu.make_async_copy(kw_ref, w_buf.at[:, pl.ds(0, HD)], sems.at[1]),
        pltpu.make_async_copy(vw_ref, w_buf.at[:, pl.ds(HD, HD)], sems.at[2]),
    ]
    for copy in copies:
        copy.start()
    for copy in copies:
        copy.wait()
    out_ref[...] = jnp.dot(h_buf[...], w_buf[...], preferred_element_type=jnp.float32)


def partial_kernel(
    column, place, h_ref, w_ref, before_ref, owner_ref, out_ref, h_buf, w_buf, sems
):
    copies = [
        pltpu.make_async_copy(w_ref, w_buf, sems.at[0]),
        chunk_copy(h_ref, place[0], h_buf, sems.at[1]),
    ]
    for copy in copies:
        copy.start()
    span = h_buf.shape[0]
    part = slice(column * HD, column * HD + HD)
    if column == 0:
        out_ref[span:] = owner_ref[...]
    for copy in copies:
        copy.wait()
    out_ref[:span] = before_ref[:, part] + jnp.dot(
        h_buf[...], w_buf[...], preferred_element_type=jnp.float32
    )


def facing_kernel(place, h_ref, kw_ref, vw_ref, *refs):
    pieces = refs[:PIECES]
    out_ref, h_buf, w_buf, sems = refs[PIECES:]
    span = h_buf.shape[0]

    @pl.when(place[3] == 1)
    def _():
        copies = [
            pltpu.make_async_copy(kw_ref, w_buf.at[:, pl.ds(0, HD)], sems.at[0]),
            pltpu.make_async_copy(vw_ref, w_buf.at[:, pl.ds(HD, HD)], sems.at[1]),
            chunk_copy(h_ref, place[0], h_buf, sems.at[2]),
        ]
        for copy in copies:
            copy.start()
        for copy in copies[:2]:
            copy.wait()
        out_ref[span:] = jnp.zeros((span, 2 * HD), jnp.float32)
        add_pieces(place[2], place[0], pieces, w_buf, out_ref.at[pl.ds(span, span)])
        copies[2].wait()
        out_ref[:span] = jnp.dot(h_buf[...], w_buf[...], preferred_element_type=jnp.float32)


def distant_kernel(column, place, h_ref, w_ref, near_ref, outer_ref, facing_ref, bias_ref, *refs):
    pieces = refs[:PIECES]
    out_ref, h_buf, w_buf, acc, *parts, sems = refs[PIECES:]
    near, outer = parts or (near_ref, outer_ref)
    span = h_buf.shape[0]
    part = slice(column * HD, column * HD + HD)

    @pl.when(place[3] == 1)
    def _():
        copies = [
            pltpu.make_async_copy(w_ref, w_buf, sems.at[0]),
            chunk_copy(h_ref, place[0], h_buf, sems.at[1]),
        ]
        if parts:
            copies.append(pltpu.make_async_copy(outer_ref, outer, sems.at[2]))
            copies.append(pltpu.make_async_copy(near_ref, near, sems.at[3]))
        for copy in copies:
            copy.start()
        for copy in copies[2:]:
            copy.wait()
        own_at = pl.multiple_of(place[1] * span, span)
        outer_at = pl.multiple_of((1 - place[1]) * span, span)
        bias = bias_ref[...].astype(jnp.float32)
        acc[...] = outer[:span] + facing_ref[span:, part] + bias
        copies[0].wait()
        add_pieces(place[2], place[0], pieces, w_buf, acc)
        out_ref[pl.ds(outer_at, span), :] = acc[...].astype(jnp.bfloat16)
        own = near[:span] + facing_ref[:span, part] + bias
        copies[1].wait()
        own += jnp.dot(h_buf[...], w_buf[...], preferred_element_type=jnp.float32)
        out_ref[pl.ds(own_at, span), :] = own.astype(jnp.bfloat16)
        if column == 0:
            mine, theirs = near[span:], outer[span:]
            lower = jnp.where(place[1] == 0, mine, theirs)
            upper = jnp.where(place[1] == 0, theirs, mine)
            out_ref[2 * span :] = jnp.concatenate([lower, upper], axis=0).astype(jnp.bfloat16)


EXTRA = 8
HELD = pl.BlockSpec(memory_space=pltpu.HBM)
FAST = pl.BlockSpec(memory_space=pltpu.VMEM)
SCALAR = pl.BlockSpec(memory_space=pltpu.SMEM)


def in_hbm(x):
    return pltpu.with_memory_space_constraint(x, pltpu.HBM)


def call_project(kernel, name, place, operands, rows, columns, kind, scratch, held=1, copies=()):
    return pl.pallas_call(
        kernel,
        in_specs=[SCALAR] + [HELD] * held + [FAST] * (len(operands) - held),
        out_specs=FAST,
        out_shape=jax.ShapeDtypeStruct((rows, columns), kind),
        scratch_shapes=scratch + [pltpu.SemaphoreType.DMA(copies)],
        compiler_params=pltpu.CompilerParams(vmem_limit_bytes=KERNEL_VMEM),
        cost_estimate=pl.CostEstimate(flops=0, bytes_accessed=0, transcendentals=0),
        name=name,
    )(place, *[in_hbm(x) for x in operands[:held]], *operands[held:])


INWARD = [(0, 1), (3, 2)]
ACROSS = [(1, 2), (2, 1)]
OUTWARD = [(1, 0), (2, 3)]
LEAP = [(1, 3), (2, 0)]
SWAP = [(0, 1), (1, 0), (2, 3), (3, 2)]


def line_of_four(hidden, key_weight, value_weight, key_bias, value_bias, page_owner):
    index = lax.axis_index("pre")
    member = lax.axis_index(("dec", "tp"))
    span, width = hidden.shape
    depth = key_weight.shape[0]
    share = width // 2 // PIECES
    facing = 3 - index
    near = jnp.bitwise_xor(index, 1)
    distant = jnp.bitwise_xor(facing, 1)
    second = (index < 2).astype(jnp.int32)
    inner = ((index == 1) | (index == 2)).astype(jnp.int32)

    def send(x, pairs):
        return lax.ppermute(x, "pre", pairs)

    def trade(x, apart):
        return lax.ppermute(x, ("dec", "tp"), [(m, m ^ apart) for m in range(PIECES)])

    mine = second * (width // 2) + member * share
    cut = lax.dynamic_slice_in_dim(hidden, mine, share, axis=1)
    tie = lax.optimization_barrier
    block = pltpu.VMEM((span, depth), jnp.bfloat16)
    both = pltpu.VMEM((depth, 2 * HD), jnp.bfloat16)
    single = pltpu.VMEM((depth, HD), jnp.bfloat16)
    key_facing = send(key_weight, ACROSS)
    cut = send(cut, INWARD)
    own_part = call_project(
        near_kernel,
        "near",
        index[None],
        [hidden, key_weight, value_weight],
        span,
        2 * HD,
        jnp.float32,
        [block, both],
        held=3,
        copies=(3,),
    )
    cut, key_facing, key_after, value_after, own_part = tie(
        (cut, key_facing, key_weight, value_weight, own_part)
    )
    value_facing = send(value_after, ACROSS)
    key_swapped = send(key_after, SWAP)
    value_swapped = send(value_after, SWAP)
    chips = [cut, trade(cut, 2), trade(cut, 4), trade(cut, 6)]
    key_swapped, value_facing = tie((key_swapped, value_facing))
    key_distant = send(key_swapped, ACROSS)
    value_distant = send(value_swapped, ACROSS)
    owners = jnp.broadcast_to(page_owner.T.astype(jnp.float32), (EXTRA, page_owner.shape[0]))
    owners = jnp.pad(owners, ((0, 0), (0, HD - page_owner.shape[0])))

    def begin(column, weight):
        part = call_project(
            functools.partial(partial_kernel, column),
            "partial",
            near[None],
            [hidden, weight, own_part, owners],
            span + (EXTRA if column == 0 else 0),
            HD,
            jnp.float32,
            [block, single],
            held=2,
            copies=(2,),
        )
        return part, send(part, INWARD)

    key_part, key_outer = begin(0, key_swapped)
    chips[2], key_distant, key_outer = tie((chips[2], key_distant, key_outer))
    mates = [trade(x, 1) for x in chips]
    pieces = [x for both_cores in zip(chips, mates) for x in both_cores]

    def place(chunk):
        return jnp.stack([chunk, second, member, inner])

    def finish(column, weight, parts, bias):
        return call_project(
            functools.partial(distant_kernel, column),
            "distant",
            place(distant),
            [hidden, weight, *parts, faced, bias[None, :]] + pieces,
            2 * span + (2 * EXTRA if column == 0 else 0),
            HD,
            jnp.bfloat16,
            [block, single, pltpu.VMEM((span, HD), jnp.float32)]
            + [pltpu.VMEM(x.shape, jnp.float32) for x in parts if column == 0],
            held=4 if column == 0 else 2,
            copies=(4,),
        )

    value_parts = begin(1, value_swapped)
    faced = call_project(
        facing_kernel,
        "facing",
        place(facing),
        [hidden, key_facing, value_facing] + pieces,
        2 * span,
        2 * HD,
        jnp.float32,
        [block, both],
        held=3,
        copies=(3,),
    )
    keys = finish(0, key_distant, (key_part, key_outer), key_bias)
    keys_far, keys_out, keys_across = send(keys, LEAP), send(keys, OUTWARD), send(keys, ACROSS)
    values = finish(1, value_distant, value_parts, value_bias)
    values_across = send(values, ACROSS)
    values_out = send(values, OUTWARD)
    values_across, keys_far, keys_out = tie((values_across, keys_far, keys_out))
    values_far = send(values_across, OUTWARD)
    return (
        (keys, keys_out, keys_across, keys_far),
        (values, values_out, values_across, values_far),
    )


def head_of(x, g):
    return x[:, g * HD : (g + 1) * HD]


def attend(q_ref, heads, keys, values, allowed, before, store):
    factor = HD**-0.5 * math.log2(math.e)

    def scores_of(g):
        return lax.dot_general(
            head_of(q_ref, g), keys, (((1,), (1,)), ((), ())), preferred_element_type=jnp.float32
        )

    following = scores_of(0)
    for g in range(heads):
        scores = jnp.where(allowed, following, NEG)
        if g + 1 < heads:
            following = scores_of(g + 1)
        peak = jnp.max(scores, axis=1, keepdims=True)
        if before is not None:
            top, total, mix = before(g)
            peak = jnp.maximum(peak, top)
        weights = jnp.exp2(scores * factor - peak * factor).astype(jnp.bfloat16)
        mixed = jnp.dot(weights, values, preferred_element_type=jnp.float32)
        sums, mixed = mixed[:, HD:], mixed[:, :HD]
        if before is not None:
            shrink = jnp.exp2((top - peak) * factor)
            sums = sums + total * shrink
            mixed = mixed + mix * shrink
        store(g, peak, sums, mixed)


def with_ones(values):
    return jnp.concatenate([values, jnp.ones_like(values)], axis=1)


def prompt_starts(seg_ref, first, span):
    seg = seg_ref[...]
    position = (lax.broadcasted_iota(jnp.int32, (span, 1), 0) + first).astype(jnp.float32)
    start = jnp.zeros((span, 1), jnp.float32)
    for v in range(1, PROMPTS):
        lower = jnp.where(seg < v, 1.0, 0.0)
        bound = jnp.sum(jnp.sum(lower, axis=1, keepdims=True), axis=0, keepdims=True)
        start = jnp.where(position >= bound, bound, start)
    return start.astype(jnp.int32)


def read_owners(held_k, span, listed, named, sem):
    listed[...] = held_k[2 * span :].astype(jnp.float32).astype(jnp.int32)
    copy = pltpu.make_async_copy(listed, named, sem)
    copy.start()
    return copy


def place_pages(index, span, named, held_k, held_v, cache_ref, laid):
    rows = cache_ref.shape[1]
    row = lax.broadcasted_iota(jnp.int32, (rows, 2 * HD), 0)
    for s in range(2):
        rank = jnp.int32(0)
        for p in range(span // PAGE):
            tokens = pl.ds(s * span + p * PAGE, PAGE)
            at = pl.ds(pl.multiple_of(rank * PAGE, PAGE), PAGE)
            laid[s, at, :HD] = held_k[tokens, :]
            laid[s, at, HD:] = held_v[tokens, :]
            rank = rank + (named[s * EXTRA, p] == index).astype(jnp.int32)
        cache_ref[s] = jnp.where(row < rank * PAGE, laid[s, :rows], 0)


def own_kernel(
    heads,
    info,
    q_ref,
    seg_ref,
    k_in,
    k_out,
    v_in,
    v_out,
    top,
    total,
    mix,
    cache_ref,
    held_k,
    held_v,
    q_buf,
    listed,
    named,
    laid,
    sems,
):
    copy = pltpu.make_async_copy(q_ref, q_buf, sems.at[0])
    copy.start()
    span = q_buf.shape[0]
    index = info[0]
    inner = (index == 1) | (index == 2)
    held_k[...] = jnp.where(inner, k_in[...], k_out[...])
    held_v[...] = jnp.where(inner, v_in[...], v_out[...])
    owners = read_owners(held_k, span, listed, named, sems.at[1])
    keys = held_k[: 2 * span]
    values = with_ones(held_v[...])
    columns = lax.broadcasted_iota(jnp.int32, (span, 2 * span), 1)
    rows = lax.broadcasted_iota(jnp.int32, (span, 2 * span), 0)
    start = prompt_starts(seg_ref, index * span, span)
    allowed = (columns <= rows + lax.rem(index, 2) * span) & (
        columns >= start - (index // 2) * 2 * span
    )
    copy.wait()

    def store(g, peak, sums, mixed):
        top[g] = peak
        total[g] = sums[:, :1]
        mix[g] = mixed

    attend(q_buf, heads, keys, values, allowed, None, store)
    owners.wait()
    place_pages(index, span, named, held_k, held_v, cache_ref, laid)


def far_kernel(
    heads,
    info,
    q_ref,
    seg_ref,
    k_across,
    k_far,
    v_across,
    v_far,
    top,
    total,
    mix,
    own_cache,
    out_ref,
    cache_ref,
    held_k,
    held_v,
    q_buf,
    listed,
    named,
    laid,
    sems,
    out_buf,
    far_cache,
):
    copy = pltpu.make_async_copy(q_ref, q_buf, sems.at[0])
    copy.start()
    span = q_buf.shape[0]
    index = info[0]
    inner = (index == 1) | (index == 2)
    held_k[...] = jnp.where(inner, k_across[...], k_far[...])
    held_v[...] = jnp.where(inner, v_across[...], v_far[...])
    owners = read_owners(held_k, span, listed, named, sems.at[1])
    own_at, far_at = index // 2 * 2, (1 - index // 2) * 2
    leaving = [pltpu.make_async_copy(own_cache, cache_ref.at[pl.ds(own_at, 2)], sems.at[2])]
    leaving[0].start()
    copy.wait()

    def leave(g):
        columns = pl.ds(g * HD, HD)
        return pltpu.make_async_copy(out_buf.at[:, columns], out_ref.at[:, columns], sems.at[4 + g])

    def place_far():
        owners.wait()
        place_pages(index, span, named, held_k, held_v, far_cache, laid)
        return pltpu.make_async_copy(far_cache, cache_ref.at[pl.ds(far_at, 2)], sems.at[3])

    @pl.when(index < 2)
    def _():
        for g in range(heads):
            out_buf[:, g * HD : (g + 1) * HD] = (mix[g] / total[g]).astype(out_buf.dtype)
            leave(g).start()
        place_far().start()

    @pl.when(index >= 2)
    def _():
        keys = held_k[: 2 * span]
        values = with_ones(held_v[...])
        columns = lax.broadcasted_iota(jnp.int32, (span, 2 * span), 1)
        allowed = columns >= prompt_starts(seg_ref, index * span, span)

        def store(g, peak, sums, mixed):
            out_buf[:, g * HD : (g + 1) * HD] = (mixed / sums).astype(out_buf.dtype)
            leave(g).start()
            if g == heads // 2:
                place_far().start()

        attend(q_buf, heads, keys, values, allowed, lambda g: (top[g], total[g], mix[g]), store)

    for g in range(heads):
        leave(g).wait()
    leaving[0].wait()
    pltpu.make_async_copy(far_cache, cache_ref.at[pl.ds(far_at, 2)], sems.at[3]).wait()


def attention_of_pairs(queries, segment_ids, keys, values, capacity):
    span = queries.shape[0]
    heads = queries.shape[1] // HD
    info = lax.axis_index("pre").astype(jnp.int32)[None]
    segments = segment_ids.reshape(-1, HD)
    scores = heads * span * 2 * span
    cost = pl.CostEstimate(flops=4 * scores * HD, bytes_accessed=8 * scores, transcendentals=scores)
    params = pltpu.CompilerParams(vmem_limit_bytes=KERNEL_VMEM)
    scratch = [
        pltpu.VMEM((2 * span + 2 * EXTRA, HD), jnp.bfloat16),
        pltpu.VMEM((2 * span, HD), jnp.bfloat16),
        pltpu.VMEM(queries.shape, jnp.bfloat16),
        pltpu.VMEM((2 * EXTRA, HD), jnp.int32),
        pltpu.SMEM((2 * EXTRA, HD), jnp.int32),
        pltpu.VMEM((2, (capacity + 1) * PAGE, 2 * HD), jnp.bfloat16),
        pltpu.SemaphoreType.DMA((4 + heads,)),
    ]
    state = pl.pallas_call(
        functools.partial(own_kernel, heads),
        in_specs=[SCALAR, HELD] + [FAST] * 5,
        out_specs=[FAST] * 4,
        out_shape=[
            jax.ShapeDtypeStruct((heads, span, 1), jnp.float32),
            jax.ShapeDtypeStruct((heads, span, 1), jnp.float32),
            jax.ShapeDtypeStruct((heads, span, HD), jnp.float32),
            jax.ShapeDtypeStruct((2, capacity * PAGE, 2 * HD), jnp.bfloat16),
        ],
        scratch_shapes=scratch,
        compiler_params=params,
        cost_estimate=cost,
        name="attend_own",
    )(info, in_hbm(queries), segments, *keys[:2], *values[:2])
    return pl.pallas_call(
        functools.partial(far_kernel, heads),
        in_specs=[SCALAR, HELD] + [FAST] * 9,
        out_specs=[HELD] * 2,
        out_shape=[
            jax.ShapeDtypeStruct(queries.shape, jnp.bfloat16),
            jax.ShapeDtypeStruct((4, capacity * PAGE, 2 * HD), jnp.bfloat16),
        ],
        scratch_shapes=scratch
        + [
            pltpu.VMEM(queries.shape, jnp.bfloat16),
            pltpu.VMEM((2, capacity * PAGE, 2 * HD), jnp.bfloat16),
        ],
        compiler_params=params,
        cost_estimate=cost,
        name="attend_far",
    )(info, in_hbm(queries), segments, *keys[2:], *values[2:], *state)


def gathered(hidden, key_weight, value_weight, key_bias, value_bias):
    joined = jnp.concatenate([key_weight, value_weight], axis=1)
    joined = lax.all_gather(joined, "pre", axis=0, tiled=True)
    bias = jnp.concatenate([key_bias, value_bias]).astype(jnp.float32)
    local = jnp.dot(hidden, joined, preferred_element_type=jnp.float32) + bias
    both = lax.all_gather(local.astype(jnp.bfloat16), "pre", axis=0, tiled=True)
    return both[:, :HD], both[:, HD:]


def body(hidden, queries, key_weight, value_weight, key_bias, value_bias, segment_ids, page_owner):
    n_pre = lax.axis_size("pre")
    index = lax.axis_index("pre")
    span = hidden.shape[0]
    pages_dev = span // PAGE
    capacity = 2 * pages_dev // n_pre
    assert key_weight.shape[1] == HD
    arrays = (hidden, key_weight, value_weight, key_bias, value_bias)
    if n_pre == 4:
        keys, values = line_of_four(*arrays, page_owner)
        mixed, cache = attention_of_pairs(queries, segment_ids, keys, values, capacity)
        return (mixed, cache[None])

    own_segments = lax.dynamic_slice_in_dim(segment_ids, index * span, span)
    start = jnp.sum(
        (segment_ids[None, :] < own_segments[:, None]).astype(jnp.int32), axis=1, keepdims=True
    )
    info = jnp.stack([index, start[0, 0] // span]).astype(jnp.int32)
    owners = lax.all_gather(page_owner[:, 0], "pre")
    keys, values = gathered(*arrays)
    mine = (owners == index).astype(jnp.int32)
    rank = jnp.cumsum(mine, axis=1) - mine
    numbers = jnp.arange(n_pre * pages_dev, dtype=jnp.int32).reshape(n_pre, 1, pages_dev)
    wanted = (mine[:, None, :] == 1) & (
        rank[:, None, :] == jnp.arange(capacity, dtype=jnp.int32)[None, :, None]
    )
    slots = jnp.max(jnp.where(wanted, numbers, -1), axis=2).reshape(-1)
    mixed, cache = attention(info, slots, queries, keys, values, start, n_pre, capacity)
    return (mixed, cache[None])


def solution(mesh):
    return jax.shard_map(
        body,
        mesh=mesh,
        in_specs=(
            P(("group", "pre"), None),
            P(("group", "pre"), ("dec", "tp")),
            P("pre", ("dec", "tp")),
            P("pre", ("dec", "tp")),
            P(("dec", "tp")),
            P(("dec", "tp")),
            P("group"),
            P(("group", "pre"), None),
        ),
        out_specs=(
            P(("group", "pre"), ("dec", "tp")),
            P(("group", "pre"), None, None, ("dec", "tp")),
        ),
        check_vma=False,
    )
```

```python
import functools
import math

import jax
import jax.numpy as jnp
from jax import lax
from jax.experimental import pallas as pl
from jax.experimental.pallas import tpu as pltpu
from jax.sharding import PartitionSpec as P

HD = 128
PAGE = 16
NEG = -1e30
KERNEL_VMEM = 16 * 1024 * 1024
PROMPTS = 4


def attention_kernel(heads, span, info, slots, q_ref, k_ref, v_ref, start_ref, out_ref, cache_ref, acc, top):
    index = info[0]
    first = info[1]
    factor = HD**-0.5 * math.log2(math.e)
    columns = lax.broadcasted_iota(jnp.int32, (span, span), 1)
    rows = lax.broadcasted_iota(jnp.int32, (span, span), 0)

    def block(j, diagonal):
        at = pl.multiple_of(j * span, span)
        keys = k_ref[pl.ds(at, span), :]
        values = jnp.concatenate(
            [v_ref[pl.ds(at, span), :], jnp.ones((span, HD), jnp.bfloat16)], axis=1
        )
        allowed = columns >= start_ref[...] - at
        if diagonal:
            allowed = allowed & (columns <= rows)
        for g in range(heads):
            scores = lax.dot_general(
                q_ref[:, g * HD : (g + 1) * HD],
                keys,
                (((1,), (1,)), ((), ())),
                preferred_element_type=jnp.float32,
            )
            scores = jnp.where(allowed, scores, NEG)
            peak = jnp.max(scores, axis=1, keepdims=True)
            if not diagonal:
                before = top[g]
                peak = jnp.maximum(peak, before)
            weights = jnp.exp2(scores * factor - peak * factor).astype(jnp.bfloat16)
            mixed = jnp.dot(weights, values, preferred_element_type=jnp.float32)
            if not diagonal:
                mixed = mixed + acc[g] * jnp.exp2((before - peak) * factor)
            top[g] = peak
            acc[g] = mixed

    block(index, True)

    @pl.loop(first, index)
    def _(j):
        block(j, False)

    for g in range(heads):
        mixed = acc[g]
        out_ref[:, g * HD : (g + 1) * HD] = (mixed[:, :HD] / mixed[:, HD:]).astype(out_ref.dtype)

    capacity = cache_ref.shape[1] // PAGE
    empty = jnp.zeros((PAGE, HD), cache_ref.dtype)
    for s in range(cache_ref.shape[0]):

        @pl.loop(0, capacity)
        def _(r):
            page = slots[s * capacity + r]
            token = pl.ds(pl.multiple_of(jnp.maximum(page, 0) * PAGE, PAGE), PAGE)
            row = pl.ds(pl.multiple_of(r * PAGE, PAGE), PAGE)
            cache_ref[s, row, :HD] = jnp.where(page >= 0, k_ref[token, :], empty)
            cache_ref[s, row, HD:] = jnp.where(page >= 0, v_ref[token, :], empty)


def attention(info, slots, queries, keys, values, start, n_pre, capacity):
    span = queries.shape[0]
    heads = queries.shape[1] // HD
    return pl.pallas_call(
        functools.partial(attention_kernel, heads, span),
        in_specs=[
            pl.BlockSpec(memory_space=pltpu.SMEM),
            pl.BlockSpec(memory_space=pltpu.SMEM),
            pl.BlockSpec(memory_space=pltpu.VMEM),
            pl.BlockSpec(memory_space=pltpu.VMEM),
            pl.BlockSpec(memory_space=pltpu.VMEM),
            pl.BlockSpec(memory_space=pltpu.VMEM),
        ],
        out_specs=[
            pl.BlockSpec(memory_space=pltpu.VMEM),
            pl.BlockSpec(memory_space=pltpu.VMEM),
        ],
        out_shape=[
            jax.ShapeDtypeStruct(queries.shape, jnp.bfloat16),
            jax.ShapeDtypeStruct((n_pre, capacity * PAGE, 2 * HD), jnp.bfloat16),
        ],
        scratch_shapes=[
            pltpu.VMEM((heads, span, 2 * HD), jnp.float32),
            pltpu.VMEM((heads, span, 1), jnp.float32),
        ],
        compiler_params=pltpu.CompilerParams(vmem_limit_bytes=KERNEL_VMEM),
        cost_estimate=pl.CostEstimate(
            flops=4 * heads * span * span * n_pre * HD,
            bytes_accessed=4 * queries.size * 2,
            transcendentals=heads * span * span * n_pre,
        ),
        name="attention",
    )(info, slots, queries, keys, values, start)


PIECES = 8


def chunk_copy(h_ref, chunk, h_buf, sem):
    depth = h_buf.shape[1]
    columns = pl.ds(pl.multiple_of(chunk * depth, depth), depth)
    return pltpu.make_async_copy(h_ref.at[:, columns], h_buf, sem)


def add_pieces(member, chunk, pieces, w_ref, acc_ref):
    share = pieces[0].shape[1]
    half = PIECES // 2
    for side in range(2):

        @pl.when(jnp.bitwise_xor(member // half, side) == lax.rem(chunk, 2))
        def _():
            total = acc_ref[...]
            for j in range(side * half, side * half + half):
                row = lax.rem(jnp.bitwise_xor(member, j), half) * share
                total += jnp.dot(
                    pieces[j][...],
                    w_ref[pl.ds(pl.multiple_of(row, share), share), :],
                    preferred_element_type=jnp.float32,
                )
            acc_ref[...] = total


def near_kernel(place, h_ref, kw_ref, vw_ref, out_ref, h_buf, w_buf, sems):
    copies = [
        chunk_copy(h_ref, place[0], h_buf, sems.at[0]),
        pltpu.make_async_copy(kw_ref, w_buf.at[:, pl.ds(0, HD)], sems.at[1]),
        pltpu.make_async_copy(vw_ref, w_buf.at[:, pl.ds(HD, HD)], sems.at[2]),
    ]
    for copy in copies:
        copy.start()
    for copy in copies:
        copy.wait()
    out_ref[...] = jnp.dot(h_buf[...], w_buf[...], preferred_element_type=jnp.float32)


def partial_kernel(
    column, place, h_ref, w_ref, before_ref, owner_ref, out_ref, h_buf, w_buf, sems
):
    copies = [
        pltpu.make_async_copy(w_ref, w_buf, sems.at[0]),
        chunk_copy(h_ref, place[0], h_buf, sems.at[1]),
    ]
    for copy in copies:
        copy.start()
    span = h_buf.shape[0]
    part = slice(column * HD, column * HD + HD)
    if column == 0:
        out_ref[span:] = owner_ref[...]
    for copy in copies:
        copy.wait()
    out_ref[:span] = before_ref[:, part] + jnp.dot(
        h_buf[...], w_buf[...], preferred_element_type=jnp.float32
    )


def facing_kernel(place, h_ref, kw_ref, vw_ref, *refs):
    pieces = refs[:PIECES]
    out_ref, h_buf, w_buf, sems = refs[PIECES:]
    span = h_buf.shape[0]

    @pl.when(place[3] == 1)
    def _():
        copies = [
            pltpu.make_async_copy(kw_ref, w_buf.at[:, pl.ds(0, HD)], sems.at[0]),
            pltpu.make_async_copy(vw_ref, w_buf.at[:, pl.ds(HD, HD)], sems.at[1]),
            chunk_copy(h_ref, place[0], h_buf, sems.at[2]),
        ]
        for copy in copies:
            copy.start()
        for copy in copies[:2]:
            copy.wait()
        out_ref[span:] = jnp.zeros((span, 2 * HD), jnp.float32)
        add_pieces(place[2], place[0], pieces, w_buf, out_ref.at[pl.ds(span, span)])
        copies[2].wait()
        out_ref[:span] = jnp.dot(h_buf[...], w_buf[...], preferred_element_type=jnp.float32)


def distant_kernel(column, place, h_ref, w_ref, near_ref, outer_ref, facing_ref, bias_ref, *refs):
    pieces = refs[:PIECES]
    out_ref, h_buf, w_buf, acc, *parts, sems = refs[PIECES:]
    near, outer = parts or (near_ref, outer_ref)
    span = h_buf.shape[0]
    part = slice(column * HD, column * HD + HD)

    @pl.when(place[3] == 1)
    def _():
        copies = [
            pltpu.make_async_copy(w_ref, w_buf, sems.at[0]),
            chunk_copy(h_ref, place[0], h_buf, sems.at[1]),
        ]
        if parts:
            copies.append(pltpu.make_async_copy(outer_ref, outer, sems.at[2]))
            copies.append(pltpu.make_async_copy(near_ref, near, sems.at[3]))
        for copy in copies:
            copy.start()
        for copy in copies[2:]:
            copy.wait()
        own_at = pl.multiple_of(place[1] * span, span)
        outer_at = pl.multiple_of((1 - place[1]) * span, span)
        bias = bias_ref[...].astype(jnp.float32)
        acc[...] = outer[:span] + facing_ref[span:, part] + bias
        copies[0].wait()
        add_pieces(place[2], place[0], pieces, w_buf, acc)
        out_ref[pl.ds(outer_at, span), :] = acc[...].astype(jnp.bfloat16)
        own = near[:span] + facing_ref[:span, part] + bias
        copies[1].wait()
        own += jnp.dot(h_buf[...], w_buf[...], preferred_element_type=jnp.float32)
        out_ref[pl.ds(own_at, span), :] = own.astype(jnp.bfloat16)
        if column == 0:
            mine, theirs = near[span:], outer[span:]
            lower = jnp.where(place[1] == 0, mine, theirs)
            upper = jnp.where(place[1] == 0, theirs, mine)
            out_ref[2 * span :] = jnp.concatenate([lower, upper], axis=0).astype(jnp.bfloat16)


EXTRA = 8
HELD = pl.BlockSpec(memory_space=pltpu.HBM)
FAST = pl.BlockSpec(memory_space=pltpu.VMEM)
SCALAR = pl.BlockSpec(memory_space=pltpu.SMEM)


def in_hbm(x):
    return pltpu.with_memory_space_constraint(x, pltpu.HBM)


def call_project(kernel, name, place, operands, rows, columns, kind, scratch, held=1, copies=()):
    return pl.pallas_call(
        kernel,
        in_specs=[SCALAR] + [HELD] * held + [FAST] * (len(operands) - held),
        out_specs=FAST,
        out_shape=jax.ShapeDtypeStruct((rows, columns), kind),
        scratch_shapes=scratch + [pltpu.SemaphoreType.DMA(copies)],
        compiler_params=pltpu.CompilerParams(vmem_limit_bytes=KERNEL_VMEM),
        cost_estimate=pl.CostEstimate(flops=0, bytes_accessed=0, transcendentals=0),
        name=name,
    )(place, *[in_hbm(x) for x in operands[:held]], *operands[held:])


INWARD = [(0, 1), (3, 2)]
ACROSS = [(1, 2), (2, 1)]
OUTWARD = [(1, 0), (2, 3)]
LEAP = [(1, 3), (2, 0)]
SWAP = [(0, 1), (1, 0), (2, 3), (3, 2)]


def line_of_four(hidden, key_weight, value_weight, key_bias, value_bias, page_owner):
    index = lax.axis_index("pre")
    member = lax.axis_index(("dec", "tp"))
    span, width = hidden.shape
    depth = key_weight.shape[0]
    share = width // 2 // PIECES
    facing = 3 - index
    near = jnp.bitwise_xor(index, 1)
    distant = jnp.bitwise_xor(facing, 1)
    second = (index < 2).astype(jnp.int32)
    inner = ((index == 1) | (index == 2)).astype(jnp.int32)

    def send(x, pairs):
        return lax.ppermute(x, "pre", pairs)

    def trade(x, apart):
        return lax.ppermute(x, ("dec", "tp"), [(m, m ^ apart) for m in range(PIECES)])

    mine = second * (width // 2) + member * share
    cut = lax.dynamic_slice_in_dim(hidden, mine, share, axis=1)
    tie = lax.optimization_barrier
    block = pltpu.VMEM((span, depth), jnp.bfloat16)
    both = pltpu.VMEM((depth, 2 * HD), jnp.bfloat16)
    single = pltpu.VMEM((depth, HD), jnp.bfloat16)
    key_facing = send(key_weight, ACROSS)
    cut = send(cut, INWARD)
    own_part = call_project(
        near_kernel,
        "near",
        index[None],
        [hidden, key_weight, value_weight],
        span,
        2 * HD,
        jnp.float32,
        [block, both],
        held=3,
        copies=(3,),
    )
    cut, key_facing, key_after, value_after, own_part = tie(
        (cut, key_facing, key_weight, value_weight, own_part)
    )
    value_facing = send(value_after, ACROSS)
    key_swapped = send(key_after, SWAP)
    value_swapped = send(value_after, SWAP)
    chips = [cut, trade(cut, 2), trade(cut, 4), trade(cut, 6)]
    key_swapped, value_facing = tie((key_swapped, value_facing))
    key_distant = send(key_swapped, ACROSS)
    value_distant = send(value_swapped, ACROSS)
    owners = jnp.broadcast_to(page_owner.T.astype(jnp.float32), (EXTRA, page_owner.shape[0]))
    owners = jnp.pad(owners, ((0, 0), (0, HD - page_owner.shape[0])))

    def begin(column, weight):
        part = call_project(
            functools.partial(partial_kernel, column),
            "partial",
            near[None],
            [hidden, weight, own_part, owners],
            span + (EXTRA if column == 0 else 0),
            HD,
            jnp.float32,
            [block, single],
            held=2,
            copies=(2,),
        )
        return part, send(part, INWARD)

    key_part, key_outer = begin(0, key_swapped)
    chips[2], key_distant, key_outer = tie((chips[2], key_distant, key_outer))
    mates = [trade(x, 1) for x in chips]
    pieces = [x for both_cores in zip(chips, mates) for x in both_cores]

    def place(chunk):
        return jnp.stack([chunk, second, member, inner])

    def finish(column, weight, parts, bias):
        return call_project(
            functools.partial(distant_kernel, column),
            "distant",
            place(distant),
            [hidden, weight, *parts, faced, bias[None, :]] + pieces,
            2 * span + (2 * EXTRA if column == 0 else 0),
            HD,
            jnp.bfloat16,
            [block, single, pltpu.VMEM((span, HD), jnp.float32)]
            + [pltpu.VMEM(x.shape, jnp.float32) for x in parts if column == 0],
            held=4 if column == 0 else 2,
            copies=(4,),
        )

    value_parts = begin(1, value_swapped)
    faced = call_project(
        facing_kernel,
        "facing",
        place(facing),
        [hidden, key_facing, value_facing] + pieces,
        2 * span,
        2 * HD,
        jnp.float32,
        [block, both],
        held=3,
        copies=(3,),
    )
    keys = finish(0, key_distant, (key_part, key_outer), key_bias)
    keys_far, keys_out, keys_across = send(keys, LEAP), send(keys, OUTWARD), send(keys, ACROSS)
    values = finish(1, value_distant, value_parts, value_bias)
    values_across = send(values, ACROSS)
    values_out = send(values, OUTWARD)
    values_across, keys_far, keys_out = tie((values_across, keys_far, keys_out))
    values_far = send(values_across, OUTWARD)
    return (
        (keys, keys_out, keys_across, keys_far),
        (values, values_out, values_across, values_far),
    )


def head_of(x, g):
    return x[:, g * HD : (g + 1) * HD]


def attend(q_ref, heads, keys, values, allowed, before, store):
    factor = HD**-0.5 * math.log2(math.e)

    def scores_of(g):
        return lax.dot_general(
            head_of(q_ref, g), keys, (((1,), (1,)), ((), ())), preferred_element_type=jnp.float32
        )

    following = scores_of(0)
    for g in range(heads):
        scores = jnp.where(allowed, following, NEG)
        if g + 1 < heads:
            following = scores_of(g + 1)
        peak = jnp.max(scores, axis=1, keepdims=True)
        if before is not None:
            top, total, mix = before(g)
            peak = jnp.maximum(peak, top)
        weights = jnp.exp2(scores * factor - peak * factor).astype(jnp.bfloat16)
        mixed = jnp.dot(weights, values, preferred_element_type=jnp.float32)
        sums, mixed = mixed[:, HD:], mixed[:, :HD]
        if before is not None:
            shrink = jnp.exp2((top - peak) * factor)
            sums = sums + total * shrink
            mixed = mixed + mix * shrink
        store(g, peak, sums, mixed)


def with_ones(values):
    return jnp.concatenate([values, jnp.ones_like(values)], axis=1)


def prompt_starts(seg_ref, first, span):
    seg = seg_ref[...]
    position = (lax.broadcasted_iota(jnp.int32, (span, 1), 0) + first).astype(jnp.float32)
    start = jnp.zeros((span, 1), jnp.float32)
    for v in range(1, PROMPTS):
        lower = jnp.where(seg < v, 1.0, 0.0)
        bound = jnp.sum(jnp.sum(lower, axis=1, keepdims=True), axis=0, keepdims=True)
        start = jnp.where(position >= bound, bound, start)
    return start.astype(jnp.int32)


def read_owners(held_k, span, listed, named, sem):
    listed[...] = held_k[2 * span :].astype(jnp.float32).astype(jnp.int32)
    copy = pltpu.make_async_copy(listed, named, sem)
    copy.start()
    return copy


def place_pages(index, span, named, held_k, held_v, cache_ref, laid):
    rows = cache_ref.shape[1]
    row = lax.broadcasted_iota(jnp.int32, (rows, 2 * HD), 0)
    for s in range(2):
        rank = jnp.int32(0)
        for p in range(span // PAGE):
            tokens = pl.ds(s * span + p * PAGE, PAGE)
            at = pl.ds(pl.multiple_of(rank * PAGE, PAGE), PAGE)
            laid[s, at, :HD] = held_k[tokens, :]
            laid[s, at, HD:] = held_v[tokens, :]
            rank = rank + (named[s * EXTRA, p] == index).astype(jnp.int32)
        cache_ref[s] = jnp.where(row < rank * PAGE, laid[s, :rows], 0)


def own_kernel(
    heads,
    info,
    q_ref,
    seg_ref,
    k_in,
    k_out,
    v_in,
    v_out,
    top,
    total,
    mix,
    cache_ref,
    held_k,
    held_v,
    q_buf,
    listed,
    named,
    laid,
    sems,
):
    copy = pltpu.make_async_copy(q_ref, q_buf, sems.at[0])
    copy.start()
    span = q_buf.shape[0]
    index = info[0]
    inner = (index == 1) | (index == 2)
    held_k[...] = jnp.where(inner, k_in[...], k_out[...])
    held_v[...] = jnp.where(inner, v_in[...], v_out[...])
    owners = read_owners(held_k, span, listed, named, sems.at[1])
    keys = held_k[: 2 * span]
    values = with_ones(held_v[...])
    columns = lax.broadcasted_iota(jnp.int32, (span, 2 * span), 1)
    rows = lax.broadcasted_iota(jnp.int32, (span, 2 * span), 0)
    start = prompt_starts(seg_ref, index * span, span)
    allowed = (columns <= rows + lax.rem(index, 2) * span) & (
        columns >= start - (index // 2) * 2 * span
    )
    copy.wait()

    def store(g, peak, sums, mixed):
        top[g] = peak
        total[g] = sums[:, :1]
        mix[g] = mixed
        if g == heads // 2:
            owners.wait()
            place_pages(index, span, named, held_k, held_v, cache_ref, laid)

    attend(q_buf, heads, keys, values, allowed, None, store)


def far_kernel(
    heads,
    info,
    q_ref,
    seg_ref,
    k_across,
    k_far,
    v_across,
    v_far,
    top,
    total,
    mix,
    own_cache,
    out_ref,
    cache_ref,
    held_k,
    held_v,
    q_buf,
    listed,
    named,
    laid,
    sems,
    out_buf,
    far_cache,
):
    copy = pltpu.make_async_copy(q_ref, q_buf, sems.at[0])
    copy.start()
    span = q_buf.shape[0]
    index = info[0]
    inner = (index == 1) | (index == 2)
    held_k[...] = jnp.where(inner, k_across[...], k_far[...])
    held_v[...] = jnp.where(inner, v_across[...], v_far[...])
    owners = read_owners(held_k, span, listed, named, sems.at[1])
    own_at, far_at = index // 2 * 2, (1 - index // 2) * 2
    leaving = [pltpu.make_async_copy(own_cache, cache_ref.at[pl.ds(own_at, 2)], sems.at[2])]
    leaving[0].start()
    copy.wait()

    def leave(g):
        columns = pl.ds(g * HD, HD)
        return pltpu.make_async_copy(out_buf.at[:, columns], out_ref.at[:, columns], sems.at[4 + g])

    def place_far():
        owners.wait()
        place_pages(index, span, named, held_k, held_v, far_cache, laid)
        return pltpu.make_async_copy(far_cache, cache_ref.at[pl.ds(far_at, 2)], sems.at[3])

    @pl.when(index < 2)
    def _():
        for g in range(heads):
            out_buf[:, g * HD : (g + 1) * HD] = (mix[g] / total[g]).astype(out_buf.dtype)
            leave(g).start()
        place_far().start()

    @pl.when(index >= 2)
    def _():
        keys = held_k[: 2 * span]
        values = with_ones(held_v[...])
        columns = lax.broadcasted_iota(jnp.int32, (span, 2 * span), 1)
        allowed = columns >= prompt_starts(seg_ref, index * span, span)

        def store(g, peak, sums, mixed):
            out_buf[:, g * HD : (g + 1) * HD] = (mixed / sums).astype(out_buf.dtype)
            leave(g).start()
            if g == heads // 2:
                place_far().start()

        attend(q_buf, heads, keys, values, allowed, lambda g: (top[g], total[g], mix[g]), store)

    for g in range(heads):
        leave(g).wait()
    leaving[0].wait()
    pltpu.make_async_copy(far_cache, cache_ref.at[pl.ds(far_at, 2)], sems.at[3]).wait()


def attention_of_pairs(queries, segment_ids, keys, values, capacity):
    span = queries.shape[0]
    heads = queries.shape[1] // HD
    info = lax.axis_index("pre").astype(jnp.int32)[None]
    segments = segment_ids.reshape(-1, HD)
    scores = heads * span * 2 * span
    cost = pl.CostEstimate(flops=4 * scores * HD, bytes_accessed=8 * scores, transcendentals=scores)
    params = pltpu.CompilerParams(vmem_limit_bytes=KERNEL_VMEM)
    scratch = [
        pltpu.VMEM((2 * span + 2 * EXTRA, HD), jnp.bfloat16),
        pltpu.VMEM((2 * span, HD), jnp.bfloat16),
        pltpu.VMEM(queries.shape, jnp.bfloat16),
        pltpu.VMEM((2 * EXTRA, HD), jnp.int32),
        pltpu.SMEM((2 * EXTRA, HD), jnp.int32),
        pltpu.VMEM((2, (capacity + 1) * PAGE, 2 * HD), jnp.bfloat16),
        pltpu.SemaphoreType.DMA((4 + heads,)),
    ]
    state = pl.pallas_call(
        functools.partial(own_kernel, heads),
        in_specs=[SCALAR, HELD] + [FAST] * 5,
        out_specs=[FAST] * 4,
        out_shape=[
            jax.ShapeDtypeStruct((heads, span, 1), jnp.float32),
            jax.ShapeDtypeStruct((heads, span, 1), jnp.float32),
            jax.ShapeDtypeStruct((heads, span, HD), jnp.float32),
            jax.ShapeDtypeStruct((2, capacity * PAGE, 2 * HD), jnp.bfloat16),
        ],
        scratch_shapes=scratch,
        compiler_params=params,
        cost_estimate=cost,
        name="attend_own",
    )(info, in_hbm(queries), segments, *keys[:2], *values[:2])
    return pl.pallas_call(
        functools.partial(far_kernel, heads),
        in_specs=[SCALAR, HELD] + [FAST] * 9,
        out_specs=[HELD] * 2,
        out_shape=[
            jax.ShapeDtypeStruct(queries.shape, jnp.bfloat16),
            jax.ShapeDtypeStruct((4, capacity * PAGE, 2 * HD), jnp.bfloat16),
        ],
        scratch_shapes=scratch
        + [
            pltpu.VMEM(queries.shape, jnp.bfloat16),
            pltpu.VMEM((2, capacity * PAGE, 2 * HD), jnp.bfloat16),
        ],
        compiler_params=params,
        cost_estimate=cost,
        name="attend_far",
    )(info, in_hbm(queries), segments, *keys[2:], *values[2:], *state)


def gathered(hidden, key_weight, value_weight, key_bias, value_bias):
    joined = jnp.concatenate([key_weight, value_weight], axis=1)
    joined = lax.all_gather(joined, "pre", axis=0, tiled=True)
    bias = jnp.concatenate([key_bias, value_bias]).astype(jnp.float32)
    local = jnp.dot(hidden, joined, preferred_element_type=jnp.float32) + bias
    both = lax.all_gather(local.astype(jnp.bfloat16), "pre", axis=0, tiled=True)
    return both[:, :HD], both[:, HD:]


def body(hidden, queries, key_weight, value_weight, key_bias, value_bias, segment_ids, page_owner):
    n_pre = lax.axis_size("pre")
    index = lax.axis_index("pre")
    span = hidden.shape[0]
    pages_dev = span // PAGE
    capacity = 2 * pages_dev // n_pre
    assert key_weight.shape[1] == HD
    arrays = (hidden, key_weight, value_weight, key_bias, value_bias)
    if n_pre == 4:
        keys, values = line_of_four(*arrays, page_owner)
        mixed, cache = attention_of_pairs(queries, segment_ids, keys, values, capacity)
        return (mixed, cache[None])

    own_segments = lax.dynamic_slice_in_dim(segment_ids, index * span, span)
    start = jnp.sum(
        (segment_ids[None, :] < own_segments[:, None]).astype(jnp.int32), axis=1, keepdims=True
    )
    info = jnp.stack([index, start[0, 0] // span]).astype(jnp.int32)
    owners = lax.all_gather(page_owner[:, 0], "pre")
    keys, values = gathered(*arrays)
    mine = (owners == index).astype(jnp.int32)
    rank = jnp.cumsum(mine, axis=1) - mine
    numbers = jnp.arange(n_pre * pages_dev, dtype=jnp.int32).reshape(n_pre, 1, pages_dev)
    wanted = (mine[:, None, :] == 1) & (
        rank[:, None, :] == jnp.arange(capacity, dtype=jnp.int32)[None, :, None]
    )
    slots = jnp.max(jnp.where(wanted, numbers, -1), axis=2).reshape(-1)
    mixed, cache = attention(info, slots, queries, keys, values, start, n_pre, capacity)
    return (mixed, cache[None])


def solution(mesh):
    return jax.shard_map(
        body,
        mesh=mesh,
        in_specs=(
            P(("group", "pre"), None),
            P(("group", "pre"), ("dec", "tp")),
            P("pre", ("dec", "tp")),
            P("pre", ("dec", "tp")),
            P(("dec", "tp")),
            P(("dec", "tp")),
            P("group"),
            P(("group", "pre"), None),
        ),
        out_specs=(
            P(("group", "pre"), ("dec", "tp")),
            P(("group", "pre"), None, None, ("dec", "tp")),
        ),
        check_vma=False,
    )
```
